256 devices in a mesh: gx: 16 (over y, x), gy: 8 (over z), gz: 2 (over core).
Axes of the slice: x: 4, y: 4, z: 8, core: 2. Of those that a mesh axis runs over, the one named last changes fastest.
Arguments:
- fine_field: bfloat16 [20480, 8, 8, 128], P(('gx', 'gy', 'gz')), may hold values from -6 to 6
- target: int32 [20480], P(('gx', 'gy', 'gz')), may hold values from 0 to 36863, as said below
- neighbour: int32 [4608, 6], P(('gx', 'gy', 'gz')), may hold values from -1 to 4607, as said below
- down_weight: bfloat16 [1024, 256], replicated, may hold values from -0.1875 to 0.1875
- conv_weight: bfloat16 [7, 256, 256], replicated, may hold values from -0.125 to 0.125
- out_cotangent: bfloat16 [4608, 4, 4, 4, 256], P(('gx', 'gy', 'gz')), may hold values from -6 to 6
Outputs:
- coarse_field: bfloat16 [4608, 4, 4, 4, 256], P(('gx', 'gy', 'gz'))
- fine_gradient: bfloat16 [20480, 8, 8, 128], P(('gx', 'gy', 'gz'))
- down_gradient: float32 [1024, 256], replicated
- conv_gradient: float32 [7, 256, 256], replicated
The draws below stay inside these ranges and needn't reach their ends.
Inputs may be any that keep to these rules, and one draw needn't show every extreme that they name: `target`: no two fine bricks name the same octant. A fine brick names a coarse brick on its own device or on a device with the same gz index whose gx and gy indices each differ from its own by at most one. At most 20 of a device's fine bricks name a coarse brick on another device; at most 8 name one given other device, and every device sends exactly 8 to some device. `neighbour`: the relation is symmetric: if brick b names n across its +x face, n names b across its -x face (likewise for y and z). A named brick lies on the same device or on the adjacent device along that face's direction (no wrap). Across one face direction exactly 8 bricks of a device name bricks on the adjacent device where that device exists.
All inputs are finite; a program needn't handle non-finite values.
Results may differ from the reference program's by a relative error of at most 0.0061.
Values may be sent and summed in bfloat16 or wider, within the bound.
A program may use at most 128 MiB of HBM per device.

```python
import jax
import jax.numpy as jnp
from jax import lax

C = 128
C2 = 256
NB = 80
CAP = 8
HC = 8
MB = 18
FINE = 20480
COARSE = 4608
N_GX = 16
N_GY = 8
N_GZ = 2
DEVICES = 256


def draw_target(key, part):
    key = jax.random.fold_in(key, 11)
    devices = N_GX * N_GY * N_GZ
    cells_dev = MB * 8
    key_raw, key_first, key_order, key_cells = jax.random.split(key, 4)
    device_ids = jnp.arange(devices, dtype=jnp.int32)
    pos_x = device_ids // (N_GY * N_GZ)
    pos_y = device_ids // N_GZ % N_GY
    step_x = jnp.array([-1, -1, -1, 0, 0, 1, 1, 1], jnp.int32)
    step_y = jnp.array([-1, 0, 1, -1, 1, -1, 0, 1], jnp.int32)
    dir_ids = jnp.arange(8, dtype=jnp.int32)
    next_x = pos_x[:, None] + step_x[None, :]
    next_y = pos_y[:, None] + step_y[None, :]
    valid = (next_x >= 0) & (next_x < N_GX) & (next_y >= 0) & (next_y < N_GY)
    raw_counts = jax.random.randint(key_raw, (devices, 8), 0, CAP + 1).astype(jnp.int32)
    scores = jax.random.randint(key_first, (devices, 8), 0, 1024).astype(jnp.int32) * 8 + dir_ids[None, :]
    scores = jnp.where(valid, scores, -1)
    first_dir = jnp.argmax(scores, axis=1).astype(jnp.int32)
    raw_counts = jnp.where(valid, raw_counts, 0)
    raw_counts = jnp.where(dir_ids[None, :] == first_dir[:, None], CAP, raw_counts)
    rolled_ids = (first_dir[:, None] + dir_ids[None, :]) % 8
    rolled = jnp.take_along_axis(raw_counts, rolled_ids, axis=1)
    inclusive = jnp.cumsum(rolled, axis=1)
    movers = jnp.clip(NB // 4 - (inclusive - rolled), 0, rolled)
    upper_end = jnp.cumsum(movers, axis=1)
    lower_end = upper_end - movers
    moved = upper_end[:, -1]
    ranks = jnp.arange(NB, dtype=jnp.int32)
    peer_pos = jnp.sum((upper_end[:, None, :] <= ranks[None, :, None]).astype(jnp.int32), axis=2)
    peer_pos = jnp.minimum(peer_pos, 7)
    lower_at = jnp.take_along_axis(lower_end, peer_pos, axis=1)
    dest_dir = jnp.take_along_axis(rolled_ids, peer_pos, axis=1)
    is_mover = ranks[None, :] < moved[:, None]
    mover_cell = dest_dir * CAP + ranks[None, :] - lower_at
    stayer_cell = 8 * CAP + ranks[None, :] - moved[:, None]
    cell_index = jnp.where(is_mover, mover_cell, stayer_cell)
    mover_dev = device_ids[:, None] + step_x[dest_dir] * (N_GY * N_GZ) + step_y[dest_dir] * N_GZ
    dest_dev = jnp.where(is_mover, mover_dev, device_ids[:, None])

    def shuffle_cells(one_key):
        return jax.random.permutation(one_key, cells_dev).astype(jnp.int32)

    def shuffle_bricks(one_key):
        return jax.random.permutation(one_key, NB).astype(jnp.int32)
    shuffles = jax.vmap(shuffle_cells)(jax.random.split(key_cells, devices))
    placed = dest_dev * cells_dev + shuffles[dest_dev, cell_index]
    orders = jax.vmap(shuffle_bricks)(jax.random.split(key_order, devices))
    result = jnp.zeros((devices, NB), jnp.int32).at[device_ids[:, None], orders].set(placed.astype(jnp.int32))
    return result.reshape(devices * NB).astype(jnp.int32)


def draw_neighbour(key, part):
    key = jax.random.fold_in(key, 23)
    devices = N_GX * N_GY * N_GZ
    device_ids = jnp.arange(devices, dtype=jnp.int32)
    coords = (device_ids // (N_GY * N_GZ), device_ids // N_GZ % N_GY, device_ids % N_GZ)
    extents = (N_GX, N_GY, N_GZ)
    strides = (N_GY * N_GZ, N_GZ, 1)
    positions = jnp.arange(MB, dtype=jnp.int32)
    relative = positions - 2 * HC

    def shuffle_slots(one_key):
        return jax.random.permutation(one_key, MB).astype(jnp.int32)
    columns = []
    for axis_pos in range(3):
        axis_key = jax.random.fold_in(key, axis_pos)
        shuffles = jax.vmap(shuffle_slots)(jax.random.split(axis_key, devices))
        has_plus = coords[axis_pos] < extents[axis_pos] - 1
        has_minus = coords[axis_pos] > 0
        plus_dev = jnp.minimum(device_ids + strides[axis_pos], devices - 1)
        minus_dev = jnp.maximum(device_ids - strides[axis_pos], 0)
        later = jnp.minimum(positions + 1, MB - 1)
        earlier = jnp.maximum(positions - 1, 0)
        head_pos = jnp.minimum(positions, HC - 1)
        tail_pos = jnp.clip(positions - HC, 0, HC - 1)
        plus_remote = plus_dev[:, None] * MB + shuffles[plus_dev][:, HC + head_pos]
        plus_local = device_ids[:, None] * MB + shuffles[:, later]
        plus_pair = (relative >= 0) & (relative % 2 == 0) & (positions + 1 < MB)
        plus_value = jnp.where((positions < HC)[None, :] & has_plus[:, None], plus_remote, jnp.where(plus_pair[None, :], plus_local, -1))
        minus_remote = minus_dev[:, None] * MB + shuffles[minus_dev][:, tail_pos]
        minus_local = device_ids[:, None] * MB + shuffles[:, earlier]
        in_tail = (positions >= HC) & (positions < 2 * HC)
        minus_pair = (relative >= 1) & (relative % 2 == 1)
        minus_value = jnp.where(in_tail[None, :] & has_minus[:, None], minus_remote, jnp.where(minus_pair[None, :], minus_local, -1))
        minus_slots = jnp.zeros((devices, MB), jnp.int32).at[device_ids[:, None], shuffles].set(minus_value.astype(jnp.int32))
        plus_slots = jnp.zeros((devices, MB), jnp.int32).at[device_ids[:, None], shuffles].set(plus_value.astype(jnp.int32))
        columns.append(minus_slots)
        columns.append(plus_slots)
    return jnp.stack(columns, axis=-1).reshape(devices * MB, 6).astype(jnp.int32)


def block_scale(own_key, extent, cuts, low, largest):
    loudness = 1.0
    for dim, blocks in cuts:
        steps = jax.random.uniform(jax.random.fold_in(jax.random.fold_in(own_key, 6), dim), (blocks,), jnp.float32, low / len(cuts), largest / len(cuts))
        loudness = loudness * jnp.repeat(jnp.exp(steps), extent[dim] // blocks).reshape((-1,) + (1,) * (len(extent) - 1 - dim))
    return loudness


def scatter_about(key, extent, width, most, cuts=(), kind=jnp.bfloat16):
    values = width * jax.random.normal(key, extent, jnp.float32)
    if cuts:
        values = values * block_scale(key, extent, cuts, -0.22, 0.18)
    return jnp.clip(values, -most, most).astype(kind)


def setup_inputs(seed: int = 0) -> dict:
    arg_keys = jax.random.split(jax.random.key(seed), 7)
    return {
        "fine_field": scatter_about(arg_keys[0], (FINE, 8, 8, C), 1.0, 6.0, ((0, 256),)),
        "target": draw_target(jax.random.fold_in(arg_keys[6], 71), 0),
        "neighbour": draw_neighbour(jax.random.fold_in(arg_keys[6], 71), 0),
        "down_weight": scatter_about(arg_keys[3], (8 * C, C2), (8 * C) ** -0.5, 0.1875),
        "conv_weight": scatter_about(arg_keys[4], (7, C2, C2), (7 * C2) ** -0.5, 0.125),
        "out_cotangent": scatter_about(arg_keys[5], (COARSE, 4, 4, 4, C2), 1.0, 6.0, ((0, 256),)),
    }


opposite = (0, 2, 1, 4, 3, 6, 5)


def to_grid(octants, blocks):
    channels = octants.shape[-1]
    spread = octants.reshape(blocks, 2, 2, 2, 2, 2, 2, channels)
    return spread.transpose(0, 1, 4, 2, 5, 3, 6, 7).reshape(blocks, 4, 4, 4, channels)


def from_grid(grid_field):
    blocks = grid_field.shape[0]
    channels = grid_field.shape[-1]
    spread = grid_field.reshape(blocks, 2, 2, 2, 2, 2, 2, channels)
    return spread.transpose(0, 1, 3, 5, 2, 4, 6, 7).reshape(blocks * 8, 8, channels)


def silu_slope(values):
    sigmoid_v = jax.nn.sigmoid(values)
    return sigmoid_v * (1.0 + values * (1.0 - sigmoid_v))


def flatten_rows(values):
    return values.reshape(-1, values.shape[-1])


def shifted_views(center, face_list):
    view_list = [center]
    for axis_pos in range(3):
        grid_dim = axis_pos + 1
        lower_face = jnp.expand_dims(face_list[2 * axis_pos], grid_dim)
        upper_face = jnp.expand_dims(face_list[2 * axis_pos + 1], grid_dim)
        inner_lower = lax.slice_in_dim(center, 0, 3, axis=grid_dim)
        inner_upper = lax.slice_in_dim(center, 1, 4, axis=grid_dim)
        view_list.append(jnp.concatenate([lower_face, inner_lower], axis=grid_dim))
        view_list.append(jnp.concatenate([inner_upper, upper_face], axis=grid_dim))
    return view_list


def neighbour_faces(field, columns):
    face_list = []
    for column_index in range(6):
        column = columns[:, column_index]
        safe_index = jnp.maximum(column, 0)
        layer_at = 3 if column_index % 2 == 0 else 0
        picked = lax.index_in_dim(field[safe_index], layer_at, column_index // 2 + 1, keepdims=False)
        face_list.append(jnp.where((column >= 0)[:, None, None, None], picked, jnp.zeros_like(picked)))
    return face_list


def reference(fine_field, target, neighbour, down_weight, conv_weight, out_cotangent):
    voxel_scale = 1.0 / (64 * MB)
    fine_rows = fine_field.reshape(DEVICES, NB * 8, 8 * C)

    def down_block(rows_block):
        return jnp.dot(rows_block, down_weight, preferred_element_type=jnp.float32).astype(jnp.bfloat16)

    reduced = lax.map(down_block, fine_rows).reshape(FINE, 8, C2)
    octant_table = jnp.zeros((COARSE * 8, 8, C2), jnp.bfloat16).at[target].set(reduced)
    before_act = to_grid(octant_table, COARSE)
    hidden = jax.nn.silu(before_act.astype(jnp.float32)).astype(jnp.bfloat16)
    block_items = (hidden.reshape(DEVICES, MB, 4, 4, 4, C2), out_cotangent.reshape(DEVICES, MB, 4, 4, 4, C2),
                   before_act.reshape(DEVICES, MB, 4, 4, 4, C2), neighbour.reshape(DEVICES, MB, 6))

    def conv_block(running, entries):
        hid_block, grad_block, pre_block, nbr_block = entries
        hidden_views = shifted_views(hid_block, neighbour_faces(hidden, nbr_block))
        grad_views = shifted_views(grad_block, neighbour_faces(out_cotangent, nbr_block))
        grad_rows = flatten_rows(grad_block)
        summed = jnp.zeros((MB * 64, C2), jnp.float32)
        backward = jnp.zeros((MB * 64, C2), jnp.float32)
        weight_terms = []
        for direction in range(7):
            summed = summed + jnp.dot(flatten_rows(hidden_views[direction]), conv_weight[direction], preferred_element_type=jnp.float32)
            backward = backward + lax.dot_general(flatten_rows(grad_views[opposite[direction]]), conv_weight[direction],
                                                  (((1,), (1,)), ((), ())), preferred_element_type=jnp.float32)
            weight_terms.append(lax.dot_general(flatten_rows(hidden_views[direction]), grad_rows,
                                                (((0,), (0,)), ((), ())), preferred_element_type=jnp.float32))
        grad_before = (backward.reshape(pre_block.shape) * silu_slope(pre_block.astype(jnp.float32))).astype(jnp.bfloat16)
        return running + jnp.stack(weight_terms), (summed.astype(jnp.bfloat16).reshape(hid_block.shape), grad_before)

    conv_total, (coarse_field, grad_before) = lax.scan(conv_block, jnp.zeros((7, C2, C2), jnp.float32), block_items)
    grad_cells = from_grid(grad_before.reshape(COARSE, 4, 4, 4, C2))
    grad_reduced = grad_cells[target].reshape(DEVICES, NB * 8, C2)

    def fine_block(running, entries):
        rows_block, grad_block = entries
        flowed = lax.dot_general(grad_block, down_weight, (((1,), (1,)), ((), ())), preferred_element_type=jnp.float32).astype(jnp.bfloat16)
        summed = running + lax.dot_general(rows_block, grad_block, (((0,), (0,)), ((), ())), preferred_element_type=jnp.float32)
        return summed, flowed

    down_total, flowed = lax.scan(fine_block, jnp.zeros((8 * C, C2), jnp.float32), (fine_rows, grad_reduced))
    return (coarse_field.reshape(COARSE, 4, 4, 4, C2), flowed.reshape(FINE, 8, 8, C),
            down_total * voxel_scale, conv_total * voxel_scale)
```

```python
import functools

import jax
import jax.numpy as jnp
from jax import lax
from jax.experimental import pallas as pl
from jax.experimental.pallas import tpu as pltpu
from jax.sharding import PartitionSpec as P

MESH = pl.DeviceIdType.MESH
BF = jnp.bfloat16
F32 = jnp.float32
I32 = jnp.int32

NX, NY, NZ = 16, 8, 2
MB = 18
BP = 32
NB = 80
CELLS = 8 * MB

OPP = (0, 2, 1, 4, 3, 6, 5)
OFFS = ((0, 0, 0), (-1, 0, 0), (1, 0, 0), (0, -1, 0), (0, 1, 0), (0, 0, -1), (0, 0, 1))
DIRS = ((-1, -1), (-1, 0), (-1, 1), (0, -1), (0, 1), (1, -1), (1, 0), (1, 1))
KA, KD = 112, 64


def iota(shape, dim):
    return lax.broadcasted_iota(I32, shape, dim)


def dot(a, b):
    return jnp.dot(a, b, preferred_element_type=F32)


def dot_nt(a, b):
    return lax.dot_general(a, b, (((1,), (1,)), ((), ())), preferred_element_type=F32)


def onehot(mask):
    return jnp.where(mask, 1.0, 0.0).astype(BF)


def ninth(u):
    return lax.shift_right_arithmetic(u * 7282, 16)


def view(ext, x, d):
    dx, dy, dz = OFFS[d]
    rows = ext[1 + x + dx, 1 + dy:5 + dy, BP * (1 + dz):BP * (5 + dz), :]
    return rows.reshape(16 * BP, 256)


def layer_quad(ext, k, q):
    if k == 0:
        return ext[4, 1 + q, BP:5 * BP, :]
    if k == 1:
        return ext[1, 1 + q, BP:5 * BP, :]
    if k == 2:
        return ext[1 + q, 4, BP:5 * BP, :]
    if k == 3:
        return ext[1 + q, 1, BP:5 * BP, :]
    z = 4 if k == 4 else 1
    return ext[1 + q, 1:5, BP * z:BP * (z + 1), :].reshape(4 * BP, 256)


def put_halo(ext, k, q, rows):
    if k == 0:
        ext[0, 1 + q, BP:5 * BP, :] = rows
    elif k == 1:
        ext[5, 1 + q, BP:5 * BP, :] = rows
    elif k == 2:
        ext[1 + q, 0, BP:5 * BP, :] = rows
    elif k == 3:
        ext[1 + q, 5, BP:5 * BP, :] = rows
    else:
        z = 0 if k == 4 else 5
        ext[1 + q, 1:5, BP * z:BP * (z + 1), :] = rows.reshape(4, BP, 256)


def kernel(fine, tgtc, tgtr, nbc, nbr, wd, wc, cot,
           coarse_o, fineg_o, ga, gd,
           cotx, hidx, gh, red, fine_t, hid_t, gbuf, gr, selc, selp,
           osnd, orcv, rsnd, rrcv, fsnd, frcv, hsnd, hrcv,
           pa, pd, ca, cd, qa, qd, xa, xd, za, zd, ya, yd, wa, wdn,
           csem, osem, rsem, fsem, hsem, coresem, xsem, zsem, zgsem, xgsem, cgsem):
    gx, gy, gz = lax.axis_index("gx"), lax.axis_index("gy"), lax.axis_index("gz")
    myself = (gx * NY + gy) * NZ + gz

    def at(dx, dy):
        return (lax.rem(gx + dx + NX, NX), lax.rem(gy + dy + NY, NY), gz)

    other = (gx, gy, 1 - gz)

    barrier = pltpu.get_barrier_semaphore()
    peers = [at(k, 0) for k in range(1, NX)] + [at(0, k) for k in range(1, NY)]
    peers += [at(a, b) for a in (-1, 1) for b in (-1, 1)] + [other]
    for peer in peers:
        pl.semaphore_signal(barrier, inc=1, device_id=peer, device_id_type=MESH)

    cot_in = pltpu.make_async_copy(cot, cotx.at[1:5, 1:5, BP:5 * BP, :], csem)
    cot_in.start()

    def remote(src, dst, sems, i, device):
        return pltpu.make_async_remote_copy(
            src_ref=src, dst_ref=dst, send_sem=sems.at[0, i], recv_sem=sems.at[1, i],
            device_id=device, device_id_type=MESH)

    def place(t):
        owner = ninth(lax.shift_right_arithmetic(t, 4))
        cell = t - owner * CELLS
        moving = owner != myself
        sx = lax.shift_right_arithmetic(owner, 4) - gx
        sy = (lax.shift_right_arithmetic(owner, 1) & 7) - gy
        flat = (sx + 1) * 3 + (sy + 1)
        return cell, moving, jnp.where(flat > 4, flat - 1, flat)

    cell_c, moving_c, dest_c = place(tgtc[...])
    cell_r, moving_r, dest_r = place(tgtr[...])
    member_c = jnp.where(moving_c & (dest_c == iota((NB, 128), 1)), 1.0, 0.0)
    lower = onehot(iota((NB, NB), 1) < iota((NB, NB), 0))
    order_c = jnp.sum(dot(lower, member_c.astype(BF)) * member_c, axis=1, keepdims=True)
    member_r = jnp.where(moving_r & (dest_r == iota((16, NB), 0)), 1.0, 0.0)
    upper = onehot(iota((NB, NB), 0) < iota((NB, NB), 1))
    order_r = jnp.sum(dot(member_r.astype(BF), upper) * member_r, axis=0, keepdims=True)
    key_c = jnp.where(moving_c, dest_c * 16 + order_c.astype(I32), -1000)
    key_r = jnp.where(moving_r, dest_r * 16 + order_r.astype(I32), -1000)

    def table_name(shape, dim):
        r = iota(shape, dim)
        b = r & 31
        return jnp.where(b < MB, b * 8 + lax.shift_right_arithmetic(r, 5), -7)

    send_hot = [onehot(key_r + 8 * h == iota((128, NB), 0)) for h in range(2)]
    back_hot = [onehot(key_c + 8 * h == iota((NB, 128), 1)) for h in range(2)]
    stay_c = onehot((cell_c == table_name((NB, 256), 1)) & jnp.logical_not(moving_c))
    stay_r = onehot((cell_r == table_name((256, NB), 0)) & jnp.logical_not(moving_r))

    red[...] = dot(fine[...], wd[...]).astype(BF)
    for pair in range(4):
        out = sum(dot(send_hot[h], red[(2 * pair + h) * NB:(2 * pair + h + 1) * NB, :]) for h in range(2))
        out = out.astype(BF)
        for d in range(8):
            osnd[d, pair * 16:(pair + 1) * 16, :] = out[d * 16:(d + 1) * 16]
    tags = jnp.broadcast_to((cell_c + 1).astype(F32), (NB, 256)).astype(BF)
    out = (dot(send_hot[0], tags) + dot(send_hot[1], tags)).astype(BF)
    for d in range(8):
        osnd[d, 64:80, :] = out[d * 16:(d + 1) * 16]

    pl.semaphore_wait(barrier, len(peers))
    octs = [remote(osnd.at[d], orcv.at[d], osem, d, at(*DIRS[d])) for d in range(8)]
    for c in octs:
        c.start()

    quad_c = lax.shift_right_arithmetic(iota((128, 128), 0), 5)
    lane = iota((128, 128), 1)

    def names(v):
        owner = ninth(lax.shift_right_arithmetic(v, 1))
        return v - owner * MB, (v >= 0) & (owner == myself), (v >= 0) & (owner != myself)

    for k in range(6):
        vc = nbc[:, k:k + 1]
        vr = nbr[k:k + 1, :]
        idx_c, home_c, far_c = names(vc)
        idx_r, home_r, far_r = names(vr)
        less = far_r & (vr < vc) & (lane < 32)
        rank_c = jnp.sum(jnp.where(less, 1.0, 0.0), axis=1, keepdims=True).astype(I32)
        selp[k, :, 0:128] = onehot(home_c & (idx_c + 32 * quad_c == lane))
        selp[k, :, 128:256] = onehot(far_c & (rank_c + 8 * quad_c == lane))
        early = far_c[0:32] & (iota((32, 128), 0) < (iota((32, 128), 1) & 31))
        rank_r = jnp.sum(jnp.where(early, 1.0, 0.0), axis=0, keepdims=True).astype(I32)
        slot = rank_r + 8 * lax.shift_right_arithmetic(iota((32, 128), 1), 5)
        selc[k] = onehot(far_r & (slot == iota((32, 128), 0)))

    face_to = (at(1, 0), at(-1, 0), at(0, 1), at(0, -1), other)

    def send_faces(ext, snd, rcv, sems):
        for k in range(4):
            for q in range(4):
                snd[k, q * 32:(q + 1) * 32, :] = dot(selc[OPP[k + 1] - 1], layer_quad(ext, k, q)).astype(BF)
        for q in range(4):
            both = dot(selc[5], layer_quad(ext, 4, q)) + dot(selc[4], layer_quad(ext, 5, q))
            snd[4, q * 32:(q + 1) * 32, :] = both.astype(BF)
        copies = [remote(snd.at[k], rcv.at[k], sems, k, face_to[k]) for k in range(5)]
        for c in copies:
            c.start()
        return copies

    def take_faces(ext, rcv, copies):
        for c in copies:
            c.wait_recv()
        for k in range(6):
            for q in range(4):
                near = dot(selp[k, :, 0:128], layer_quad(ext, k, q))
                far = dot(selp[k, :, 128:160], rcv[min(k, 4), q * 32:(q + 1) * 32, :])
                put_halo(ext, k, q, (near + far).astype(BF))

    cot_in.wait()
    cot_faces = send_faces(cotx, fsnd, frcv, fsem)
    fine_t[...] = fine[...].T
    take_faces(cotx, frcv, cot_faces)

    def back_conv(x, carry):
        acc = dot_nt(view(cotx, x, 0), wc[0])
        for d in range(1, 7):
            acc = acc + dot_nt(view(cotx, x, OPP[d]), wc[d])
        gh[x] = acc
        return carry

    lax.fori_loop(0, 4, back_conv, 0)

    for c in octs:
        c.wait_recv()
    tag = orcv[:, 64:80, :].reshape(128, 256).astype(F32)
    row_half = lax.shift_right_arithmetic(iota((128, 256), 0), 3) & 1
    match = tag - 1.0 == table_name((128, 256), 1).astype(F32)
    came = [jnp.where(match & (row_half == h), 1.0, 0.0) for h in range(2)]
    came_t = [m.T.astype(BF) for m in came]
    came = [m.astype(BF) for m in came]
    for c in range(8):
        i, j, k = c >> 2, (c >> 1) & 1, c & 1
        pair = c >> 1
        got = orcv[:, pair * 16:(pair + 1) * 16, :].reshape(128, 256)
        pre = dot(came_t[c & 1], got) + dot(stay_r, red[c * NB:(c + 1) * NB, :])
        sig = 1.0 / (1.0 + jnp.exp(-pre))
        hid = (pre * sig).astype(BF)
        slope = sig * (1.0 + pre * (1.0 - sig))
        for o in range(8):
            x, y, z = 2 * (o >> 2) + i, 2 * ((o >> 1) & 1) + j, 2 * (o & 1) + k
            rows = slice(o * BP, (o + 1) * BP)
            hidx[1 + x, 1 + y, BP * (1 + z):BP * (2 + z), :] = hid[rows]
            grad = gh[x, (y * 4 + z) * BP:(y * 4 + z + 1) * BP, :]
            gbuf[c, rows, :] = (grad * slope[rows]).astype(BF)

    for pair in range(4):
        out = (dot(came[0], gbuf[2 * pair]) + dot(came[1], gbuf[2 * pair + 1])).astype(BF)
        for d in range(8):
            rsnd[d, pair * 16:(pair + 1) * 16, :] = out[d * 16:(d + 1) * 16]
    rets = [remote(rsnd.at[d], rrcv.at[d], rsem, d, at(-DIRS[d][0], -DIRS[d][1])) for d in range(8)]
    for c in rets:
        c.start()
    hid_faces = send_faces(hidx, hsnd, hrcv, hsem)

    for x in range(4):
        hid_t[:, x * 512:(x + 1) * 512] = view(hidx, x, 0).T
    for d in range(7):
        acc = dot(hid_t[:, 0:512], view(cotx, 0, OPP[d]))
        for x in range(1, 4):
            acc = acc + dot(hid_t[:, x * 512:(x + 1) * 512], view(cotx, x, OPP[d]))
        acc = acc.astype(BF)
        for h in range(2):
            pa[h, d * 256:(d + 1) * 256, :] = acc[:, h * 128:(h + 1) * 128]
    core_a = remote(pa.at[1 - gz], ca, coresem, 0, other)
    core_a.start()

    for c in rets:
        c.wait_recv()
    for c in range(8):
        back = rrcv[:, (c >> 1) * 16:(c >> 1) * 16 + 16, :].reshape(128, 256)
        gr[c * NB:(c + 1) * NB, :] = (dot(stay_c, gbuf[c]) + dot(back_hot[c & 1], back)).astype(BF)
    for m in range(4):
        acc = dot(fine_t[m * 256:(m + 1) * 256, :], gr[...]).astype(BF)
        for h in range(2):
            pd[h, m * 256:(m + 1) * 256, :] = acc[:, h * 128:(h + 1) * 128]
    core_d = remote(pd.at[1 - gz], cd, coresem, 1, other)
    core_d.start()

    def x_start(core, p, cbuf, q, xbuf, n, s):
        core.wait_recv()
        q[...] = (p[gz].astype(F32) + cbuf[...].astype(F32)).astype(BF)
        copies = []
        for k in range(1, NX):
            to = at(k, 0)
            copies.append(remote(q.at[pl.ds(pl.multiple_of(to[0] * n, 16), n)], xbuf.at[k], xsem, s * NX + k, to))
        for c in copies:
            c.start()
        return copies

    def z_start(copies, q, xbuf, zbuf, ybuf, n, s):
        for c in copies:
            c.wait_recv()
        acc = q[pl.ds(pl.multiple_of(gx * n, 16), n), :].astype(F32)
        for k in range(1, NX):
            acc = acc + xbuf[k].astype(F32)
        units = n // 16
        zbuf[0:units] = acc.astype(BF).reshape(units, 16, 128)
        zbuf[units:8] = jnp.zeros((8 - units, 16, 128), BF)
        out = []
        for k in range(1, NY):
            to = at(0, k)
            out.append(remote(zbuf.at[to[1]], ybuf.at[k], zsem, s * NY + k, to))
        for c in out:
            c.start()
        return out

    def zg_start(copies, zbuf, ybuf, wbuf, s):
        for c in copies:
            c.wait_recv()
        acc = zbuf[gy].astype(F32)
        for k in range(1, NY):
            acc = acc + ybuf[k].astype(F32)
        wbuf[gy] = acc.astype(BF)
        out = [remote(wbuf.at[gy], wbuf.at[gy], zgsem, s * NY + k, at(0, k)) for k in range(1, NY)]
        for c in out:
            c.start()
        return out

    def xg_start(copies, wbuf, g, n, s):
        for c in copies:
            c.wait_recv()
        mine = pl.ds(pl.multiple_of(gx * n, 16), n)
        g[gz, mine, :] = wbuf[0:n // 16].reshape(n, 128)
        out = [remote(g.at[gz, mine], g.at[gz, mine], xgsem, s * NX + k, at(k, 0)) for k in range(1, NX)]
        for c in out:
            c.start()
        return out

    def cg_start(copies, g, s):
        for c in copies:
            c.wait_recv()
        out = remote(g.at[gz], g.at[gz], cgsem, s, other)
        out.start()
        return out

    xs_a = x_start(core_a, pa, ca, qa, xa, KA, 0)
    xs_d = x_start(core_d, pd, cd, qd, xd, KD, 1)

    take_faces(hidx, hrcv, hid_faces)

    def conv(x, carry):
        acc = dot(view(hidx, x, 0), wc[0])
        for d in range(1, 7):
            acc = acc + dot(view(hidx, x, d), wc[d])
        coarse_o[x] = acc.astype(BF)
        return carry

    lax.fori_loop(0, 4, conv, 0)
    zs_a = z_start(xs_a, qa, xa, za, ya, KA, 0)
    zs_d = z_start(xs_d, qd, xd, zd, yd, KD, 1)
    fineg_o[...] = dot_nt(gr[...], wd[...]).astype(BF)

    zg_a = zg_start(zs_a, za, ya, wa, 0)
    zg_d = zg_start(zs_d, zd, yd, wdn, 1)
    xg_a = xg_start(zg_a, wa, ga, KA, 0)
    xg_d = xg_start(zg_d, wdn, gd, KD, 1)
    cg_a = cg_start(xg_a, ga, 0)
    cg_d = cg_start(xg_d, gd, 1)
    cg_a.wait_recv()
    cg_d.wait_recv()

    for c in (octs + cot_faces + rets + hid_faces + [core_a, core_d] + xs_a + xs_d + zs_a + zs_d
              + zg_a + zg_d + xg_a + xg_d + [cg_a, cg_d]):
        c.wait_send()


def shards(fine_field, target, neighbour, down_weight, conv_weight, out_cotangent):
    fine = fine_field.reshape(NB, 8, 1024).transpose(1, 0, 2).reshape(8 * NB, 1024)
    cot = jnp.pad(out_cotangent.transpose(1, 2, 3, 0, 4), ((0, 0), (0, 0), (0, 0), (0, BP - MB), (0, 0)))
    cot = cot.reshape(4, 4, 4 * BP, 256)
    nb = jnp.pad(neighbour, ((0, BP - MB), (0, 2)), constant_values=-1)
    nbc = jnp.tile(nb, (4, 1))
    vmem = pl.BlockSpec(memory_space=pltpu.VMEM)
    dma = pltpu.SemaphoreType.DMA
    coarse, fineg, ga, gd = pl.pallas_call(
        kernel,
        out_shape=(
            jax.ShapeDtypeStruct((4, 512, 256), BF),
            jax.ShapeDtypeStruct((8 * NB, 1024), BF),
            jax.ShapeDtypeStruct((2, 1792, 128), BF),
            jax.ShapeDtypeStruct((2, 1024, 128), BF),
        ),
        in_specs=[vmem] * 7 + [pl.BlockSpec(memory_space=pl.ANY)],
        out_specs=[vmem] * 4,
        scratch_shapes=[
            pltpu.VMEM((6, 6, 6 * BP, 256), BF),
            pltpu.VMEM((6, 6, 6 * BP, 256), BF),
            pltpu.VMEM((4, 512, 256), F32),
            pltpu.VMEM((8 * NB, 256), BF),
            pltpu.VMEM((1024, 8 * NB), BF),
            pltpu.VMEM((256, 2048), BF),
            pltpu.VMEM((8, 256, 256), BF),
            pltpu.VMEM((8 * NB, 256), BF),
            pltpu.VMEM((6, 32, 128), BF),
            pltpu.VMEM((6, 128, 256), BF),
            pltpu.VMEM((8, 80, 256), BF),
            pltpu.VMEM((8, 80, 256), BF),
            pltpu.VMEM((8, 64, 256), BF),
            pltpu.VMEM((8, 64, 256), BF),
            pltpu.VMEM((5, 128, 256), BF),
            pltpu.VMEM((5, 128, 256), BF),
            pltpu.VMEM((5, 128, 256), BF),
            pltpu.VMEM((5, 128, 256), BF),
            pltpu.VMEM((2, 1792, 128), BF),
            pltpu.VMEM((2, 1024, 128), BF),
            pltpu.VMEM((1792, 128), BF),
            pltpu.VMEM((1024, 128), BF),
            pltpu.VMEM((1792, 128), BF),
            pltpu.VMEM((1024, 128), BF),
            pltpu.VMEM((NX, KA, 128), BF),
            pltpu.VMEM((NX, KD, 128), BF),
            pltpu.VMEM((NY, 16, 128), BF),
            pltpu.VMEM((NY, 16, 128), BF),
            pltpu.VMEM((NY, 16, 128), BF),
            pltpu.VMEM((NY, 16, 128), BF),
            pltpu.VMEM((NY, 16, 128), BF),
            pltpu.VMEM((NY, 16, 128), BF),
            dma,
            dma((2, 8)),
            dma((2, 8)),
            dma((2, 5)),
            dma((2, 5)),
            dma((2, 2)),
            dma((2, 2 * NX)),
            dma((2, 2 * NY)),
            dma((2, 2 * NY)),
            dma((2, 2 * NX)),
            dma((2, 2)),
        ],
        compiler_params=pltpu.CompilerParams(
            collective_id=0, has_side_effects=True, vmem_limit_bytes=56 * 1024 * 1024),
        cost_estimate=pl.CostEstimate(flops=6_000_000_000, bytes_accessed=10_000_000, transcendentals=600_000),
    )(fine, target.reshape(NB, 1), target.reshape(1, NB), nbc, nbc.T, down_weight, conv_weight, cot)

    scale = 1.0 / (64 * MB)
    coarse = coarse.reshape(4, 4, 4, BP, 256)[:, :, :, :MB].transpose(3, 0, 1, 2, 4)
    fineg = fineg.reshape(8, NB, 1024).transpose(1, 0, 2).reshape(NB, 8, 8, 128)
    conv_g = jnp.concatenate([ga[0], ga[1]], axis=1).astype(F32) * scale
    down_g = jnp.concatenate([gd[0], gd[1]], axis=1).astype(F32) * scale
    return coarse, fineg, down_g, conv_g.reshape(7, 256, 256)


def solution(mesh):
    every = ("gx", "gy", "gz")
    in_specs = (
        P(every, None, None, None),
        P(every),
        P(every, None),
        P(),
        P(),
        P(every, None, None, None, None),
    )
    out_specs = (
        P(every, None, None, None, None),
        P(every, None, None, None),
        P(),
        P(),
    )
    return jax.shard_map(shards, mesh=mesh, in_specs=in_specs, out_specs=out_specs, check_vma=False)
```

```python
import functools

import jax
import jax.numpy as jnp
from jax import lax
from jax.experimental import pallas as pl
from jax.experimental.pallas import tpu as pltpu
from jax.sharding import PartitionSpec as P

MESH = pl.DeviceIdType.MESH
BF = jnp.bfloat16
F32 = jnp.float32
I32 = jnp.int32

NX, NY, NZ = 16, 8, 2
MB = 18
BP = 32
NB = 80
CELLS = 8 * MB

OPP = (0, 2, 1, 4, 3, 6, 5)
OFFS = ((0, 0, 0), (-1, 0, 0), (1, 0, 0), (0, -1, 0), (0, 1, 0), (0, 0, -1), (0, 0, 1))
DIRS = ((-1, -1), (-1, 0), (-1, 1), (0, -1), (0, 1), (1, -1), (1, 0), (1, 1))
KA, KD = 112, 64


def iota(shape, dim):
    return lax.broadcasted_iota(I32, shape, dim)


def dot(a, b):
    return jnp.dot(a, b, preferred_element_type=F32)


def dot_nt(a, b):
    return lax.dot_general(a, b, (((1,), (1,)), ((), ())), preferred_element_type=F32)


def onehot(mask):
    return jnp.where(mask, 1.0, 0.0).astype(BF)


def ninth(u):
    return lax.shift_right_arithmetic(u * 7282, 16)


def view(ext, x, d):
    dx, dy, dz = OFFS[d]
    rows = ext[1 + x + dx, 1 + dy:5 + dy, BP * (1 + dz):BP * (5 + dz), :]
    return rows.reshape(16 * BP, 256)


def layer_quad(ext, k, q):
    if k == 0:
        return ext[4, 1 + q, BP:5 * BP, :]
    if k == 1:
        return ext[1, 1 + q, BP:5 * BP, :]
    if k == 2:
        return ext[1 + q, 4, BP:5 * BP, :]
    if k == 3:
        return ext[1 + q, 1, BP:5 * BP, :]
    z = 4 if k == 4 else 1
    return ext[1 + q, 1:5, BP * z:BP * (z + 1), :].reshape(4 * BP, 256)


def put_halo(ext, k, q, rows):
    if k == 0:
        ext[0, 1 + q, BP:5 * BP, :] = rows
    elif k == 1:
        ext[5, 1 + q, BP:5 * BP, :] = rows
    elif k == 2:
        ext[1 + q, 0, BP:5 * BP, :] = rows
    elif k == 3:
        ext[1 + q, 5, BP:5 * BP, :] = rows
    else:
        z = 0 if k == 4 else 5
        ext[1 + q, 1:5, BP * z:BP * (z + 1), :] = rows.reshape(4, BP, 256)


def kernel(fine_h, tgt, nb, wd_h, wc_h, cot_h,
           coarse_h, fineg_h, ga, gd,
           fin, cin, wd, wc, wt, t_scr, n_scr, wide, tall, fine, coarse_v, fineg_v,
           cotx, hidx, gh, red, slope, fine_t, hid_t, gr, selc, selp,
           osnd, orcv, rsnd, rrcv, fsnd, frcv, hsnd, hrcv,
           pa, pd, ca, cd, qa, qd, xa, xd, za, ya, yd, wa,
           isem, esem, osem, rsem, fsem, hsem, coresem, xsem, zsem, zgsem, xgsem, cgsem):
    gx, gy, gz = lax.axis_index("gx"), lax.axis_index("gy"), lax.axis_index("gz")
    myself = (gx * NY + gy) * NZ + gz

    def at(dx, dy):
        return (lax.rem(gx + dx + NX, NX), lax.rem(gy + dy + NY, NY), gz)

    other = (gx, gy, 1 - gz)

    barrier = pltpu.get_barrier_semaphore()
    peers = [at(k, 0) for k in range(1, NX)] + [at(0, k) for k in range(1, NY)]
    peers += [at(a, b) for a in (-1, 1) for b in (-1, 1)] + [other]
    for peer in peers:
        pl.semaphore_signal(barrier, inc=1, device_id=peer, device_id_type=MESH)

    loads = [pltpu.make_async_copy(src, dst, isem.at[i]) for i, (src, dst) in enumerate(
        ((cot_h, cin), (fine_h, fin), (wd_h, wd), (wc_h, wc)))]
    for c in loads:
        c.start()

    def remote(src, dst, sems, i, device):
        return pltpu.make_async_remote_copy(
            src_ref=src, dst_ref=dst, send_sem=sems.at[0, i], recv_sem=sems.at[1, i],
            device_id=device, device_id_type=MESH)

    quad_c = lax.shift_right_arithmetic(iota((128, 128), 0), 5)
    lane = iota((128, 128), 1)

    n_scr[...] = jnp.full((8, 128), -1, I32)
    for q in range(4):
        n_scr[0:6, BP * q:BP * q + MB] = nb[...]
    nb_r = n_scr[...]
    nb_c = nb_r.T

    def names(v):
        owner = ninth(lax.shift_right_arithmetic(v, 1))
        return v - owner * MB, (v >= 0) & (owner == myself), (v >= 0) & (owner != myself)

    for k in range(6):
        vc = nb_c[:, k:k + 1]
        vr = nb_r[k:k + 1, :]
        idx_c, home_c, far_c = names(vc)
        idx_r, home_r, far_r = names(vr)
        less = far_r & (vr < vc) & (lane < 32)
        rank_c = jnp.sum(jnp.where(less, 1.0, 0.0), axis=1, keepdims=True).astype(I32)
        selp[k, :, 0:128] = onehot(home_c & (idx_c + 32 * quad_c == lane))
        selp[k, :, 128:256] = onehot(far_c & (rank_c + 8 * quad_c == lane))
        early = far_c[0:32] & (iota((32, 128), 0) < (iota((32, 128), 1) & 31))
        rank_r = jnp.sum(jnp.where(early, 1.0, 0.0), axis=0, keepdims=True).astype(I32)
        slot = rank_r + 8 * lax.shift_right_arithmetic(iota((32, 128), 1), 5)
        selc[k] = onehot(far_r & (slot == iota((32, 128), 0)))

    face_to = (at(1, 0), at(-1, 0), at(0, 1), at(0, -1), other)

    def send_faces(ext, snd, rcv, sems):
        for k in range(4):
            for q in range(4):
                snd[k, q * 32:(q + 1) * 32, :] = dot(selc[OPP[k + 1] - 1], layer_quad(ext, k, q)).astype(BF)
        for q in range(4):
            both = dot(selc[5], layer_quad(ext, 4, q)) + dot(selc[4], layer_quad(ext, 5, q))
            snd[4, q * 32:(q + 1) * 32, :] = both.astype(BF)
        copies = [remote(snd.at[k], rcv.at[k], sems, k, face_to[k]) for k in range(5)]
        for c in copies:
            c.start()
        return copies

    def take_faces(ext, rcv, copies):
        for c in copies:
            c.wait_recv()
        for k in range(6):
            for q in range(4):
                near = dot(selp[k, :, 0:128], layer_quad(ext, k, q))
                far = dot(selp[k, :, 128:160], rcv[min(k, 4), q * 32:(q + 1) * 32, :])
                put_halo(ext, k, q, (near + far).astype(BF))

    loads[0].wait()
    tall[...] = jnp.zeros_like(tall)
    for m in range(16 * MB):
        part = cin[m].astype(F32)
        for h in range(2):
            tall[h, 4 * m:4 * m + 4, :] = part[:, h * 128:(h + 1) * 128]
    for p in range(64):
        x, y, z = p >> 4, (p >> 2) & 3, p & 3
        for h in range(2):
            rows = tall[h, pl.ds(p, BP, stride=64), :]
            cotx[1 + x, 1 + y, BP * (1 + z):BP * (2 + z), h * 128:(h + 1) * 128] = rows.astype(BF)
    pl.semaphore_wait(barrier, len(peers))
    cot_faces = send_faces(cotx, fsnd, frcv, fsem)

    def place(t):
        owner = ninth(lax.shift_right_arithmetic(t, 4))
        cell = t - owner * CELLS
        moving = owner != myself
        sx = lax.shift_right_arithmetic(owner, 4) - gx
        sy = (lax.shift_right_arithmetic(owner, 1) & 7) - gy
        flat = (sx + 1) * 3 + (sy + 1)
        return cell, moving, jnp.where(flat > 4, flat - 1, flat)

    t_scr[:, 0:NB] = jnp.broadcast_to(tgt[...], (128, NB))
    cell_c, moving_c, dest_c = place(t_scr[...].T[0:NB, 0:1])
    cell_r, moving_r, dest_r = place(tgt[...])
    member_c = jnp.where(moving_c & (dest_c == iota((NB, 128), 1)), 1.0, 0.0)
    lower = onehot(iota((NB, NB), 1) < iota((NB, NB), 0))
    order_c = jnp.sum(dot(lower, member_c.astype(BF)) * member_c, axis=1, keepdims=True)
    member_r = jnp.where(moving_r & (dest_r == iota((16, NB), 0)), 1.0, 0.0)
    upper = onehot(iota((NB, NB), 0) < iota((NB, NB), 1))
    order_r = jnp.sum(dot(member_r.astype(BF), upper) * member_r, axis=0, keepdims=True)
    key_c = jnp.where(moving_c, dest_c * 16 + order_c.astype(I32), -1000)
    key_r = jnp.where(moving_r, dest_r * 16 + order_r.astype(I32), -1000)

    def table_name(shape, dim):
        r = iota(shape, dim)
        b = r & 31
        return jnp.where(b < MB, b * 8 + lax.shift_right_arithmetic(r, 5), -7)

    send_hot = [onehot(key_r + 8 * h == iota((128, NB), 0)) for h in range(2)]
    back_hot = [onehot(key_c + 8 * h == iota((NB, 128), 1)) for h in range(2)]
    stay_c = onehot((cell_c == table_name((NB, 256), 1)) & jnp.logical_not(moving_c))
    stay_r = onehot((cell_r == table_name((256, NB), 0)) & jnp.logical_not(moving_r))

    loads[1].wait()
    wide[...] = fin[...].astype(F32)
    for c in range(8):
        for v in range(8):
            part = wide[pl.ds(c * 8 + v, NB, stride=64), :]
            fine[c * NB:(c + 1) * NB, v * 128:(v + 1) * 128] = part.astype(BF)
    loads[2].wait()
    red[...] = dot(fine[...], wd[...]).astype(BF)
    for pair in range(4):
        out = sum(dot(send_hot[h], red[(2 * pair + h) * NB:(2 * pair + h + 1) * NB, :]) for h in range(2))
        out = out.astype(BF)
        for d in range(8):
            osnd[d, pair * 16:(pair + 1) * 16, :] = out[d * 16:(d + 1) * 16]
    tags = jnp.broadcast_to((cell_c + 1).astype(F32), (NB, 256)).astype(BF)
    out = (dot(send_hot[0], tags) + dot(send_hot[1], tags)).astype(BF)
    for d in range(8):
        osnd[d, 64:80, :] = out[d * 16:(d + 1) * 16]

    octs = [remote(osnd.at[d], orcv.at[d], osem, d, at(*DIRS[d])) for d in range(8)]
    for c in octs:
        c.start()

    fine_t[...] = fine[...].T
    pre = red[...].astype(F32)
    sig = 1.0 / (1.0 + jnp.exp(-pre))
    slope[...] = sig * (1.0 + pre * (1.0 - sig))
    loads[3].wait()
    for d in range(7):
        wt[d * 256:(d + 1) * 256, :] = wc[d * 256:(d + 1) * 256, :].T
    take_faces(cotx, frcv, cot_faces)

    def back_conv(x, carry):
        rows = jnp.concatenate([view(cotx, x, OPP[d]) for d in range(7)], axis=1)
        gh[x] = dot(rows, wt[...]).astype(BF)
        return carry

    lax.fori_loop(0, 4, back_conv, 0)

    for c in octs:
        c.wait_recv()
    tag = orcv[:, 64:80, :].reshape(128, 256).astype(F32)
    row_half = lax.shift_right_arithmetic(iota((128, 256), 0), 3) & 1
    match = tag - 1.0 == table_name((128, 256), 1).astype(F32)
    came = [jnp.where(match & (row_half == h), 1.0, 0.0) for h in range(2)]
    came_t = [m.T.astype(BF) for m in came]
    came = [m.astype(BF) for m in came]

    def grads(c):
        i, j, k = c >> 2, (c >> 1) & 1, c & 1
        out = []
        for o in range(8):
            x, y, z = 2 * (o >> 2) + i, 2 * ((o >> 1) & 1) + j, 2 * (o & 1) + k
            out.append(gh[x, (y * 4 + z) * BP:(y * 4 + z + 1) * BP, :])
        return jnp.concatenate(out, axis=0)

    for pair in range(4):
        out = (dot(came[0], grads(2 * pair)) + dot(came[1], grads(2 * pair + 1))).astype(BF)
        for d in range(8):
            rsnd[d, pair * 16:(pair + 1) * 16, :] = out[d * 16:(d + 1) * 16]
    rets = [remote(rsnd.at[d], rrcv.at[d], rsem, d, at(-DIRS[d][0], -DIRS[d][1])) for d in range(8)]
    for c in rets:
        c.start()

    for c in range(8):
        i, j, k = c >> 2, (c >> 1) & 1, c & 1
        pair = c >> 1
        got = orcv[:, pair * 16:(pair + 1) * 16, :].reshape(128, 256)
        pre = dot(came_t[c & 1], got) + dot(stay_r, red[c * NB:(c + 1) * NB, :])
        hid = (pre / (1.0 + jnp.exp(-pre))).astype(BF)
        for o in range(8):
            x, y, z = 2 * (o >> 2) + i, 2 * ((o >> 1) & 1) + j, 2 * (o & 1) + k
            hidx[1 + x, 1 + y, BP * (1 + z):BP * (2 + z), :] = hid[o * BP:(o + 1) * BP]
    hid_faces = send_faces(hidx, hsnd, hrcv, hsem)

    for x in range(4):
        hid_t[:, x * 512:(x + 1) * 512] = view(hidx, x, 0).T
    for d in range(7):
        rows = jnp.concatenate([view(cotx, x, OPP[d]) for x in range(4)], axis=0)
        acc = dot(hid_t[...], rows).astype(BF)
        for h in range(2):
            pa[h, d * 256:(d + 1) * 256, :] = acc[:, h * 128:(h + 1) * 128]
    core_a = remote(pa.at[1 - gz], ca, coresem, 0, other)
    core_a.start()

    for c in rets:
        c.wait_recv()
    for c in range(8):
        back = rrcv[:, (c >> 1) * 16:(c >> 1) * 16 + 16, :].reshape(128, 256)
        grad = dot(stay_c, grads(c)) + dot(back_hot[c & 1], back)
        gr[c * NB:(c + 1) * NB, :] = (grad * slope[c * NB:(c + 1) * NB, :]).astype(BF)
    for m in range(4):
        acc = dot(fine_t[m * 256:(m + 1) * 256, :], gr[...]).astype(BF)
        for h in range(2):
            pd[h, m * 256:(m + 1) * 256, :] = acc[:, h * 128:(h + 1) * 128]
    core_d = remote(pd.at[1 - gz], cd, coresem, 1, other)
    core_d.start()

    def x_start(core, p, cbuf, q, xbuf, n, s):
        core.wait_recv()
        q[...] = (p[gz].astype(F32) + cbuf[...].astype(F32)).astype(BF)
        copies = []
        for k in range(1, NX):
            to = at(k, 0)
            copies.append(remote(q.at[pl.ds(pl.multiple_of(to[0] * n, 16), n)], xbuf.at[k], xsem, s * NX + k, to))
        for c in copies:
            c.start()
        return copies

    def z_start(copies, q, xbuf, zbuf, ybuf, n, s):
        for c in copies:
            c.wait_recv()
        acc = q[pl.ds(pl.multiple_of(gx * n, 16), n), :].astype(F32)
        for k in range(1, NX):
            acc = acc + xbuf[k].astype(F32)
        units = n // 16
        zbuf[0:units] = acc.astype(BF).reshape(units, 16, 128)
        zbuf[units:8] = jnp.zeros((8 - units, 16, 128), BF)
        out = []
        for k in range(1, NY):
            to = at(0, k)
            out.append(remote(zbuf.at[to[1]], ybuf.at[k], zsem, s * NY + k, to))
        for c in out:
            c.start()
        return out

    def zg_start(copies, zbuf, ybuf, wbuf, s):
        for c in copies:
            c.wait_recv()
        acc = zbuf[gy].astype(F32)
        for k in range(1, NY):
            acc = acc + ybuf[k].astype(F32)
        wbuf[gy] = acc.astype(BF)
        out = [remote(wbuf.at[gy], wbuf.at[gy], zgsem, s * NY + k, at(0, k)) for k in range(1, NY)]
        for c in out:
            c.start()
        return out

    def xg_start(copies, wbuf, g, n, s):
        for c in copies:
            c.wait_recv()
        mine = pl.ds(pl.multiple_of(gx * n, 16), n)
        g[gz, mine, :] = wbuf[0:n // 16].reshape(n, 128)
        out = [remote(g.at[gz, mine], g.at[gz, mine], xgsem, s * NX + k, at(k, 0)) for k in range(1, NX)]
        for c in out:
            c.start()
        return out

    def cg_start(copies, g, s):
        for c in copies:
            c.wait_recv()
        out = remote(g.at[gz], g.at[gz], cgsem, s, other)
        out.start()
        return out

    def zb_start(copies, q, xbuf, ybuf, n, s):
        for c in copies:
            c.wait_recv()
        acc = q[pl.ds(pl.multiple_of(gx * n, 16), n), :].astype(F32)
        for k in range(1, NX):
            acc = acc + xbuf[k].astype(F32)
        ybuf[gy] = acc.astype(BF)
        out = [remote(ybuf.at[gy], ybuf.at[gy], zsem, s * NY + k, at(0, k)) for k in range(1, NY)]
        for c in out:
            c.start()
        return out

    def xb_start(copies, ybuf, g, n, s):
        for c in copies:
            c.wait_recv()
        acc = ybuf[0].astype(F32)
        for k in range(1, NY):
            acc = acc + ybuf[k].astype(F32)
        mine = pl.ds(pl.multiple_of(gx * n, 16), n)
        g[gz, mine, :] = acc.astype(BF)
        out = [remote(g.at[gz, mine], g.at[gz, mine], xgsem, s * NX + k, at(k, 0)) for k in range(1, NX)]
        for c in out:
            c.start()
        return out

    xs_a = x_start(core_a, pa, ca, qa, xa, KA, 0)
    xs_d = x_start(core_d, pd, cd, qd, xd, KD, 1)

    take_faces(hidx, hrcv, hid_faces)

    def conv(x, carry):
        rows = jnp.concatenate([view(hidx, x, d) for d in range(7)], axis=1)
        acc = dot(rows, wc[...])
        for p in range(16):
            for h in range(2):
                tall[h, pl.ds(x * 16 + p, BP, stride=64), :] = acc[p * BP:(p + 1) * BP, h * 128:(h + 1) * 128]
        return carry

    lax.fori_loop(0, 4, conv, 0)
    for m in range(16 * MB):
        for h in range(2):
            coarse_v[m, :, h * 128:(h + 1) * 128] = tall[h, 4 * m:4 * m + 4, :].astype(BF)
    stores = [pltpu.make_async_copy(coarse_v, coarse_h, esem.at[0])]
    stores[0].start()

    zs_a = z_start(xs_a, qa, xa, za, ya, KA, 0)
    zs_d = zb_start(xs_d, qd, xd, yd, KD, 1)
    zg_a = zg_start(zs_a, za, ya, wa, 0)
    xg_d = xb_start(zs_d, yd, gd, KD, 1)

    for c in range(8):
        flow = dot_nt(gr[c * NB:(c + 1) * NB, :], wd[...])
        for v in range(8):
            wide[pl.ds(c * 8 + v, NB, stride=64), :] = flow[:, v * 128:(v + 1) * 128]
    fineg_v[...] = wide[...].astype(BF)
    stores.append(pltpu.make_async_copy(fineg_v, fineg_h, esem.at[1]))
    stores[1].start()

    xg_a = xg_start(zg_a, wa, ga, KA, 0)
    cg_d = cg_start(xg_d, gd, 1)
    cg_a = cg_start(xg_a, ga, 0)
    cg_d.wait_recv()
    cg_a.wait_recv()
    for c in stores:
        c.wait()

    for c in (octs + cot_faces + rets + hid_faces + [core_a, core_d] + xs_a + xs_d + zs_a + zs_d
              + zg_a + xg_a + xg_d + [cg_a, cg_d]):
        c.wait_send()


def finish(coarse_h, fineg_h, ga, gd, coarse_o, fineg_o, down_o, conv_o, sem):
    copies = [pltpu.make_async_copy(coarse_h, coarse_o, sem.at[0]),
              pltpu.make_async_copy(fineg_h, fineg_o, sem.at[1])]
    for c in copies:
        c.start()
    scale = 1.0 / (64 * MB)
    for h in range(2):
        down_o[:, h * 128:(h + 1) * 128] = gd[h].astype(F32) * scale
        conv_o[:, h * 128:(h + 1) * 128] = ga[h].astype(F32) * scale
    for c in copies:
        c.wait()


def shards(fine_field, target, neighbour, down_weight, conv_weight, out_cotangent):
    vmem = pl.BlockSpec(memory_space=pltpu.VMEM)
    anyw = pl.BlockSpec(memory_space=pl.ANY)
    dma = pltpu.SemaphoreType.DMA
    coarse, fineg, ga, gd = pl.pallas_call(
        kernel,
        out_shape=(
            jax.ShapeDtypeStruct((16 * MB, 4, 256), BF),
            jax.ShapeDtypeStruct((64 * NB, 128), BF),
            jax.ShapeDtypeStruct((2, 1792, 128), BF),
            jax.ShapeDtypeStruct((2, 1024, 128), BF),
        ),
        in_specs=[anyw, vmem, vmem, anyw, anyw, anyw],
        out_specs=[anyw, anyw, vmem, vmem],
        scratch_shapes=[
            pltpu.VMEM((64 * NB, 128), BF),
            pltpu.VMEM((16 * MB, 4, 256), BF),
            pltpu.VMEM((1024, 256), BF),
            pltpu.VMEM((1792, 256), BF),
            pltpu.VMEM((1792, 256), BF),
            pltpu.VMEM((128, 128), I32),
            pltpu.VMEM((8, 128), I32),
            pltpu.VMEM((64 * NB, 128), F32),
            pltpu.VMEM((2, 64 * BP, 128), F32),
            pltpu.VMEM((8 * NB, 1024), BF),
            pltpu.VMEM((16 * MB, 4, 256), BF),
            pltpu.VMEM((64 * NB, 128), BF),
            pltpu.VMEM((6, 6, 6 * BP, 256), BF),
            pltpu.VMEM((6, 6, 6 * BP, 256), BF),
            pltpu.VMEM((4, 512, 256), BF),
            pltpu.VMEM((8 * NB, 256), BF),
            pltpu.VMEM((8 * NB, 256), F32),
            pltpu.VMEM((1024, 8 * NB), BF),
            pltpu.VMEM((256, 2048), BF),
            pltpu.VMEM((8 * NB, 256), BF),
            pltpu.VMEM((6, 32, 128), BF),
            pltpu.VMEM((6, 128, 256), BF),
            pltpu.VMEM((8, 80, 256), BF),
            pltpu.VMEM((8, 80, 256), BF),
            pltpu.VMEM((8, 64, 256), BF),
            pltpu.VMEM((8, 64, 256), BF),
            pltpu.VMEM((5, 128, 256), BF),
            pltpu.VMEM((5, 128, 256), BF),
            pltpu.VMEM((5, 128, 256), BF),
            pltpu.VMEM((5, 128, 256), BF),
            pltpu.VMEM((2, 1792, 128), BF),
            pltpu.VMEM((2, 1024, 128), BF),
            pltpu.VMEM((1792, 128), BF),
            pltpu.VMEM((1024, 128), BF),
            pltpu.VMEM((1792, 128), BF),
            pltpu.VMEM((1024, 128), BF),
            pltpu.VMEM((NX, KA, 128), BF),
            pltpu.VMEM((NX, KD, 128), BF),
            pltpu.VMEM((NY, 16, 128), BF),
            pltpu.VMEM((NY, 16, 128), BF),
            pltpu.VMEM((NY, KD, 128), BF),
            pltpu.VMEM((NY, 16, 128), BF),
            dma((4,)),
            dma((2,)),
            dma((2, 8)),
            dma((2, 8)),
            dma((2, 5)),
            dma((2, 5)),
            dma((2, 2)),
            dma((2, 2 * NX)),
            dma((2, 2 * NY)),
            dma((2, 2 * NY)),
            dma((2, 2 * NX)),
            dma((2, 2)),
        ],
        compiler_params=pltpu.CompilerParams(
            collective_id=0, has_side_effects=True, vmem_limit_bytes=56 * 1024 * 1024),
        cost_estimate=pl.CostEstimate(flops=6_000_000_000, bytes_accessed=10_000_000, transcendentals=600_000),
    )(fine_field.reshape(64 * NB, 128), target.reshape(1, NB), neighbour.T, down_weight,
      conv_weight.reshape(1792, 256), out_cotangent.reshape(16 * MB, 4, 256))

    coarse, fineg, down_g, conv_g = pl.pallas_call(
        finish,
        out_shape=(
            jax.ShapeDtypeStruct((16 * MB, 4, 256), BF),
            jax.ShapeDtypeStruct((64 * NB, 128), BF),
            jax.ShapeDtypeStruct((1024, 256), F32),
            jax.ShapeDtypeStruct((1792, 256), F32),
        ),
        in_specs=[anyw, anyw, vmem, vmem],
        out_specs=[anyw, anyw, vmem, vmem],
        scratch_shapes=[dma((2,))],
        compiler_params=pltpu.CompilerParams(vmem_limit_bytes=32 * 1024 * 1024),
    )(coarse, fineg, ga, gd)
    return (coarse.reshape(MB, 4, 4, 4, 256), fineg.reshape(NB, 8, 8, 128), down_g,
            conv_g.reshape(7, 256, 256))


def solution(mesh):
    every = ("gx", "gy", "gz")
    in_specs = (
        P(every, None, None, None),
        P(every),
        P(every, None),
        P(),
        P(),
        P(every, None, None, None, None),
    )
    out_specs = (
        P(every, None, None, None, None),
        P(every, None, None, None),
        P(),
        P(),
    )
    return jax.shard_map(shards, mesh=mesh, in_specs=in_specs, out_specs=out_specs, check_vma=False)
```

```python
import functools

import jax
import jax.numpy as jnp
from jax import lax
from jax.experimental import pallas as pl
from jax.experimental.pallas import tpu as pltpu
from jax.sharding import PartitionSpec as P

MESH = pl.DeviceIdType.MESH
BF = jnp.bfloat16
F32 = jnp.float32
I32 = jnp.int32

NX, NY, NZ = 16, 8, 2
MB = 18
BP = 32
NB = 80
CELLS = 8 * MB

OPP = (0, 2, 1, 4, 3, 6, 5)
OFFS = ((0, 0, 0), (-1, 0, 0), (1, 0, 0), (0, -1, 0), (0, 1, 0), (0, 0, -1), (0, 0, 1))
DIRS = ((-1, -1), (-1, 0), (-1, 1), (0, -1), (0, 1), (1, -1), (1, 0), (1, 1))
KA, KD = 112, 64


def iota(shape, dim):
    return lax.broadcasted_iota(I32, shape, dim)


def dot(a, b):
    return jnp.dot(a, b, preferred_element_type=F32)


def dot_nt(a, b):
    return lax.dot_general(a, b, (((1,), (1,)), ((), ())), preferred_element_type=F32)


def onehot(mask):
    return jnp.where(mask, 1.0, 0.0).astype(BF)


def ninth(u):
    return lax.shift_right_arithmetic(u * 7282, 16)


def view(ext, x, d):
    dx, dy, dz = OFFS[d]
    rows = ext[1 + x + dx, 1 + dy:5 + dy, BP * (1 + dz):BP * (5 + dz), :]
    return rows.reshape(16 * BP, 256)


def layer_quad(ext, k, q):
    if k == 0:
        return ext[4, 1 + q, BP:5 * BP, :]
    if k == 1:
        return ext[1, 1 + q, BP:5 * BP, :]
    if k == 2:
        return ext[1 + q, 4, BP:5 * BP, :]
    if k == 3:
        return ext[1 + q, 1, BP:5 * BP, :]
    z = 4 if k == 4 else 1
    return ext[1 + q, 1:5, BP * z:BP * (z + 1), :].reshape(4 * BP, 256)


def put_halo(ext, k, q, rows):
    if k == 0:
        ext[0, 1 + q, BP:5 * BP, :] = rows
    elif k == 1:
        ext[5, 1 + q, BP:5 * BP, :] = rows
    elif k == 2:
        ext[1 + q, 0, BP:5 * BP, :] = rows
    elif k == 3:
        ext[1 + q, 5, BP:5 * BP, :] = rows
    else:
        z = 0 if k == 4 else 5
        ext[1 + q, 1:5, BP * z:BP * (z + 1), :] = rows.reshape(4, BP, 256)


def kernel(fine_h, tgt_h, nb_h, wd_h, wc_h, cot_h,
           coarse_h, fineg_h, ga_h, gd_h,
           tgt, nb, ga, gd, fin, cin, wd, wc, wt, t_scr, n_scr, wide, tall, fine, coarse_v, fineg_v,
           cotx, hidx, gh, red, slope, fine_t, hid_t, gr, selc, selp,
           osnd, orcv, rsnd, rrcv, fsnd, frcv, hsnd, hrcv,
           pa, pd, ca, cd, qa, qd, xa, xd, za, ya, yd, wa,
           isem, esem, osem, rsem, fsem, hsem, coresem, xsem, zsem, zgsem, xgsem, cgsem):
    gx, gy, gz = lax.axis_index("gx"), lax.axis_index("gy"), lax.axis_index("gz")
    myself = (gx * NY + gy) * NZ + gz

    def at(dx, dy):
        return (lax.rem(gx + dx + NX, NX), lax.rem(gy + dy + NY, NY), gz)

    other = (gx, gy, 1 - gz)

    barrier = pltpu.get_barrier_semaphore()
    peers = [at(k, 0) for k in range(1, NX)] + [at(0, k) for k in range(1, NY)]
    peers += [at(a, b) for a in (-1, 1) for b in (-1, 1)] + [other]
    for peer in peers:
        pl.semaphore_signal(barrier, inc=1, device_id=peer, device_id_type=MESH)

    loads = [pltpu.make_async_copy(src, dst, isem.at[i]) for i, (src, dst) in enumerate(
        ((cot_h, cin), (fine_h, fin), (wd_h, wd), (wc_h, wc), (nb_h, nb), (tgt_h, tgt)))]
    for c in loads:
        c.start()

    def remote(src, dst, sems, i, device):
        return pltpu.make_async_remote_copy(
            src_ref=src, dst_ref=dst, send_sem=sems.at[0, i], recv_sem=sems.at[1, i],
            device_id=device, device_id_type=MESH)

    quad_c = lax.shift_right_arithmetic(iota((128, 128), 0), 5)
    lane = iota((128, 128), 1)

    loads[4].wait()
    n_scr[...] = jnp.full((8, 128), -1, I32)
    for q in range(4):
        n_scr[0:6, BP * q:BP * q + MB] = nb[...]
    nb_r = n_scr[...]
    nb_c = nb_r.T

    def names(v):
        owner = ninth(lax.shift_right_arithmetic(v, 1))
        return v - owner * MB, (v >= 0) & (owner == myself), (v >= 0) & (owner != myself)

    for k in range(6):
        vc = nb_c[:, k:k + 1]
        vr = nb_r[k:k + 1, :]
        idx_c, home_c, far_c = names(vc)
        idx_r, home_r, far_r = names(vr)
        less = far_r & (vr < vc) & (lane < 32)
        rank_c = jnp.sum(jnp.where(less, 1.0, 0.0), axis=1, keepdims=True).astype(I32)
        selp[k, :, 0:128] = onehot(home_c & (idx_c + 32 * quad_c == lane))
        selp[k, :, 128:256] = onehot(far_c & (rank_c + 8 * quad_c == lane))
        early = far_c[0:32] & (iota((32, 128), 0) < (iota((32, 128), 1) & 31))
        rank_r = jnp.sum(jnp.where(early, 1.0, 0.0), axis=0, keepdims=True).astype(I32)
        slot = rank_r + 8 * lax.shift_right_arithmetic(iota((32, 128), 1), 5)
        selc[k] = onehot(far_r & (slot == iota((32, 128), 0)))

    face_to = (at(1, 0), at(-1, 0), at(0, 1), at(0, -1), other)

    def send_faces(ext, snd, rcv, sems):
        for k in range(4):
            for q in range(4):
                snd[k, q * 32:(q + 1) * 32, :] = dot(selc[OPP[k + 1] - 1], layer_quad(ext, k, q)).astype(BF)
        for q in range(4):
            both = dot(selc[5], layer_quad(ext, 4, q)) + dot(selc[4], layer_quad(ext, 5, q))
            snd[4, q * 32:(q + 1) * 32, :] = both.astype(BF)
        copies = [remote(snd.at[k], rcv.at[k], sems, k, face_to[k]) for k in range(5)]
        for c in copies:
            c.start()
        return copies

    def take_faces(ext, rcv, copies):
        for c in copies:
            c.wait_recv()
        for k in range(6):
            for q in range(4):
                near = dot(selp[k, :, 0:128], layer_quad(ext, k, q))
                far = dot(selp[k, :, 128:160], rcv[min(k, 4), q * 32:(q + 1) * 32, :])
                put_halo(ext, k, q, (near + far).astype(BF))

    loads[0].wait()
    tall[...] = jnp.zeros_like(tall)
    for m in range(16 * MB):
        part = cin[m].astype(F32)
        for h in range(2):
            tall[h, 4 * m:4 * m + 4, :] = part[:, h * 128:(h + 1) * 128]
    for p in range(64):
        x, y, z = p >> 4, (p >> 2) & 3, p & 3
        for h in range(2):
            rows = tall[h, pl.ds(p, BP, stride=64), :]
            cotx[1 + x, 1 + y, BP * (1 + z):BP * (2 + z), h * 128:(h + 1) * 128] = rows.astype(BF)
    pl.semaphore_wait(barrier, len(peers))
    cot_faces = send_faces(cotx, fsnd, frcv, fsem)

    def place(t):
        owner = ninth(lax.shift_right_arithmetic(t, 4))
        cell = t - owner * CELLS
        moving = owner != myself
        sx = lax.shift_right_arithmetic(owner, 4) - gx
        sy = (lax.shift_right_arithmetic(owner, 1) & 7) - gy
        flat = (sx + 1) * 3 + (sy + 1)
        return cell, moving, jnp.where(flat > 4, flat - 1, flat)

    loads[5].wait()
    t_scr[:, 0:NB] = jnp.broadcast_to(tgt[...], (128, NB))
    cell_c, moving_c, dest_c = place(t_scr[...].T[0:NB, 0:1])
    cell_r, moving_r, dest_r = place(tgt[...])
    member_c = jnp.where(moving_c & (dest_c == iota((NB, 128), 1)), 1.0, 0.0)
    lower = onehot(iota((NB, NB), 1) < iota((NB, NB), 0))
    order_c = jnp.sum(dot(lower, member_c.astype(BF)) * member_c, axis=1, keepdims=True)
    member_r = jnp.where(moving_r & (dest_r == iota((16, NB), 0)), 1.0, 0.0)
    upper = onehot(iota((NB, NB), 0) < iota((NB, NB), 1))
    order_r = jnp.sum(dot(member_r.astype(BF), upper) * member_r, axis=0, keepdims=True)
    key_c = jnp.where(moving_c, dest_c * 16 + order_c.astype(I32), -1000)
    key_r = jnp.where(moving_r, dest_r * 16 + order_r.astype(I32), -1000)

    def table_name(shape, dim):
        r = iota(shape, dim)
        b = r & 31
        return jnp.where(b < MB, b * 8 + lax.shift_right_arithmetic(r, 5), -7)

    send_hot = [onehot(key_r + 8 * h == iota((128, NB), 0)) for h in range(2)]
    back_hot = [onehot(key_c + 8 * h == iota((NB, 128), 1)) for h in range(2)]
    stay_c = onehot((cell_c == table_name((NB, 256), 1)) & jnp.logical_not(moving_c))
    stay_r = onehot((cell_r == table_name((256, NB), 0)) & jnp.logical_not(moving_r))

    loads[1].wait()
    wide[...] = fin[...].astype(F32)
    for c in range(8):
        for v in range(8):
            part = wide[pl.ds(c * 8 + v, NB, stride=64), :]
            fine[c * NB:(c + 1) * NB, v * 128:(v + 1) * 128] = part.astype(BF)
    loads[2].wait()
    red[...] = dot(fine[...], wd[...]).astype(BF)
    for pair in range(4):
        out = sum(dot(send_hot[h], red[(2 * pair + h) * NB:(2 * pair + h + 1) * NB, :]) for h in range(2))
        out = out.astype(BF)
        for d in range(8):
            osnd[d, pair * 16:(pair + 1) * 16, :] = out[d * 16:(d + 1) * 16]
    tags = jnp.broadcast_to((cell_c + 1).astype(F32), (NB, 256)).astype(BF)
    out = (dot(send_hot[0], tags) + dot(send_hot[1], tags)).astype(BF)
    for d in range(8):
        osnd[d, 64:80, :] = out[d * 16:(d + 1) * 16]

    octs = [remote(osnd.at[d], orcv.at[d], osem, d, at(*DIRS[d])) for d in range(8)]
    for c in octs:
        c.start()

    fine_t[...] = fine[...].T
    pre = red[...].astype(F32)
    sig = 1.0 / (1.0 + jnp.exp(-pre))
    slope[...] = sig * (1.0 + pre * (1.0 - sig))
    loads[3].wait()
    for d in range(7):
        wt[d * 256:(d + 1) * 256, :] = wc[d * 256:(d + 1) * 256, :].T
    take_faces(cotx, frcv, cot_faces)

    for c in octs:
        c.wait_recv()
    tag = orcv[:, 64:80, :].reshape(128, 256).astype(F32)
    row_half = lax.shift_right_arithmetic(iota((128, 256), 0), 3) & 1
    match = tag - 1.0 == table_name((128, 256), 1).astype(F32)
    came = [jnp.where(match & (row_half == h), 1.0, 0.0) for h in range(2)]
    came_t = [m.T.astype(BF) for m in came]
    came = [m.astype(BF) for m in came]

    for c in range(8):
        i, j, k = c >> 2, (c >> 1) & 1, c & 1
        pair = c >> 1
        got = orcv[:, pair * 16:(pair + 1) * 16, :].reshape(128, 256)
        pre = dot(came_t[c & 1], got) + dot(stay_r, red[c * NB:(c + 1) * NB, :])
        hid = (pre / (1.0 + jnp.exp(-pre))).astype(BF)
        for o in range(8):
            x, y, z = 2 * (o >> 2) + i, 2 * ((o >> 1) & 1) + j, 2 * (o & 1) + k
            hidx[1 + x, 1 + y, BP * (1 + z):BP * (2 + z), :] = hid[o * BP:(o + 1) * BP]
    hid_faces = send_faces(hidx, hsnd, hrcv, hsem)

    for x in range(4):
        hid_t[:, x * 512:(x + 1) * 512] = view(hidx, x, 0).T
    for d in range(7):
        rows = jnp.concatenate([view(cotx, x, OPP[d]) for x in range(4)], axis=0)
        acc = dot(hid_t[...], rows).astype(BF)
        for h in range(2):
            pa[h, d * 256:(d + 1) * 256, :] = acc[:, h * 128:(h + 1) * 128]
    core_a = remote(pa.at[1 - gz], ca, coresem, 0, other)
    core_a.start()

    def x_start(core, p, cbuf, q, xbuf, n, s):
        core.wait_recv()
        q[...] = (p[gz].astype(F32) + cbuf[...].astype(F32)).astype(BF)
        copies = []
        for k in range(1, NX):
            to = at(k, 0)
            copies.append(remote(q.at[pl.ds(pl.multiple_of(to[0] * n, 16), n)], xbuf.at[k], xsem, s * NX + k, to))
        for c in copies:
            c.start()
        return copies

    def z_start(copies, q, xbuf, zbuf, ybuf, n, s):
        for c in copies:
            c.wait_recv()
        acc = q[pl.ds(pl.multiple_of(gx * n, 16), n), :].astype(F32)
        for k in range(1, NX):
            acc = acc + xbuf[k].astype(F32)
        units = n // 16
        zbuf[0:units] = acc.astype(BF).reshape(units, 16, 128)
        zbuf[units:8] = jnp.zeros((8 - units, 16, 128), BF)
        out = []
        for k in range(1, NY):
            to = at(0, k)
            out.append(remote(zbuf.at[to[1]], ybuf.at[k], zsem, s * NY + k, to))
        for c in out:
            c.start()
        return out

    def zg_start(copies, zbuf, ybuf, wbuf, s):
        for c in copies:
            c.wait_recv()
        acc = zbuf[gy].astype(F32)
        for k in range(1, NY):
            acc = acc + ybuf[k].astype(F32)
        wbuf[gy] = acc.astype(BF)
        out = [remote(wbuf.at[gy], wbuf.at[gy], zgsem, s * NY + k, at(0, k)) for k in range(1, NY)]
        for c in out:
            c.start()
        return out

    def xg_start(copies, wbuf, g, n, s):
        for c in copies:
            c.wait_recv()
        mine = pl.ds(pl.multiple_of(gx * n, 16), n)
        g[gz, mine, :] = wbuf[0:n // 16].reshape(n, 128)
        out = [remote(g.at[gz, mine], g.at[gz, mine], xgsem, s * NX + k, at(k, 0)) for k in range(1, NX)]
        for c in out:
            c.start()
        return out

    def cg_start(copies, g, s):
        for c in copies:
            c.wait_recv()
        out = remote(g.at[gz], g.at[gz], cgsem, s, other)
        out.start()
        return out

    def zb_start(copies, q, xbuf, ybuf, n, s):
        for c in copies:
            c.wait_recv()
        acc = q[pl.ds(pl.multiple_of(gx * n, 16), n), :].astype(F32)
        for k in range(1, NX):
            acc = acc + xbuf[k].astype(F32)
        ybuf[gy] = acc.astype(BF)
        out = [remote(ybuf.at[gy], ybuf.at[gy], zsem, s * NY + k, at(0, k)) for k in range(1, NY)]
        for c in out:
            c.start()
        return out

    def xb_start(copies, ybuf, g, n, s):
        for c in copies:
            c.wait_recv()
        acc = ybuf[0].astype(F32)
        for k in range(1, NY):
            acc = acc + ybuf[k].astype(F32)
        mine = pl.ds(pl.multiple_of(gx * n, 16), n)
        g[gz, mine, :] = acc.astype(BF)
        out = [remote(g.at[gz, mine], g.at[gz, mine], xgsem, s * NX + k, at(k, 0)) for k in range(1, NX)]
        for c in out:
            c.start()
        return out

    def back_conv(x, carry):
        rows = jnp.concatenate([view(cotx, x, OPP[d]) for d in range(7)], axis=1)
        gh[x] = dot(rows, wt[...]).astype(BF)
        return carry

    lax.fori_loop(0, 3, back_conv, 0)
    xs_a = x_start(core_a, pa, ca, qa, xa, KA, 0)
    lax.fori_loop(3, 4, back_conv, 0)

    def grads(c):
        i, j, k = c >> 2, (c >> 1) & 1, c & 1
        out = []
        for o in range(8):
            x, y, z = 2 * (o >> 2) + i, 2 * ((o >> 1) & 1) + j, 2 * (o & 1) + k
            out.append(gh[x, (y * 4 + z) * BP:(y * 4 + z + 1) * BP, :])
        return jnp.concatenate(out, axis=0)

    for pair in range(4):
        out = (dot(came[0], grads(2 * pair)) + dot(came[1], grads(2 * pair + 1))).astype(BF)
        for d in range(8):
            rsnd[d, pair * 16:(pair + 1) * 16, :] = out[d * 16:(d + 1) * 16]
    rets = [remote(rsnd.at[d], rrcv.at[d], rsem, d, at(-DIRS[d][0], -DIRS[d][1])) for d in range(8)]
    for c in rets:
        c.start()

    take_faces(hidx, hrcv, hid_faces)

    def conv(x, carry):
        rows = jnp.concatenate([view(hidx, x, d) for d in range(7)], axis=1)
        acc = dot(rows, wc[...])
        for p in range(16):
            for h in range(2):
                tall[h, pl.ds(x * 16 + p, BP, stride=64), :] = acc[p * BP:(p + 1) * BP, h * 128:(h + 1) * 128]
        return carry

    lax.fori_loop(0, 2, conv, 0)

    for c in rets:
        c.wait_recv()
    for c in range(8):
        back = rrcv[:, (c >> 1) * 16:(c >> 1) * 16 + 16, :].reshape(128, 256)
        grad = dot(stay_c, grads(c)) + dot(back_hot[c & 1], back)
        gr[c * NB:(c + 1) * NB, :] = (grad * slope[c * NB:(c + 1) * NB, :]).astype(BF)
    for m in range(4):
        acc = dot(fine_t[m * 256:(m + 1) * 256, :], gr[...]).astype(BF)
        for h in range(2):
            pd[h, m * 256:(m + 1) * 256, :] = acc[:, h * 128:(h + 1) * 128]
    core_d = remote(pd.at[1 - gz], cd, coresem, 1, other)
    core_d.start()

    lax.fori_loop(2, 4, conv, 0)
    xs_d = x_start(core_d, pd, cd, qd, xd, KD, 1)
    zs_a = z_start(xs_a, qa, xa, za, ya, KA, 0)
    for m in range(16 * MB):
        for h in range(2):
            coarse_v[m, :, h * 128:(h + 1) * 128] = tall[h, 4 * m:4 * m + 4, :].astype(BF)
    stores = [pltpu.make_async_copy(coarse_v, coarse_h, esem.at[0])]
    stores[0].start()
    zg_a = zg_start(zs_a, za, ya, wa, 0)

    for c in range(8):
        flow = dot_nt(gr[c * NB:(c + 1) * NB, :], wd[...])
        for v in range(8):
            wide[pl.ds(c * 8 + v, NB, stride=64), :] = flow[:, v * 128:(v + 1) * 128]
    fineg_v[...] = wide[...].astype(BF)
    stores.append(pltpu.make_async_copy(fineg_v, fineg_h, esem.at[1]))
    stores[1].start()

    zs_d = zb_start(xs_d, qd, xd, yd, KD, 1)
    xg_a = xg_start(zg_a, wa, ga, KA, 0)
    xg_d = xb_start(zs_d, yd, gd, KD, 1)
    cg_a = cg_start(xg_a, ga, 0)
    stores.append(pltpu.make_async_copy(ga.at[gz], ga_h.at[gz], esem.at[2]))
    stores[2].start()
    cg_d = cg_start(xg_d, gd, 1)
    stores.append(pltpu.make_async_copy(gd.at[gz], gd_h.at[gz], esem.at[3]))
    stores[3].start()
    cg_a.wait_recv()
    stores.append(pltpu.make_async_copy(ga.at[1 - gz], ga_h.at[1 - gz], esem.at[4]))
    stores[4].start()
    cg_d.wait_recv()
    stores.append(pltpu.make_async_copy(gd.at[1 - gz], gd_h.at[1 - gz], esem.at[5]))
    stores[5].start()
    for c in stores:
        c.wait()

    for c in (octs + cot_faces + rets + hid_faces + [core_a, core_d] + xs_a + xs_d + zs_a + zs_d
              + zg_a + xg_a + xg_d + [cg_a, cg_d]):
        c.wait_send()


def finish(coarse_h, fineg_h, ga_h, gd_h, coarse_o, fineg_o, down_h, conv_h,
           coarse, fineg, ga, gd, down, conv, sem):
    reads = [pltpu.make_async_copy(src, dst, sem.at[i]) for i, (src, dst) in enumerate(
        ((gd_h, gd), (ga_h, ga), (fineg_h, fineg), (coarse_h, coarse)))]
    for c in reads:
        c.start()
    writes = [pltpu.make_async_copy(src, dst, sem.at[4 + i]) for i, (src, dst) in enumerate(
        ((down, down_h), (fineg, fineg_o), (coarse, coarse_o)))]
    scale = 1.0 / (64 * MB)
    reads[0].wait()
    for h in range(2):
        down[:, h * 128:(h + 1) * 128] = gd[h].astype(F32) * scale
    writes[0].start()
    reads[1].wait()
    for m in range(7):
        rows = slice(m * 256, (m + 1) * 256)
        for h in range(2):
            conv[rows, h * 128:(h + 1) * 128] = ga[h, rows].astype(F32) * scale
        writes.append(pltpu.make_async_copy(conv.at[rows], conv_h.at[rows], sem.at[7 + m]))
        writes[3 + m].start()
    reads[2].wait()
    writes[1].start()
    reads[3].wait()
    writes[2].start()
    for c in writes:
        c.wait()


def shards(fine_field, target, neighbour, down_weight, conv_weight, out_cotangent):
    anyw = pl.BlockSpec(memory_space=pl.ANY)
    dma = pltpu.SemaphoreType.DMA
    coarse, fineg, ga, gd = pl.pallas_call(
        kernel,
        out_shape=(
            jax.ShapeDtypeStruct((16 * MB, 4, 256), BF),
            jax.ShapeDtypeStruct((64 * NB, 128), BF),
            jax.ShapeDtypeStruct((2, 1792, 128), BF),
            jax.ShapeDtypeStruct((2, 1024, 128), BF),
        ),
        in_specs=[anyw] * 6,
        out_specs=[anyw] * 4,
        scratch_shapes=[
            pltpu.VMEM((1, NB), I32),
            pltpu.VMEM((6, MB), I32),
            pltpu.VMEM((2, 1792, 128), BF),
            pltpu.VMEM((2, 1024, 128), BF),
            pltpu.VMEM((64 * NB, 128), BF),
            pltpu.VMEM((16 * MB, 4, 256), BF),
            pltpu.VMEM((1024, 256), BF),
            pltpu.VMEM((1792, 256), BF),
            pltpu.VMEM((1792, 256), BF),
            pltpu.VMEM((128, 128), I32),
            pltpu.VMEM((8, 128), I32),
            pltpu.VMEM((64 * NB, 128), F32),
            pltpu.VMEM((2, 64 * BP, 128), F32),
            pltpu.VMEM((8 * NB, 1024), BF),
            pltpu.VMEM((16 * MB, 4, 256), BF),
            pltpu.VMEM((64 * NB, 128), BF),
            pltpu.VMEM((6, 6, 6 * BP, 256), BF),
            pltpu.VMEM((6, 6, 6 * BP, 256), BF),
            pltpu.VMEM((4, 512, 256), BF),
            pltpu.VMEM((8 * NB, 256), BF),
            pltpu.VMEM((8 * NB, 256), F32),
            pltpu.VMEM((1024, 8 * NB), BF),
            pltpu.VMEM((256, 2048), BF),
            pltpu.VMEM((8 * NB, 256), BF),
            pltpu.VMEM((6, 32, 128), BF),
            pltpu.VMEM((6, 128, 256), BF),
            pltpu.VMEM((8, 80, 256), BF),
            pltpu.VMEM((8, 80, 256), BF),
            pltpu.VMEM((8, 64, 256), BF),
            pltpu.VMEM((8, 64, 256), BF),
            pltpu.VMEM((5, 128, 256), BF),
            pltpu.VMEM((5, 128, 256), BF),
            pltpu.VMEM((5, 128, 256), BF),
            pltpu.VMEM((5, 128, 256), BF),
            pltpu.VMEM((2, 1792, 128), BF),
            pltpu.VMEM((2, 1024, 128), BF),
            pltpu.VMEM((1792, 128), BF),
            pltpu.VMEM((1024, 128), BF),
            pltpu.VMEM((1792, 128), BF),
            pltpu.VMEM((1024, 128), BF),
            pltpu.VMEM((NX, KA, 128), BF),
            pltpu.VMEM((NX, KD, 128), BF),
            pltpu.VMEM((NY, 16, 128), BF),
            pltpu.VMEM((NY, 16, 128), BF),
            pltpu.VMEM((NY, KD, 128), BF),
            pltpu.VMEM((NY, 16, 128), BF),
            dma((6,)),
            dma((6,)),
            dma((2, 8)),
            dma((2, 8)),
            dma((2, 5)),
            dma((2, 5)),
            dma((2, 2)),
            dma((2, 2 * NX)),
            dma((2, 2 * NY)),
            dma((2, 2 * NY)),
            dma((2, 2 * NX)),
            dma((2, 2)),
        ],
        compiler_params=pltpu.CompilerParams(
            collective_id=0, has_side_effects=True, vmem_limit_bytes=56 * 1024 * 1024),
        cost_estimate=pl.CostEstimate(flops=6_000_000_000, bytes_accessed=10_000_000, transcendentals=600_000),
    )(fine_field.reshape(64 * NB, 128), target.reshape(1, NB), neighbour.T, down_weight,
      conv_weight.reshape(1792, 256), out_cotangent.reshape(16 * MB, 4, 256))

    coarse, fineg, down_g, conv_g = pl.pallas_call(
        finish,
        out_shape=(
            jax.ShapeDtypeStruct((16 * MB, 4, 256), BF),
            jax.ShapeDtypeStruct((64 * NB, 128), BF),
            jax.ShapeDtypeStruct((1024, 256), F32),
            jax.ShapeDtypeStruct((1792, 256), F32),
        ),
        in_specs=[anyw] * 4,
        out_specs=[anyw] * 4,
        scratch_shapes=[
            pltpu.VMEM((16 * MB, 4, 256), BF),
            pltpu.VMEM((64 * NB, 128), BF),
            pltpu.VMEM((2, 1792, 128), BF),
            pltpu.VMEM((2, 1024, 128), BF),
            pltpu.VMEM((1024, 256), F32),
            pltpu.VMEM((1792, 256), F32),
            dma((14,)),
        ],
        compiler_params=pltpu.CompilerParams(vmem_limit_bytes=60 * 1024 * 1024),
    )(coarse, fineg, ga, gd)
    return (coarse.reshape(MB, 4, 4, 4, 256), fineg.reshape(NB, 8, 8, 128), down_g,
            conv_g.reshape(7, 256, 256))


def solution(mesh):
    every = ("gx", "gy", "gz")
    in_specs = (
        P(every, None, None, None),
        P(every),
        P(every, None),
        P(),
        P(),
        P(every, None, None, None, None),
    )
    out_specs = (
        P(every, None, None, None, None),
        P(every, None, None, None),
        P(),
        P(),
    )
    return jax.shard_map(shards, mesh=mesh, in_specs=in_specs, out_specs=out_specs, check_vma=False)
```

```python
import functools

import jax
import jax.numpy as jnp
from jax import lax
from jax.experimental import pallas as pl
from jax.experimental.pallas import tpu as pltpu
from jax.sharding import PartitionSpec as P

MESH = pl.DeviceIdType.MESH
BF = jnp.bfloat16
F32 = jnp.float32
I32 = jnp.int32

NX, NY, NZ = 16, 8, 2
MB = 18
BP = 32
NB = 80
CELLS = 8 * MB

OPP = (0, 2, 1, 4, 3, 6, 5)
OFFS = ((0, 0, 0), (-1, 0, 0), (1, 0, 0), (0, -1, 0), (0, 1, 0), (0, 0, -1), (0, 0, 1))
DIRS = ((-1, -1), (-1, 0), (-1, 1), (0, -1), (0, 1), (1, -1), (1, 0), (1, 1))
KA, KD = 112, 64


def iota(shape, dim):
    return lax.broadcasted_iota(I32, shape, dim)


def dot(a, b):
    return jnp.dot(a, b, preferred_element_type=F32)


def dot_nt(a, b):
    return lax.dot_general(a, b, (((1,), (1,)), ((), ())), preferred_element_type=F32)


def onehot(mask):
    return jnp.where(mask, 1.0, 0.0).astype(BF)


def ninth(u):
    return lax.shift_right_arithmetic(u * 7282, 16)


def view(ext, x, d):
    dx, dy, dz = OFFS[d]
    rows = ext[1 + x + dx, 1 + dy:5 + dy, BP * (1 + dz):BP * (5 + dz), :]
    return rows.reshape(16 * BP, 256)


def layer_quad(ext, k, q):
    if k == 0:
        return ext[4, 1 + q, BP:5 * BP, :]
    if k == 1:
        return ext[1, 1 + q, BP:5 * BP, :]
    if k == 2:
        return ext[1 + q, 4, BP:5 * BP, :]
    if k == 3:
        return ext[1 + q, 1, BP:5 * BP, :]
    z = 4 if k == 4 else 1
    return ext[1 + q, 1:5, BP * z:BP * (z + 1), :].reshape(4 * BP, 256)


def put_halo(ext, k, q, rows):
    if k == 0:
        ext[0, 1 + q, BP:5 * BP, :] = rows
    elif k == 1:
        ext[5, 1 + q, BP:5 * BP, :] = rows
    elif k == 2:
        ext[1 + q, 0, BP:5 * BP, :] = rows
    elif k == 3:
        ext[1 + q, 5, BP:5 * BP, :] = rows
    else:
        z = 0 if k == 4 else 5
        ext[1 + q, 1:5, BP * z:BP * (z + 1), :] = rows.reshape(4, BP, 256)


def kernel(fine_h, tgt_h, nb_h, wd_h, wc_h, cot_h,
           coarse_h, fineg_h, ga_h, gd_h,
           tgt, nb, ga, gd, fin, cin, wd, wc, wt, t_scr, n_scr, wide, tall, fine, coarse_v, fineg_v,
           cotx, hidx, gh, red, slope, fine_t, hid_t, gr, selc, selp,
           osnd, orcv, rsnd, rrcv, fsnd, frcv, hsnd, hrcv,
           pa, pd, ca, cd, qa, qd, xa, xd, za, ya, yd, wa,
           isem, esem, osem, rsem, fsem, hsem, coresem, xsem, zsem, zgsem, xgsem, cgsem):
    gx, gy, gz = lax.axis_index("gx"), lax.axis_index("gy"), lax.axis_index("gz")
    myself = (gx * NY + gy) * NZ + gz

    def at(dx, dy):
        return (lax.rem(gx + dx + NX, NX), lax.rem(gy + dy + NY, NY), gz)

    other = (gx, gy, 1 - gz)

    barrier = pltpu.get_barrier_semaphore()
    peers = [at(k, 0) for k in range(1, NX)] + [at(0, k) for k in range(1, NY)]
    peers += [at(a, b) for a in (-1, 1) for b in (-1, 1)] + [other]
    for peer in peers:
        pl.semaphore_signal(barrier, inc=1, device_id=peer, device_id_type=MESH)

    loads = [pltpu.make_async_copy(src, dst, isem.at[i]) for i, (src, dst) in enumerate(
        ((cot_h, cin), (fine_h, fin), (wd_h, wd), (wc_h, wc), (nb_h, nb), (tgt_h, tgt)))]
    for c in loads:
        c.start()

    def remote(src, dst, sems, i, device):
        return pltpu.make_async_remote_copy(
            src_ref=src, dst_ref=dst, send_sem=sems.at[0, i], recv_sem=sems.at[1, i],
            device_id=device, device_id_type=MESH)

    quad_c = lax.shift_right_arithmetic(iota((128, 128), 0), 5)
    lane = iota((128, 128), 1)

    loads[4].wait()
    n_scr[...] = jnp.full((8, 128), -1, I32)
    for q in range(4):
        n_scr[0:6, BP * q:BP * q + MB] = nb[...]
    nb_r = n_scr[...]
    nb_c = nb_r.T

    def names(v):
        owner = ninth(lax.shift_right_arithmetic(v, 1))
        return v - owner * MB, (v >= 0) & (owner == myself), (v >= 0) & (owner != myself)

    for k in range(6):
        vc = nb_c[:, k:k + 1]
        vr = nb_r[k:k + 1, :]
        idx_c, home_c, far_c = names(vc)
        idx_r, home_r, far_r = names(vr)
        less = far_r & (vr < vc) & (lane < 32)
        rank_c = jnp.sum(jnp.where(less, 1.0, 0.0), axis=1, keepdims=True).astype(I32)
        selp[k, :, 0:128] = onehot(home_c & (idx_c + 32 * quad_c == lane))
        selp[k, :, 128:256] = onehot(far_c & (rank_c + 8 * quad_c == lane))
        early = far_c[0:32] & (iota((32, 128), 0) < (iota((32, 128), 1) & 31))
        rank_r = jnp.sum(jnp.where(early, 1.0, 0.0), axis=0, keepdims=True).astype(I32)
        slot = rank_r + 8 * lax.shift_right_arithmetic(iota((32, 128), 1), 5)
        selc[k] = onehot(far_r & (slot == iota((32, 128), 0)))

    face_to = (at(1, 0), at(-1, 0), at(0, 1), at(0, -1), other)

    def send_faces(ext, snd, rcv, sems):
        for k in range(4):
            for q in range(4):
                snd[k, q * 32:(q + 1) * 32, :] = dot(selc[OPP[k + 1] - 1], layer_quad(ext, k, q)).astype(BF)
        for q in range(4):
            both = dot(selc[5], layer_quad(ext, 4, q)) + dot(selc[4], layer_quad(ext, 5, q))
            snd[4, q * 32:(q + 1) * 32, :] = both.astype(BF)
        copies = [remote(snd.at[k], rcv.at[k], sems, k, face_to[k]) for k in range(5)]
        for c in copies:
            c.start()
        return copies

    def take_faces(ext, rcv, copies):
        for c in copies:
            c.wait_recv()
        for k in range(6):
            for q in range(4):
                near = dot(selp[k, :, 0:128], layer_quad(ext, k, q))
                far = dot(selp[k, :, 128:160], rcv[min(k, 4), q * 32:(q + 1) * 32, :])
                put_halo(ext, k, q, (near + far).astype(BF))

    loads[0].wait()
    tall[...] = jnp.zeros_like(tall)
    for m in range(16 * MB):
        part = cin[m].astype(F32)
        for h in range(2):
            tall[h, 4 * m:4 * m + 4, :] = part[:, h * 128:(h + 1) * 128]
    for p in range(64):
        x, y, z = p >> 4, (p >> 2) & 3, p & 3
        for h in range(2):
            rows = tall[h, pl.ds(p, BP, stride=64), :]
            cotx[1 + x, 1 + y, BP * (1 + z):BP * (2 + z), h * 128:(h + 1) * 128] = rows.astype(BF)
    pl.semaphore_wait(barrier, len(peers))
    cot_faces = send_faces(cotx, fsnd, frcv, fsem)

    def place(t):
        owner = ninth(lax.shift_right_arithmetic(t, 4))
        cell = t - owner * CELLS
        moving = owner != myself
        sx = lax.shift_right_arithmetic(owner, 4) - gx
        sy = (lax.shift_right_arithmetic(owner, 1) & 7) - gy
        flat = (sx + 1) * 3 + (sy + 1)
        return cell, moving, jnp.where(flat > 4, flat - 1, flat)

    loads[5].wait()
    t_scr[:, 0:NB] = jnp.broadcast_to(tgt[...], (128, NB))
    cell_c, moving_c, dest_c = place(t_scr[...].T[0:NB, 0:1])
    cell_r, moving_r, dest_r = place(tgt[...])
    member_c = jnp.where(moving_c & (dest_c == iota((NB, 128), 1)), 1.0, 0.0)
    lower = onehot(iota((NB, NB), 1) < iota((NB, NB), 0))
    order_c = jnp.sum(dot(lower, member_c.astype(BF)) * member_c, axis=1, keepdims=True)
    member_r = jnp.where(moving_r & (dest_r == iota((16, NB), 0)), 1.0, 0.0)
    upper = onehot(iota((NB, NB), 0) < iota((NB, NB), 1))
    order_r = jnp.sum(dot(member_r.astype(BF), upper) * member_r, axis=0, keepdims=True)
    key_c = jnp.where(moving_c, dest_c * 16 + order_c.astype(I32), -1000)
    key_r = jnp.where(moving_r, dest_r * 16 + order_r.astype(I32), -1000)

    def table_name(shape, dim):
        r = iota(shape, dim)
        b = r & 31
        return jnp.where(b < MB, b * 8 + lax.shift_right_arithmetic(r, 5), -7)

    send_hot = [onehot(key_r + 8 * h == iota((128, NB), 0)) for h in range(2)]
    back_hot = [onehot(key_c + 8 * h == iota((NB, 128), 1)) for h in range(2)]
    stay_c = onehot((cell_c == table_name((NB, 256), 1)) & jnp.logical_not(moving_c))
    stay_r = onehot((cell_r == table_name((256, NB), 0)) & jnp.logical_not(moving_r))

    loads[1].wait()
    wide[...] = fin[...].astype(F32)
    for c in range(8):
        for v in range(8):
            part = wide[pl.ds(c * 8 + v, NB, stride=64), :]
            fine[c * NB:(c + 1) * NB, v * 128:(v + 1) * 128] = part.astype(BF)
    loads[2].wait()
    red[...] = dot(fine[...], wd[...]).astype(BF)
    for pair in range(4):
        out = sum(dot(send_hot[h], red[(2 * pair + h) * NB:(2 * pair + h + 1) * NB, :]) for h in range(2))
        out = out.astype(BF)
        for d in range(8):
            osnd[d, pair * 16:(pair + 1) * 16, :] = out[d * 16:(d + 1) * 16]
    tags = jnp.broadcast_to((cell_c + 1).astype(F32), (NB, 256)).astype(BF)
    out = (dot(send_hot[0], tags) + dot(send_hot[1], tags)).astype(BF)
    for d in range(8):
        osnd[d, 64:80, :] = out[d * 16:(d + 1) * 16]

    octs = [remote(osnd.at[d], orcv.at[d], osem, d, at(*DIRS[d])) for d in range(8)]
    for c in octs:
        c.start()

    fine_t[...] = fine[...].T
    pre = red[...].astype(F32)
    sig = 1.0 / (1.0 + jnp.exp(-pre))
    slope[...] = sig * (1.0 + pre * (1.0 - sig))
    loads[3].wait()
    for d in range(7):
        wt[d * 256:(d + 1) * 256, :] = wc[d * 256:(d + 1) * 256, :].T
    take_faces(cotx, frcv, cot_faces)

    def back_conv(x, carry):
        rows = jnp.concatenate([view(cotx, x, OPP[d]) for d in range(7)], axis=1)
        gh[x] = dot(rows, wt[...]).astype(BF)
        return carry

    lax.fori_loop(0, 4, back_conv, 0)

    for c in octs:
        c.wait_recv()
    tag = orcv[:, 64:80, :].reshape(128, 256).astype(F32)
    row_half = lax.shift_right_arithmetic(iota((128, 256), 0), 3) & 1
    match = tag - 1.0 == table_name((128, 256), 1).astype(F32)
    came = [jnp.where(match & (row_half == h), 1.0, 0.0) for h in range(2)]
    came_t = [m.T.astype(BF) for m in came]
    came = [m.astype(BF) for m in came]

    def grads(c):
        i, j, k = c >> 2, (c >> 1) & 1, c & 1
        out = []
        for o in range(8):
            x, y, z = 2 * (o >> 2) + i, 2 * ((o >> 1) & 1) + j, 2 * (o & 1) + k
            out.append(gh[x, (y * 4 + z) * BP:(y * 4 + z + 1) * BP, :])
        return jnp.concatenate(out, axis=0)

    for pair in range(4):
        out = (dot(came[0], grads(2 * pair)) + dot(came[1], grads(2 * pair + 1))).astype(BF)
        for d in range(8):
            rsnd[d, pair * 16:(pair + 1) * 16, :] = out[d * 16:(d + 1) * 16]
    rets = [remote(rsnd.at[d], rrcv.at[d], rsem, d, at(-DIRS[d][0], -DIRS[d][1])) for d in range(8)]
    for c in rets:
        c.start()

    for c in range(8):
        i, j, k = c >> 2, (c >> 1) & 1, c & 1
        pair = c >> 1
        got = orcv[:, pair * 16:(pair + 1) * 16, :].reshape(128, 256)
        pre = dot(came_t[c & 1], got) + dot(stay_r, red[c * NB:(c + 1) * NB, :])
        hid = (pre / (1.0 + jnp.exp(-pre))).astype(BF)
        for o in range(8):
            x, y, z = 2 * (o >> 2) + i, 2 * ((o >> 1) & 1) + j, 2 * (o & 1) + k
            hidx[1 + x, 1 + y, BP * (1 + z):BP * (2 + z), :] = hid[o * BP:(o + 1) * BP]
    hid_faces = send_faces(hidx, hsnd, hrcv, hsem)

    def core_send(p, cbuf, m, s):
        rows = pl.ds(m * 256, 256)
        c = remote(p.at[1 - gz, rows], cbuf.at[rows], coresem, 7 * s + m, other)
        c.start()
        return c

    def x_copy(src, dst, sems, s, p):
        return pltpu.make_async_remote_copy(
            src_ref=src, dst_ref=dst, send_sem=sems.at[0, s * NX + p], recv_sem=sems.at[1, s * NX + gx],
            device_id=(p, gy, gz), device_id_type=MESH)

    def x_from(dst, sems, s, p):
        return pltpu.make_async_remote_copy(
            src_ref=dst, dst_ref=dst, send_sem=sems.at[0, s * NX + p], recv_sem=sems.at[1, s * NX + p],
            device_id=(p, gy, gz), device_id_type=MESH)

    def away(p, fn):
        @pl.when(gx != p)
        def _():
            fn()

    def core_take(core, p, cbuf, q, xbuf, n, m, s):
        core.wait_recv()
        rows = slice(m * 256, (m + 1) * 256)
        q[rows] = (p[gz, rows].astype(F32) + cbuf[rows].astype(F32)).astype(BF)
        for j in range(NX):
            if m * 256 < (j + 1) * n <= (m + 1) * 256:
                away(j, lambda j=j: x_copy(q.at[pl.ds(j * n, n)], xbuf.at[gx], xsem, s, j).start())

    def x_sum(q, xbuf, n, s):
        xbuf[gx] = q[pl.ds(pl.multiple_of(gx * n, 16), n), :]
        for j in range(NX):
            away(j, lambda j=j: x_from(xbuf.at[j], xsem, s, j).wait_recv())
        acc = xbuf[0].astype(F32)
        for j in range(1, NX):
            acc = acc + xbuf[j].astype(F32)
        return acc.astype(BF)

    def z_start(acc, zbuf, ybuf, n, s):
        units = n // 16
        zbuf[0:units] = acc.reshape(units, 16, 128)
        zbuf[units:8] = jnp.zeros((8 - units, 16, 128), BF)
        out = []
        for k in range(1, NY):
            to = at(0, k)
            out.append(remote(zbuf.at[to[1]], ybuf.at[k], zsem, s * NY + k, to))
        for c in out:
            c.start()
        return out

    def zg_start(copies, zbuf, ybuf, wbuf, s):
        for c in copies:
            c.wait_recv()
        acc = zbuf[gy].astype(F32)
        for k in range(1, NY):
            acc = acc + ybuf[k].astype(F32)
        wbuf[gy] = acc.astype(BF)
        out = [remote(wbuf.at[gy], wbuf.at[gy], zgsem, s * NY + k, at(0, k)) for k in range(1, NY)]
        for c in out:
            c.start()
        return out

    def zb_start(acc, ybuf, s):
        ybuf[gy] = acc
        out = [remote(ybuf.at[gy], ybuf.at[gy], zsem, s * NY + k, at(0, k)) for k in range(1, NY)]
        for c in out:
            c.start()
        return out

    def xg_start(rows, g, n, s):
        mine = pl.ds(pl.multiple_of(gx * n, 16), n)
        g[gz, mine, :] = rows
        for j in range(NX):
            away(j, lambda j=j: x_copy(g.at[gz, mine], g.at[gz, mine], xgsem, s, j).start())

    def gathered_w(copies, wbuf, n):
        for c in copies:
            c.wait_recv()
        return wbuf[0:n // 16].reshape(n, 128)

    def gathered_y(copies, ybuf):
        for c in copies:
            c.wait_recv()
        acc = ybuf[0].astype(F32)
        for k in range(1, NY):
            acc = acc + ybuf[k].astype(F32)
        return acc.astype(BF)

    def cg_start(g, n, s):
        out = []
        for quarter in range(4):
            for j in range(4 * quarter, 4 * quarter + 4):
                away(j, lambda j=j: x_from(g.at[gz, pl.ds(j * n, n)], xgsem, s, j).wait_recv())
            rows = pl.ds(4 * quarter * n, 4 * n)
            out.append(remote(g.at[gz, rows], g.at[gz, rows], cgsem, 4 * s + quarter, other))
            out[quarter].start()
        return out

    for x in range(4):
        hid_t[:, x * 512:(x + 1) * 512] = view(hidx, x, 0).T
    cores_a = []
    for d in range(7):
        rows = jnp.concatenate([view(cotx, x, OPP[d]) for x in range(4)], axis=0)
        acc = dot(hid_t[...], rows).astype(BF)
        for h in range(2):
            pa[h, d * 256:(d + 1) * 256, :] = acc[:, h * 128:(h + 1) * 128]
        cores_a.append(core_send(pa, ca, d, 0))
        if d >= 5:
            core_take(cores_a[d - 5], pa, ca, qa, xa, KA, d - 5, 0)
    for d in range(2, 7):
        core_take(cores_a[d], pa, ca, qa, xa, KA, d, 0)

    for c in rets:
        c.wait_recv()
    for c in range(8):
        back = rrcv[:, (c >> 1) * 16:(c >> 1) * 16 + 16, :].reshape(128, 256)
        grad = dot(stay_c, grads(c)) + dot(back_hot[c & 1], back)
        gr[c * NB:(c + 1) * NB, :] = (grad * slope[c * NB:(c + 1) * NB, :]).astype(BF)
    cores_d = []
    for m in range(4):
        acc = dot(fine_t[m * 256:(m + 1) * 256, :], gr[...]).astype(BF)
        for h in range(2):
            pd[h, m * 256:(m + 1) * 256, :] = acc[:, h * 128:(h + 1) * 128]
        cores_d.append(core_send(pd, cd, m, 1))

    take_faces(hidx, hrcv, hid_faces)
    for m in range(4):
        core_take(cores_d[m], pd, cd, qd, xd, KD, m, 1)

    def conv(x, carry):
        rows = jnp.concatenate([view(hidx, x, d) for d in range(7)], axis=1)
        acc = dot(rows, wc[...])
        for p in range(16):
            for h in range(2):
                tall[h, pl.ds(x * 16 + p, BP, stride=64), :] = acc[p * BP:(p + 1) * BP, h * 128:(h + 1) * 128]
        return carry

    lax.fori_loop(0, 4, conv, 0)
    zs_a = z_start(x_sum(qa, xa, KA, 0), za, ya, KA, 0)
    zs_d = zb_start(x_sum(qd, xd, KD, 1), yd, 1)

    for c in range(8):
        flow = dot_nt(gr[c * NB:(c + 1) * NB, :], wd[...])
        for v in range(8):
            wide[pl.ds(c * 8 + v, NB, stride=64), :] = flow[:, v * 128:(v + 1) * 128]
    fineg_v[...] = wide[...].astype(BF)
    stores = [pltpu.make_async_copy(fineg_v, fineg_h, esem.at[1])]
    stores[0].start()
    zg_a = zg_start(zs_a, za, ya, wa, 0)

    for m in range(16 * MB):
        for h in range(2):
            coarse_v[m, :, h * 128:(h + 1) * 128] = tall[h, 4 * m:4 * m + 4, :].astype(BF)
    stores.append(pltpu.make_async_copy(coarse_v, coarse_h, esem.at[0]))
    stores[1].start()

    xg_start(gathered_y(zs_d, yd), gd, KD, 1)
    xg_start(gathered_w(zg_a, wa, KA), ga, KA, 0)
    cg_d = cg_start(gd, KD, 1)
    stores.append(pltpu.make_async_copy(gd.at[gz], gd_h.at[gz], esem.at[3]))
    stores[2].start()
    cg_a = cg_start(ga, KA, 0)
    stores.append(pltpu.make_async_copy(ga.at[gz], ga_h.at[gz], esem.at[2]))
    stores[3].start()
    for c in cg_d:
        c.wait_recv()
    stores.append(pltpu.make_async_copy(gd.at[1 - gz], gd_h.at[1 - gz], esem.at[5]))
    stores[4].start()
    for c in cg_a:
        c.wait_recv()
    stores.append(pltpu.make_async_copy(ga.at[1 - gz], ga_h.at[1 - gz], esem.at[4]))
    stores[5].start()
    for c in stores:
        c.wait()
    for j in range(NX):
        def sent(j=j):
            x_from(xa.at[j], xsem, 0, j).wait_send()
            x_from(xd.at[j], xsem, 1, j).wait_send()
            x_from(ga.at[gz, pl.ds(j * KA, KA)], xgsem, 0, j).wait_send()
            x_from(gd.at[gz, pl.ds(j * KD, KD)], xgsem, 1, j).wait_send()

        away(j, sent)
    for c in (octs + cot_faces + rets + hid_faces + cores_a + cores_d + zs_a + zs_d + zg_a + cg_a + cg_d):
        c.wait_send()


def finish(coarse_h, fineg_h, ga_h, gd_h, coarse_o, fineg_o, down_h, conv_h,
           coarse, fineg, ga, gd, down, conv, sem):
    reads = [pltpu.make_async_copy(src, dst, sem.at[i]) for i, (src, dst) in enumerate(
        ((gd_h, gd), (ga_h, ga), (fineg_h, fineg), (coarse_h, coarse)))]
    for c in reads:
        c.start()
    writes = [pltpu.make_async_copy(src, dst, sem.at[4 + i]) for i, (src, dst) in enumerate(
        ((down, down_h), (fineg, fineg_o), (coarse, coarse_o)))]
    scale = 1.0 / (64 * MB)
    reads[0].wait()
    for h in range(2):
        down[:, h * 128:(h + 1) * 128] = gd[h].astype(F32) * scale
    writes[0].start()
    reads[1].wait()
    for m in range(7):
        rows = slice(m * 256, (m + 1) * 256)
        for h in range(2):
            conv[rows, h * 128:(h + 1) * 128] = ga[h, rows].astype(F32) * scale
        writes.append(pltpu.make_async_copy(conv.at[rows], conv_h.at[rows], sem.at[7 + m]))
        writes[3 + m].start()
    reads[2].wait()
    writes[1].start()
    reads[3].wait()
    writes[2].start()
    for c in writes:
        c.wait()


def shards(fine_field, target, neighbour, down_weight, conv_weight, out_cotangent):
    anyw = pl.BlockSpec(memory_space=pl.ANY)
    dma = pltpu.SemaphoreType.DMA
    coarse, fineg, ga, gd = pl.pallas_call(
        kernel,
        out_shape=(
            jax.ShapeDtypeStruct((16 * MB, 4, 256), BF),
            jax.ShapeDtypeStruct((64 * NB, 128), BF),
            jax.ShapeDtypeStruct((2, 1792, 128), BF),
            jax.ShapeDtypeStruct((2, 1024, 128), BF),
        ),
        in_specs=[anyw] * 6,
        out_specs=[anyw] * 4,
        scratch_shapes=[
            pltpu.VMEM((1, NB), I32),
            pltpu.VMEM((6, MB), I32),
            pltpu.VMEM((2, 1792, 128), BF),
            pltpu.VMEM((2, 1024, 128), BF),
            pltpu.VMEM((64 * NB, 128), BF),
            pltpu.VMEM((16 * MB, 4, 256), BF),
            pltpu.VMEM((1024, 256), BF),
            pltpu.VMEM((1792, 256), BF),
            pltpu.VMEM((1792, 256), BF),
            pltpu.VMEM((128, 128), I32),
            pltpu.VMEM((8, 128), I32),
            pltpu.VMEM((64 * NB, 128), F32),
            pltpu.VMEM((2, 64 * BP, 128), F32),
            pltpu.VMEM((8 * NB, 1024), BF),
            pltpu.VMEM((16 * MB, 4, 256), BF),
            pltpu.VMEM((64 * NB, 128), BF),
            pltpu.VMEM((6, 6, 6 * BP, 256), BF),
            pltpu.VMEM((6, 6, 6 * BP, 256), BF),
            pltpu.VMEM((4, 512, 256), BF),
            pltpu.VMEM((8 * NB, 256), BF),
            pltpu.VMEM((8 * NB, 256), F32),
            pltpu.VMEM((1024, 8 * NB), BF),
            pltpu.VMEM((256, 2048), BF),
            pltpu.VMEM((8 * NB, 256), BF),
            pltpu.VMEM((6, 32, 128), BF),
            pltpu.VMEM((6, 128, 256), BF),
            pltpu.VMEM((8, 80, 256), BF),
            pltpu.VMEM((8, 80, 256), BF),
            pltpu.VMEM((8, 64, 256), BF),
            pltpu.VMEM((8, 64, 256), BF),
            pltpu.VMEM((5, 128, 256), BF),
            pltpu.VMEM((5, 128, 256), BF),
            pltpu.VMEM((5, 128, 256), BF),
            pltpu.VMEM((5, 128, 256), BF),
            pltpu.VMEM((2, 1792, 128), BF),
            pltpu.VMEM((2, 1024, 128), BF),
            pltpu.VMEM((1792, 128), BF),
            pltpu.VMEM((1024, 128), BF),
            pltpu.VMEM((1792, 128), BF),
            pltpu.VMEM((1024, 128), BF),
            pltpu.VMEM((NX, KA, 128), BF),
            pltpu.VMEM((NX, KD, 128), BF),
            pltpu.VMEM((NY, 16, 128), BF),
            pltpu.VMEM((NY, 16, 128), BF),
            pltpu.VMEM((NY, KD, 128), BF),
            pltpu.VMEM((NY, 16, 128), BF),
            dma((6,)),
            dma((6,)),
            dma((2, 8)),
            dma((2, 8)),
            dma((2, 5)),
            dma((2, 5)),
            dma((2, 11)),
            dma((2, 2 * NX)),
            dma((2, 2 * NY)),
            dma((2, 2 * NY)),
            dma((2, 2 * NX)),
            dma((2, 8)),
        ],
        compiler_params=pltpu.CompilerParams(
            collective_id=0, has_side_effects=True, vmem_limit_bytes=56 * 1024 * 1024),
        cost_estimate=pl.CostEstimate(flops=6_000_000_000, bytes_accessed=10_000_000, transcendentals=600_000),
    )(fine_field.reshape(64 * NB, 128), target.reshape(1, NB), neighbour.T, down_weight,
      conv_weight.reshape(1792, 256), out_cotangent.reshape(16 * MB, 4, 256))

    coarse, fineg, down_g, conv_g = pl.pallas_call(
        finish,
        out_shape=(
            jax.ShapeDtypeStruct((16 * MB, 4, 256), BF),
            jax.ShapeDtypeStruct((64 * NB, 128), BF),
            jax.ShapeDtypeStruct((1024, 256), F32),
            jax.ShapeDtypeStruct((1792, 256), F32),
        ),
        in_specs=[anyw] * 4,
        out_specs=[anyw] * 4,
        scratch_shapes=[
            pltpu.VMEM((16 * MB, 4, 256), BF),
            pltpu.VMEM((64 * NB, 128), BF),
            pltpu.VMEM((2, 1792, 128), BF),
            pltpu.VMEM((2, 1024, 128), BF),
            pltpu.VMEM((1024, 256), F32),
            pltpu.VMEM((1792, 256), F32),
            dma((14,)),
        ],
        compiler_params=pltpu.CompilerParams(vmem_limit_bytes=60 * 1024 * 1024),
    )(coarse, fineg, ga, gd)
    return (coarse.reshape(MB, 4, 4, 4, 256), fineg.reshape(NB, 8, 8, 128), down_g,
            conv_g.reshape(7, 256, 256))


def solution(mesh):
    every = ("gx", "gy", "gz")
    in_specs = (
        P(every, None, None, None),
        P(every),
        P(every, None),
        P(),
        P(),
        P(every, None, None, None, None),
    )
    out_specs = (
        P(every, None, None, None, None),
        P(every, None, None, None),
        P(),
        P(),
    )
    return jax.shard_map(shards, mesh=mesh, in_specs=in_specs, out_specs=out_specs, check_vma=False)
```

```python
import functools

import jax
import jax.numpy as jnp
from jax import lax
from jax.experimental import pallas as pl
from jax.experimental.pallas import tpu as pltpu
from jax.sharding import PartitionSpec as P

MESH = pl.DeviceIdType.MESH
BF = jnp.bfloat16
F32 = jnp.float32
I32 = jnp.int32

NX, NY, NZ = 16, 8, 2
MB = 18
BP = 32
NB = 80
CELLS = 8 * MB

OPP = (0, 2, 1, 4, 3, 6, 5)
OFFS = ((0, 0, 0), (-1, 0, 0), (1, 0, 0), (0, -1, 0), (0, 1, 0), (0, 0, -1), (0, 0, 1))
DIRS = ((-1, -1), (-1, 0), (-1, 1), (0, -1), (0, 1), (1, -1), (1, 0), (1, 1))
KA, KD = 112, 64


def iota(shape, dim):
    return lax.broadcasted_iota(I32, shape, dim)


def dot(a, b):
    return jnp.dot(a, b, preferred_element_type=F32)


def dot_nt(a, b):
    return lax.dot_general(a, b, (((1,), (1,)), ((), ())), preferred_element_type=F32)


def onehot(mask):
    return jnp.where(mask, 1.0, 0.0).astype(BF)


def ninth(u):
    return lax.shift_right_arithmetic(u * 7282, 16)


def view(ext, x, d):
    dx, dy, dz = OFFS[d]
    rows = ext[1 + x + dx, 1 + dy:5 + dy, BP * (1 + dz):BP * (5 + dz), :]
    return rows.reshape(16 * BP, 256)


def layer_quad(ext, k, q):
    if k == 0:
        return ext[4, 1 + q, BP:5 * BP, :]
    if k == 1:
        return ext[1, 1 + q, BP:5 * BP, :]
    if k == 2:
        return ext[1 + q, 4, BP:5 * BP, :]
    if k == 3:
        return ext[1 + q, 1, BP:5 * BP, :]
    z = 4 if k == 4 else 1
    return ext[1 + q, 1:5, BP * z:BP * (z + 1), :].reshape(4 * BP, 256)


def put_halo(ext, k, q, rows):
    if k == 0:
        ext[0, 1 + q, BP:5 * BP, :] = rows
    elif k == 1:
        ext[5, 1 + q, BP:5 * BP, :] = rows
    elif k == 2:
        ext[1 + q, 0, BP:5 * BP, :] = rows
    elif k == 3:
        ext[1 + q, 5, BP:5 * BP, :] = rows
    else:
        z = 0 if k == 4 else 5
        ext[1 + q, 1:5, BP * z:BP * (z + 1), :] = rows.reshape(4, BP, 256)


def kernel(fine_h, tgt_h, nb_h, wd_h, wc_h, cot_h,
           coarse_h, fineg_h, ga_h, gd_h,
           tgt, nb, ga, gd, fin, cin, wd, wc, wt, t_scr, n_scr, wide, tall, fine, coarse_v, fineg_v,
           cotx, hidx, gh, red, slope, fine_t, hid_t, gr, selc, selp,
           osnd, orcv, rsnd, rrcv, fsnd, frcv, hsnd, hrcv,
           pa, pd, ca, cd, qa, qd, xa, xd, ya, yd,
           isem, esem, osem, rsem, fsem, hsem, coresem, xsem, zsem, xgsem, cgsem):
    gx, gy, gz = lax.axis_index("gx"), lax.axis_index("gy"), lax.axis_index("gz")
    myself = (gx * NY + gy) * NZ + gz

    def at(dx, dy):
        return (lax.rem(gx + dx + NX, NX), lax.rem(gy + dy + NY, NY), gz)

    other = (gx, gy, 1 - gz)

    barrier = pltpu.get_barrier_semaphore()
    peers = [at(k, 0) for k in range(1, NX)] + [at(0, k) for k in range(1, NY)]
    peers += [at(a, b) for a in (-1, 1) for b in (-1, 1)] + [other]
    for peer in peers:
        pl.semaphore_signal(barrier, inc=1, device_id=peer, device_id_type=MESH)

    loads = [pltpu.make_async_copy(src, dst, isem.at[i]) for i, (src, dst) in enumerate(
        ((cot_h, cin), (fine_h, fin), (wd_h, wd), (wc_h, wc), (nb_h, nb), (tgt_h, tgt)))]
    for c in loads:
        c.start()

    def remote(src, dst, sems, i, device):
        return pltpu.make_async_remote_copy(
            src_ref=src, dst_ref=dst, send_sem=sems.at[0, i], recv_sem=sems.at[1, i],
            device_id=device, device_id_type=MESH)

    quad_c = lax.shift_right_arithmetic(iota((128, 128), 0), 5)
    lane = iota((128, 128), 1)

    loads[4].wait()
    n_scr[...] = jnp.full((8, 128), -1, I32)
    for q in range(4):
        n_scr[0:6, BP * q:BP * q + MB] = nb[...]
    nb_r = n_scr[...]
    nb_c = nb_r.T

    def names(v):
        owner = ninth(lax.shift_right_arithmetic(v, 1))
        return v - owner * MB, (v >= 0) & (owner == myself), (v >= 0) & (owner != myself)

    for k in range(6):
        vc = nb_c[:, k:k + 1]
        vr = nb_r[k:k + 1, :]
        idx_c, home_c, far_c = names(vc)
        idx_r, home_r, far_r = names(vr)
        less = far_r & (vr < vc) & (lane < 32)
        rank_c = jnp.sum(jnp.where(less, 1.0, 0.0), axis=1, keepdims=True).astype(I32)
        selp[k, :, 0:128] = onehot(home_c & (idx_c + 32 * quad_c == lane))
        selp[k, :, 128:256] = onehot(far_c & (rank_c + 8 * quad_c == lane))
        early = far_c[0:32] & (iota((32, 128), 0) < (iota((32, 128), 1) & 31))
        rank_r = jnp.sum(jnp.where(early, 1.0, 0.0), axis=0, keepdims=True).astype(I32)
        slot = rank_r + 8 * lax.shift_right_arithmetic(iota((32, 128), 1), 5)
        selc[k] = onehot(far_r & (slot == iota((32, 128), 0)))

    face_to = (at(1, 0), at(-1, 0), at(0, 1), at(0, -1), other)

    def send_faces(ext, snd, rcv, sems):
        copies = [remote(snd.at[k], rcv.at[k], sems, k, face_to[k]) for k in range(5)]
        for k in range(4):
            for q in range(4):
                snd[k, q * 32:(q + 1) * 32, :] = dot(selc[OPP[k + 1] - 1], layer_quad(ext, k, q)).astype(BF)
            copies[k].start()
        for q in range(4):
            both = dot(selc[5], layer_quad(ext, 4, q)) + dot(selc[4], layer_quad(ext, 5, q))
            snd[4, q * 32:(q + 1) * 32, :] = both.astype(BF)
        copies[4].start()
        return copies

    def take_faces(ext, rcv, copies):
        for c in copies:
            c.wait_recv()
        for k in range(6):
            for q in range(4):
                near = dot(selp[k, :, 0:128], layer_quad(ext, k, q))
                far = dot(selp[k, :, 128:160], rcv[min(k, 4), q * 32:(q + 1) * 32, :])
                put_halo(ext, k, q, (near + far).astype(BF))

    loads[0].wait()
    tall[...] = jnp.zeros_like(tall)
    for m in range(16 * MB):
        part = cin[m].astype(F32)
        for h in range(2):
            tall[h, 4 * m:4 * m + 4, :] = part[:, h * 128:(h + 1) * 128]
    for p in range(64):
        x, y, z = p >> 4, (p >> 2) & 3, p & 3
        for h in range(2):
            rows = tall[h, pl.ds(p, BP, stride=64), :]
            cotx[1 + x, 1 + y, BP * (1 + z):BP * (2 + z), h * 128:(h + 1) * 128] = rows.astype(BF)
    pl.semaphore_wait(barrier, len(peers))
    cot_faces = send_faces(cotx, fsnd, frcv, fsem)

    def place(t):
        owner = ninth(lax.shift_right_arithmetic(t, 4))
        cell = t - owner * CELLS
        moving = owner != myself
        sx = lax.shift_right_arithmetic(owner, 4) - gx
        sy = (lax.shift_right_arithmetic(owner, 1) & 7) - gy
        flat = (sx + 1) * 3 + (sy + 1)
        return cell, moving, jnp.where(flat > 4, flat - 1, flat)

    loads[5].wait()
    t_scr[:, 0:NB] = jnp.broadcast_to(tgt[...], (128, NB))
    cell_c, moving_c, dest_c = place(t_scr[...].T[0:NB, 0:1])
    cell_r, moving_r, dest_r = place(tgt[...])
    member_c = jnp.where(moving_c & (dest_c == iota((NB, 128), 1)), 1.0, 0.0)
    lower = onehot(iota((NB, NB), 1) < iota((NB, NB), 0))
    order_c = jnp.sum(dot(lower, member_c.astype(BF)) * member_c, axis=1, keepdims=True)
    member_r = jnp.where(moving_r & (dest_r == iota((16, NB), 0)), 1.0, 0.0)
    upper = onehot(iota((NB, NB), 0) < iota((NB, NB), 1))
    order_r = jnp.sum(dot(member_r.astype(BF), upper) * member_r, axis=0, keepdims=True)
    key_c = jnp.where(moving_c, dest_c * 16 + order_c.astype(I32), -1000)
    key_r = jnp.where(moving_r, dest_r * 16 + order_r.astype(I32), -1000)

    def table_name(shape, dim):
        r = iota(shape, dim)
        b = r & 31
        return jnp.where(b < MB, b * 8 + lax.shift_right_arithmetic(r, 5), -7)

    send_hot = [onehot(key_r + 8 * h == iota((128, NB), 0)) for h in range(2)]
    back_hot = [onehot(key_c + 8 * h == iota((NB, 128), 1)) for h in range(2)]
    stay_c = onehot((cell_c == table_name((NB, 256), 1)) & jnp.logical_not(moving_c))
    stay_r = onehot((cell_r == table_name((256, NB), 0)) & jnp.logical_not(moving_r))

    loads[1].wait()
    wide[...] = fin[...].astype(F32)
    for c in range(8):
        for v in range(8):
            part = wide[pl.ds(c * 8 + v, NB, stride=64), :]
            fine[c * NB:(c + 1) * NB, v * 128:(v + 1) * 128] = part.astype(BF)
    loads[2].wait()
    red[...] = dot(fine[...], wd[...]).astype(BF)
    for pair in range(4):
        out = sum(dot(send_hot[h], red[(2 * pair + h) * NB:(2 * pair + h + 1) * NB, :]) for h in range(2))
        out = out.astype(BF)
        for d in range(8):
            osnd[d, pair * 16:(pair + 1) * 16, :] = out[d * 16:(d + 1) * 16]
    tags = jnp.broadcast_to((cell_c + 1).astype(F32), (NB, 256)).astype(BF)
    out = (dot(send_hot[0], tags) + dot(send_hot[1], tags)).astype(BF)
    for d in range(8):
        osnd[d, 64:80, :] = out[d * 16:(d + 1) * 16]

    octs = [remote(osnd.at[d], orcv.at[d], osem, d, at(*DIRS[d])) for d in range(8)]
    for c in octs:
        c.start()

    fine_t[...] = fine[...].T
    pre = red[...].astype(F32)
    sig = 1.0 / (1.0 + jnp.exp(-pre))
    slope[...] = sig * (1.0 + pre * (1.0 - sig))
    loads[3].wait()
    for d in range(7):
        wt[d * 256:(d + 1) * 256, :] = wc[d * 256:(d + 1) * 256, :].T
    take_faces(cotx, frcv, cot_faces)

    for x in range(4):
        rows = jnp.concatenate([view(cotx, x, OPP[d]) for d in range(7)], axis=1)
        gh[x] = dot(rows, wt[...]).astype(BF)

    for c in octs:
        c.wait_recv()
    tag = orcv[:, 64:80, :].reshape(128, 256).astype(F32)
    row_half = lax.shift_right_arithmetic(iota((128, 256), 0), 3) & 1
    match = tag - 1.0 == table_name((128, 256), 1).astype(F32)
    came = [jnp.where(match & (row_half == h), 1.0, 0.0) for h in range(2)]
    came_t = [m.T.astype(BF) for m in came]
    came = [m.astype(BF) for m in came]

    def grads(c):
        i, j, k = c >> 2, (c >> 1) & 1, c & 1
        out = []
        for o in range(8):
            x, y, z = 2 * (o >> 2) + i, 2 * ((o >> 1) & 1) + j, 2 * (o & 1) + k
            out.append(gh[x, (y * 4 + z) * BP:(y * 4 + z + 1) * BP, :])
        return jnp.concatenate(out, axis=0)

    for pair in range(4):
        out = (dot(came[0], grads(2 * pair)) + dot(came[1], grads(2 * pair + 1))).astype(BF)
        for d in range(8):
            rsnd[d, pair * 16:(pair + 1) * 16, :] = out[d * 16:(d + 1) * 16]
    rets = [remote(rsnd.at[d], rrcv.at[d], rsem, d, at(-DIRS[d][0], -DIRS[d][1])) for d in range(8)]
    for c in rets:
        c.start()

    for c in range(8):
        i, j, k = c >> 2, (c >> 1) & 1, c & 1
        pair = c >> 1
        got = orcv[:, pair * 16:(pair + 1) * 16, :].reshape(128, 256)
        pre = dot(came_t[c & 1], got) + dot(stay_r, red[c * NB:(c + 1) * NB, :])
        hid = (pre / (1.0 + jnp.exp(-pre))).astype(BF)
        for o in range(8):
            x, y, z = 2 * (o >> 2) + i, 2 * ((o >> 1) & 1) + j, 2 * (o & 1) + k
            hidx[1 + x, 1 + y, BP * (1 + z):BP * (2 + z), :] = hid[o * BP:(o + 1) * BP]
    hid_faces = send_faces(hidx, hsnd, hrcv, hsem)

    def core_send(p, cbuf, m, s):
        rows = pl.ds(m * 256, 256)
        c = remote(p.at[1 - gz, rows], cbuf.at[rows], coresem, 7 * s + m, other)
        c.start()
        return c

    def x_copy(src, dst, sems, s, p):
        return pltpu.make_async_remote_copy(
            src_ref=src, dst_ref=dst, send_sem=sems.at[0, s * NX + p], recv_sem=sems.at[1, s * NX + gx],
            device_id=(p, gy, gz), device_id_type=MESH)

    def x_from(dst, sems, s, p):
        return pltpu.make_async_remote_copy(
            src_ref=dst, dst_ref=dst, send_sem=sems.at[0, s * NX + p], recv_sem=sems.at[1, s * NX + p],
            device_id=(p, gy, gz), device_id_type=MESH)

    def away(p, fn):
        @pl.when(gx != p)
        def _():
            fn()

    def core_take(core, p, cbuf, q, xbuf, n, m, s):
        core.wait_recv()
        rows = slice(m * 256, (m + 1) * 256)
        q[rows] = (p[gz, rows].astype(F32) + cbuf[rows].astype(F32)).astype(BF)
        for j in range(NX):
            if m * 256 < (j + 1) * n <= (m + 1) * 256:
                away(j, lambda j=j: x_copy(q.at[pl.ds(j * n, n)], xbuf.at[gx], xsem, s, j).start())

    def x_sum(q, xbuf, n, s):
        xbuf[gx] = q[pl.ds(pl.multiple_of(gx * n, 16), n), :]
        for j in range(NX):
            away(j, lambda j=j: x_from(xbuf.at[j], xsem, s, j).wait_recv())
        acc = xbuf[0].astype(F32)
        for j in range(1, NX):
            acc = acc + xbuf[j].astype(F32)
        return acc.astype(BF)

    def zb_start(acc, ybuf, s):
        ybuf[gy] = acc
        out = [remote(ybuf.at[gy], ybuf.at[gy], zsem, s * NY + k, at(0, k)) for k in range(1, NY)]
        for c in out:
            c.start()
        return out

    def xg_start(rows, g, n, s):
        mine = pl.ds(pl.multiple_of(gx * n, 16), n)
        g[gz, mine, :] = rows
        for j in range(NX):
            away(j, lambda j=j: x_copy(g.at[gz, mine], g.at[gz, mine], xgsem, s, j).start())

    def gathered_y(copies, ybuf):
        for c in copies:
            c.wait_recv()
        acc = ybuf[0].astype(F32)
        for k in range(1, NY):
            acc = acc + ybuf[k].astype(F32)
        return acc.astype(BF)

    def cg_start(g, n, s):
        out = []
        for quarter in range(4):
            for j in range(4 * quarter, 4 * quarter + 4):
                away(j, lambda j=j: x_from(g.at[gz, pl.ds(j * n, n)], xgsem, s, j).wait_recv())
            rows = pl.ds(4 * quarter * n, 4 * n)
            out.append(remote(g.at[gz, rows], g.at[gz, rows], cgsem, 4 * s + quarter, other))
            out[quarter].start()
        return out

    for x in range(4):
        hid_t[:, x * 512:(x + 1) * 512] = view(hidx, x, 0).T
    cores_a = []
    for d in range(7):
        rows = jnp.concatenate([view(cotx, x, OPP[d]) for x in range(4)], axis=0)
        acc = dot(hid_t[...], rows).astype(BF)
        for h in range(2):
            pa[h, d * 256:(d + 1) * 256, :] = acc[:, h * 128:(h + 1) * 128]
        cores_a.append(core_send(pa, ca, d, 0))
        if d >= 5:
            core_take(cores_a[d - 5], pa, ca, qa, xa, KA, d - 5, 0)
    for d in range(2, 7):
        core_take(cores_a[d], pa, ca, qa, xa, KA, d, 0)

    for c in rets:
        c.wait_recv()
    for c in range(8):
        back = rrcv[:, (c >> 1) * 16:(c >> 1) * 16 + 16, :].reshape(128, 256)
        grad = dot(stay_c, grads(c)) + dot(back_hot[c & 1], back)
        gr[c * NB:(c + 1) * NB, :] = (grad * slope[c * NB:(c + 1) * NB, :]).astype(BF)
    cores_d = []
    for m in range(4):
        acc = dot(fine_t[m * 256:(m + 1) * 256, :], gr[...]).astype(BF)
        for h in range(2):
            pd[h, m * 256:(m + 1) * 256, :] = acc[:, h * 128:(h + 1) * 128]
        cores_d.append(core_send(pd, cd, m, 1))

    take_faces(hidx, hrcv, hid_faces)
    for m in range(4):
        core_take(cores_d[m], pd, cd, qd, xd, KD, m, 1)

    def conv(x):
        rows = jnp.concatenate([view(hidx, x, d) for d in range(7)], axis=1)
        acc = dot(rows, wc[...])
        for p in range(16):
            for h in range(2):
                tall[h, pl.ds(x * 16 + p, BP, stride=64), :] = acc[p * BP:(p + 1) * BP, h * 128:(h + 1) * 128]

    for x in range(3):
        conv(x)
    zs_a = zb_start(x_sum(qa, xa, KA, 0), ya, 0)
    conv(3)
    zs_d = zb_start(x_sum(qd, xd, KD, 1), yd, 1)

    for c in range(8):
        flow = dot_nt(gr[c * NB:(c + 1) * NB, :], wd[...])
        for v in range(8):
            wide[pl.ds(c * 8 + v, NB, stride=64), :] = flow[:, v * 128:(v + 1) * 128]
    fineg_v[...] = wide[...].astype(BF)
    stores = [pltpu.make_async_copy(fineg_v, fineg_h, esem.at[1])]
    stores[0].start()

    for m in range(16 * MB):
        for h in range(2):
            coarse_v[m, :, h * 128:(h + 1) * 128] = tall[h, 4 * m:4 * m + 4, :].astype(BF)
    stores.append(pltpu.make_async_copy(coarse_v, coarse_h, esem.at[0]))
    stores[1].start()

    xg_start(gathered_y(zs_a, ya), ga, KA, 0)
    xg_start(gathered_y(zs_d, yd), gd, KD, 1)
    cg_a = cg_start(ga, KA, 0)
    stores.append(pltpu.make_async_copy(ga.at[gz], ga_h.at[gz], esem.at[2]))
    stores[2].start()
    cg_d = cg_start(gd, KD, 1)
    stores.append(pltpu.make_async_copy(gd.at[gz], gd_h.at[gz], esem.at[3]))
    stores[3].start()
    for c in cg_a:
        c.wait_recv()
    stores.append(pltpu.make_async_copy(ga.at[1 - gz], ga_h.at[1 - gz], esem.at[4]))
    stores[4].start()
    for c in cg_d:
        c.wait_recv()
    stores.append(pltpu.make_async_copy(gd.at[1 - gz], gd_h.at[1 - gz], esem.at[5]))
    stores[5].start()
    for c in stores:
        c.wait()
    for j in range(NX):
        def sent(j=j):
            x_from(xa.at[j], xsem, 0, j).wait_send()
            x_from(xd.at[j], xsem, 1, j).wait_send()
            x_from(ga.at[gz, pl.ds(j * KA, KA)], xgsem, 0, j).wait_send()
            x_from(gd.at[gz, pl.ds(j * KD, KD)], xgsem, 1, j).wait_send()

        away(j, sent)
    for c in (octs + cot_faces + rets + hid_faces + cores_a + cores_d + zs_a + zs_d + cg_a + cg_d):
        c.wait_send()


def finish(coarse_h, fineg_h, ga_h, gd_h, coarse_o, fineg_o, down_h, conv_h,
           coarse, fineg, ga, gd, down, conv, sem):
    reads = [pltpu.make_async_copy(gd_h, gd, sem.at[0])]
    for m in range(7):
        rows = pl.ds(m * 256, 256)
        reads.append(pltpu.make_async_copy(ga_h.at[:, rows], ga.at[:, rows], sem.at[1 + m]))
    reads += [pltpu.make_async_copy(coarse_h, coarse, sem.at[8]), pltpu.make_async_copy(fineg_h, fineg, sem.at[9])]
    for c in reads:
        c.start()
    scale = 1.0 / (64 * MB)
    reads[0].wait()
    for h in range(2):
        down[:, h * 128:(h + 1) * 128] = gd[h].astype(F32) * scale
    writes = [pltpu.make_async_copy(down, down_h, sem.at[10])]
    writes[0].start()
    for m in range(7):
        reads[1 + m].wait()
        rows = slice(m * 256, (m + 1) * 256)
        for h in range(2):
            conv[rows, h * 128:(h + 1) * 128] = ga[h, rows].astype(F32) * scale
        writes.append(pltpu.make_async_copy(conv.at[rows], conv_h.at[rows], sem.at[11 + m]))
        writes[1 + m].start()
    reads[8].wait()
    writes.append(pltpu.make_async_copy(coarse, coarse_o, sem.at[18]))
    writes[8].start()
    reads[9].wait()
    writes.append(pltpu.make_async_copy(fineg, fineg_o, sem.at[19]))
    writes[9].start()
    for c in writes:
        c.wait()


def shards(fine_field, target, neighbour, down_weight, conv_weight, out_cotangent):
    anyw = pl.BlockSpec(memory_space=pl.ANY)
    dma = pltpu.SemaphoreType.DMA
    coarse, fineg, ga, gd = pl.pallas_call(
        kernel,
        out_shape=(
            jax.ShapeDtypeStruct((16 * MB, 4, 256), BF),
            jax.ShapeDtypeStruct((64 * NB, 128), BF),
            jax.ShapeDtypeStruct((2, 1792, 128), BF),
            jax.ShapeDtypeStruct((2, 1024, 128), BF),
        ),
        in_specs=[anyw] * 6,
        out_specs=[anyw] * 4,
        scratch_shapes=[
            pltpu.VMEM((1, NB), I32),
            pltpu.VMEM((6, MB), I32),
            pltpu.VMEM((2, 1792, 128), BF),
            pltpu.VMEM((2, 1024, 128), BF),
            pltpu.VMEM((64 * NB, 128), BF),
            pltpu.VMEM((16 * MB, 4, 256), BF),
            pltpu.VMEM((1024, 256), BF),
            pltpu.VMEM((1792, 256), BF),
            pltpu.VMEM((1792, 256), BF),
            pltpu.VMEM((128, 128), I32),
            pltpu.VMEM((8, 128), I32),
            pltpu.VMEM((64 * NB, 128), F32),
            pltpu.VMEM((2, 64 * BP, 128), F32),
            pltpu.VMEM((8 * NB, 1024), BF),
            pltpu.VMEM((16 * MB, 4, 256), BF),
            pltpu.VMEM((64 * NB, 128), BF),
            pltpu.VMEM((6, 6, 6 * BP, 256), BF),
            pltpu.VMEM((6, 6, 6 * BP, 256), BF),
            pltpu.VMEM((4, 512, 256), BF),
            pltpu.VMEM((8 * NB, 256), BF),
            pltpu.VMEM((8 * NB, 256), F32),
            pltpu.VMEM((1024, 8 * NB), BF),
            pltpu.VMEM((256, 2048), BF),
            pltpu.VMEM((8 * NB, 256), BF),
            pltpu.VMEM((6, 32, 128), BF),
            pltpu.VMEM((6, 128, 256), BF),
            pltpu.VMEM((8, 80, 256), BF),
            pltpu.VMEM((8, 80, 256), BF),
            pltpu.VMEM((8, 64, 256), BF),
            pltpu.VMEM((8, 64, 256), BF),
            pltpu.VMEM((5, 128, 256), BF),
            pltpu.VMEM((5, 128, 256), BF),
            pltpu.VMEM((5, 128, 256), BF),
            pltpu.VMEM((5, 128, 256), BF),
            pltpu.VMEM((2, 1792, 128), BF),
            pltpu.VMEM((2, 1024, 128), BF),
            pltpu.VMEM((1792, 128), BF),
            pltpu.VMEM((1024, 128), BF),
            pltpu.VMEM((1792, 128), BF),
            pltpu.VMEM((1024, 128), BF),
            pltpu.VMEM((NX, KA, 128), BF),
            pltpu.VMEM((NX, KD, 128), BF),
            pltpu.VMEM((NY, KA, 128), BF),
            pltpu.VMEM((NY, KD, 128), BF),
            dma((6,)),
            dma((6,)),
            dma((2, 8)),
            dma((2, 8)),
            dma((2, 5)),
            dma((2, 5)),
            dma((2, 11)),
            dma((2, 2 * NX)),
            dma((2, 2 * NY)),
            dma((2, 2 * NX)),
            dma((2, 8)),
        ],
        compiler_params=pltpu.CompilerParams(
            collective_id=0, has_side_effects=True, vmem_limit_bytes=56 * 1024 * 1024),
        cost_estimate=pl.CostEstimate(flops=6_000_000_000, bytes_accessed=10_000_000, transcendentals=600_000),
    )(fine_field.reshape(64 * NB, 128), target.reshape(1, NB), neighbour.T, down_weight,
      conv_weight.reshape(1792, 256), out_cotangent.reshape(16 * MB, 4, 256))

    coarse, fineg, down_g, conv_g = pl.pallas_call(
        finish,
        out_shape=(
            jax.ShapeDtypeStruct((16 * MB, 4, 256), BF),
            jax.ShapeDtypeStruct((64 * NB, 128), BF),
            jax.ShapeDtypeStruct((1024, 256), F32),
            jax.ShapeDtypeStruct((1792, 256), F32),
        ),
        in_specs=[anyw] * 4,
        out_specs=[anyw] * 4,
        scratch_shapes=[
            pltpu.VMEM((16 * MB, 4, 256), BF),
            pltpu.VMEM((64 * NB, 128), BF),
            pltpu.VMEM((2, 1792, 128), BF),
            pltpu.VMEM((2, 1024, 128), BF),
            pltpu.VMEM((1024, 256), F32),
            pltpu.VMEM((1792, 256), F32),
            dma((20,)),
        ],
        compiler_params=pltpu.CompilerParams(vmem_limit_bytes=60 * 1024 * 1024),
    )(coarse, fineg, ga, gd)
    return (coarse.reshape(MB, 4, 4, 4, 256), fineg.reshape(NB, 8, 8, 128), down_g,
            conv_g.reshape(7, 256, 256))


def solution(mesh):
    every = ("gx", "gy", "gz")
    in_specs = (
        P(every, None, None, None),
        P(every),
        P(every, None),
        P(),
        P(),
        P(every, None, None, None, None),
    )
    out_specs = (
        P(every, None, None, None, None),
        P(every, None, None, None),
        P(),
        P(),
    )
    return jax.shard_map(shards, mesh=mesh, in_specs=in_specs, out_specs=out_specs, check_vma=False)
```

```python
import functools

import jax
import jax.numpy as jnp
from jax import lax
from jax.experimental import pallas as pl
from jax.experimental.pallas import tpu as pltpu
from jax.sharding import PartitionSpec as P

MESH = pl.DeviceIdType.MESH
BF = jnp.bfloat16
F32 = jnp.float32
I32 = jnp.int32

NX, NY, NZ = 16, 8, 2
MB = 18
BP = 32
NB = 80
CELLS = 8 * MB

OPP = (0, 2, 1, 4, 3, 6, 5)
OFFS = ((0, 0, 0), (-1, 0, 0), (1, 0, 0), (0, -1, 0), (0, 1, 0), (0, 0, -1), (0, 0, 1))
DIRS = ((-1, -1), (-1, 0), (-1, 1), (0, -1), (0, 1), (1, -1), (1, 0), (1, 1))
KA, KD = 112, 64


def iota(shape, dim):
    return lax.broadcasted_iota(I32, shape, dim)


def dot(a, b):
    return jnp.dot(a, b, preferred_element_type=F32)


def dot_nt(a, b):
    return lax.dot_general(a, b, (((1,), (1,)), ((), ())), preferred_element_type=F32)


def onehot(mask):
    return jnp.where(mask, 1.0, 0.0).astype(BF)


def ninth(u):
    return lax.shift_right_arithmetic(u * 7282, 16)


def view(ext, x, d):
    dx, dy, dz = OFFS[d]
    rows = ext[1 + x + dx, 1 + dy:5 + dy, BP * (1 + dz):BP * (5 + dz), :]
    return rows.reshape(16 * BP, 256)


def layer_quad(ext, k, q):
    if k == 0:
        return ext[4, 1 + q, BP:5 * BP, :]
    if k == 1:
        return ext[1, 1 + q, BP:5 * BP, :]
    if k == 2:
        return ext[1 + q, 4, BP:5 * BP, :]
    if k == 3:
        return ext[1 + q, 1, BP:5 * BP, :]
    z = 4 if k == 4 else 1
    return ext[1 + q, 1:5, BP * z:BP * (z + 1), :].reshape(4 * BP, 256)


def put_halo(ext, k, q, rows):
    if k == 0:
        ext[0, 1 + q, BP:5 * BP, :] = rows
    elif k == 1:
        ext[5, 1 + q, BP:5 * BP, :] = rows
    elif k == 2:
        ext[1 + q, 0, BP:5 * BP, :] = rows
    elif k == 3:
        ext[1 + q, 5, BP:5 * BP, :] = rows
    else:
        z = 0 if k == 4 else 5
        ext[1 + q, 1:5, BP * z:BP * (z + 1), :] = rows.reshape(4, BP, 256)


def kernel(fine_h, tgt_h, nb_h, wd_h, wc_h, cot_h,
           coarse_h, fineg_h, ga_h, gd_h,
           tgt, nb, ga, gd, fin, cin, wd, wc, wt, t_scr, n_scr, wide, tall, fine, coarse_v, fineg_v,
           cotx, hidx, gh, red, slope, fine_t, hid_t, gr, selc, selp,
           osnd, orcv, rsnd, rrcv, fsnd, frcv, hsnd, hrcv,
           pa, pd, ca, cd, qa, qd, xa, xd, ya, yd,
           isem, esem, osem, rsem, fsem, hsem, coresem, xsem, zsem, xgsem, cgsem):
    gx, gy, gz = lax.axis_index("gx"), lax.axis_index("gy"), lax.axis_index("gz")
    myself = (gx * NY + gy) * NZ + gz

    def at(dx, dy):
        return (lax.rem(gx + dx + NX, NX), lax.rem(gy + dy + NY, NY), gz)

    other = (gx, gy, 1 - gz)

    barrier = pltpu.get_barrier_semaphore()
    peers = [at(k, 0) for k in range(1, NX)] + [at(0, k) for k in range(1, NY)]
    peers += [at(a, b) for a in (-1, 1) for b in (-1, 1)] + [other]
    for peer in peers:
        pl.semaphore_signal(barrier, inc=1, device_id=peer, device_id_type=MESH)

    loads = [pltpu.make_async_copy(src, dst, isem.at[i]) for i, (src, dst) in enumerate(
        ((tgt_h, tgt), (fine_h, fin), (wd_h, wd), (cot_h, cin), (nb_h, nb), (wc_h, wc)))]
    for c in loads:
        c.start()

    def remote(src, dst, sems, i, device):
        return pltpu.make_async_remote_copy(
            src_ref=src, dst_ref=dst, send_sem=sems.at[0, i], recv_sem=sems.at[1, i],
            device_id=device, device_id_type=MESH)

    def place(t):
        owner = ninth(lax.shift_right_arithmetic(t, 4))
        cell = t - owner * CELLS
        moving = owner != myself
        sx = lax.shift_right_arithmetic(owner, 4) - gx
        sy = (lax.shift_right_arithmetic(owner, 1) & 7) - gy
        flat = (sx + 1) * 3 + (sy + 1)
        return cell, moving, jnp.where(flat > 4, flat - 1, flat)

    loads[0].wait()
    t_scr[:, 0:NB] = jnp.broadcast_to(tgt[...], (128, NB))
    cell_c, moving_c, dest_c = place(t_scr[...].T[0:NB, 0:1])
    cell_r, moving_r, dest_r = place(tgt[...])
    member_c = jnp.where(moving_c & (dest_c == iota((NB, 128), 1)), 1.0, 0.0)
    lower = onehot(iota((NB, NB), 1) < iota((NB, NB), 0))
    order_c = jnp.sum(dot(lower, member_c.astype(BF)) * member_c, axis=1, keepdims=True)
    member_r = jnp.where(moving_r & (dest_r == iota((16, NB), 0)), 1.0, 0.0)
    upper = onehot(iota((NB, NB), 0) < iota((NB, NB), 1))
    order_r = jnp.sum(dot(member_r.astype(BF), upper) * member_r, axis=0, keepdims=True)
    key_c = jnp.where(moving_c, dest_c * 16 + order_c.astype(I32), -1000)
    key_r = jnp.where(moving_r, dest_r * 16 + order_r.astype(I32), -1000)

    def table_name(shape, dim):
        r = iota(shape, dim)
        b = r & 31
        return jnp.where(b < MB, b * 8 + lax.shift_right_arithmetic(r, 5), -7)

    send_hot = [onehot(key_r + 8 * h == iota((128, NB), 0)) for h in range(2)]
    back_hot = [onehot(key_c + 8 * h == iota((NB, 128), 1)) for h in range(2)]
    stay_c = onehot((cell_c == table_name((NB, 256), 1)) & jnp.logical_not(moving_c))
    stay_r = onehot((cell_r == table_name((256, NB), 0)) & jnp.logical_not(moving_r))

    loads[1].wait()
    wide[...] = fin[...].astype(F32)
    for c in range(8):
        for v in range(8):
            part = wide[pl.ds(c * 8 + v, NB, stride=64), :]
            fine[c * NB:(c + 1) * NB, v * 128:(v + 1) * 128] = part.astype(BF)
    loads[2].wait()
    red[...] = dot(fine[...], wd[...]).astype(BF)
    for pair in range(4):
        out = sum(dot(send_hot[h], red[(2 * pair + h) * NB:(2 * pair + h + 1) * NB, :]) for h in range(2))
        out = out.astype(BF)
        for d in range(8):
            osnd[d, pair * 16:(pair + 1) * 16, :] = out[d * 16:(d + 1) * 16]
    tags = jnp.broadcast_to((cell_c + 1).astype(F32), (NB, 256)).astype(BF)
    out = (dot(send_hot[0], tags) + dot(send_hot[1], tags)).astype(BF)
    for d in range(8):
        osnd[d, 64:80, :] = out[d * 16:(d + 1) * 16]

    pl.semaphore_wait(barrier, len(peers))
    octs = [remote(osnd.at[d], orcv.at[d], osem, d, at(*DIRS[d])) for d in range(8)]
    for c in octs:
        c.start()

    quad_c = lax.shift_right_arithmetic(iota((128, 128), 0), 5)
    lane = iota((128, 128), 1)

    loads[4].wait()
    n_scr[...] = jnp.full((8, 128), -1, I32)
    for q in range(4):
        n_scr[0:6, BP * q:BP * q + MB] = nb[...]
    nb_r = n_scr[...]
    nb_c = nb_r.T

    def names(v):
        owner = ninth(lax.shift_right_arithmetic(v, 1))
        return v - owner * MB, (v >= 0) & (owner == myself), (v >= 0) & (owner != myself)

    for k in range(6):
        vc = nb_c[:, k:k + 1]
        vr = nb_r[k:k + 1, :]
        idx_c, home_c, far_c = names(vc)
        idx_r, home_r, far_r = names(vr)
        less = far_r & (vr < vc) & (lane < 32)
        rank_c = jnp.sum(jnp.where(less, 1.0, 0.0), axis=1, keepdims=True).astype(I32)
        selp[k, :, 0:128] = onehot(home_c & (idx_c + 32 * quad_c == lane))
        selp[k, :, 128:256] = onehot(far_c & (rank_c + 8 * quad_c == lane))
        early = far_c[0:32] & (iota((32, 128), 0) < (iota((32, 128), 1) & 31))
        rank_r = jnp.sum(jnp.where(early, 1.0, 0.0), axis=0, keepdims=True).astype(I32)
        slot = rank_r + 8 * lax.shift_right_arithmetic(iota((32, 128), 1), 5)
        selc[k] = onehot(far_r & (slot == iota((32, 128), 0)))

    face_to = (at(1, 0), at(-1, 0), at(0, 1), at(0, -1), other)

    def send_faces(ext, snd, rcv, sems):
        copies = [remote(snd.at[k], rcv.at[k], sems, k, face_to[k]) for k in range(5)]
        for k in range(4):
            for q in range(4):
                snd[k, q * 32:(q + 1) * 32, :] = dot(selc[OPP[k + 1] - 1], layer_quad(ext, k, q)).astype(BF)
            copies[k].start()
        for q in range(4):
            both = dot(selc[5], layer_quad(ext, 4, q)) + dot(selc[4], layer_quad(ext, 5, q))
            snd[4, q * 32:(q + 1) * 32, :] = both.astype(BF)
        copies[4].start()
        return copies

    def take_faces(ext, rcv, copies):
        for c in copies:
            c.wait_recv()
        for k in range(6):
            for q in range(4):
                near = dot(selp[k, :, 0:128], layer_quad(ext, k, q))
                far = dot(selp[k, :, 128:160], rcv[min(k, 4), q * 32:(q + 1) * 32, :])
                put_halo(ext, k, q, (near + far).astype(BF))

    loads[3].wait()
    tall[...] = jnp.zeros_like(tall)
    for m in range(16 * MB):
        part = cin[m].astype(F32)
        for h in range(2):
            tall[h, 4 * m:4 * m + 4, :] = part[:, h * 128:(h + 1) * 128]
    for p in range(64):
        x, y, z = p >> 4, (p >> 2) & 3, p & 3
        for h in range(2):
            rows = tall[h, pl.ds(p, BP, stride=64), :]
            cotx[1 + x, 1 + y, BP * (1 + z):BP * (2 + z), h * 128:(h + 1) * 128] = rows.astype(BF)
    cot_faces = send_faces(cotx, fsnd, frcv, fsem)

    fine_t[...] = fine[...].T
    pre = red[...].astype(F32)
    sig = 1.0 / (1.0 + jnp.exp(-pre))
    slope[...] = sig * (1.0 + pre * (1.0 - sig))
    loads[5].wait()
    for d in range(7):
        wt[d * 256:(d + 1) * 256, :] = wc[d * 256:(d + 1) * 256, :].T
    for c in octs:
        c.wait_recv()
    tag = orcv[:, 64:80, :].reshape(128, 256).astype(F32)
    row_half = lax.shift_right_arithmetic(iota((128, 256), 0), 3) & 1
    match = tag - 1.0 == table_name((128, 256), 1).astype(F32)
    came = [jnp.where(match & (row_half == h), 1.0, 0.0) for h in range(2)]
    came_t = [m.T.astype(BF) for m in came]
    came = [m.astype(BF) for m in came]

    for c in range(8):
        i, j, k = c >> 2, (c >> 1) & 1, c & 1
        pair = c >> 1
        got = orcv[:, pair * 16:(pair + 1) * 16, :].reshape(128, 256)
        pre = dot(came_t[c & 1], got) + dot(stay_r, red[c * NB:(c + 1) * NB, :])
        hid = (pre / (1.0 + jnp.exp(-pre))).astype(BF)
        for o in range(8):
            x, y, z = 2 * (o >> 2) + i, 2 * ((o >> 1) & 1) + j, 2 * (o & 1) + k
            hidx[1 + x, 1 + y, BP * (1 + z):BP * (2 + z), :] = hid[o * BP:(o + 1) * BP]
    hid_faces = send_faces(hidx, hsnd, hrcv, hsem)
    for x in range(4):
        hid_t[:, x * 512:(x + 1) * 512] = view(hidx, x, 0).T

    take_faces(cotx, frcv, cot_faces)

    for x in range(4):
        rows = jnp.concatenate([view(cotx, x, OPP[d]) for d in range(7)], axis=1)
        gh[x] = dot(rows, wt[...]).astype(BF)

    def grads(c):
        i, j, k = c >> 2, (c >> 1) & 1, c & 1
        out = []
        for o in range(8):
            x, y, z = 2 * (o >> 2) + i, 2 * ((o >> 1) & 1) + j, 2 * (o & 1) + k
            out.append(gh[x, (y * 4 + z) * BP:(y * 4 + z + 1) * BP, :])
        return jnp.concatenate(out, axis=0)

    for pair in range(4):
        out = (dot(came[0], grads(2 * pair)) + dot(came[1], grads(2 * pair + 1))).astype(BF)
        for d in range(8):
            rsnd[d, pair * 16:(pair + 1) * 16, :] = out[d * 16:(d + 1) * 16]
    rets = [remote(rsnd.at[d], rrcv.at[d], rsem, d, at(-DIRS[d][0], -DIRS[d][1])) for d in range(8)]
    for c in rets:
        c.start()

    def core_send(p, cbuf, m, s):
        rows = pl.ds(m * 256, 256)
        c = remote(p.at[1 - gz, rows], cbuf.at[rows], coresem, 7 * s + m, other)
        c.start()
        return c

    def x_copy(src, dst, sems, s, p):
        return pltpu.make_async_remote_copy(
            src_ref=src, dst_ref=dst, send_sem=sems.at[0, s * NX + p], recv_sem=sems.at[1, s * NX + gx],
            device_id=(p, gy, gz), device_id_type=MESH)

    def x_from(dst, sems, s, p):
        return pltpu.make_async_remote_copy(
            src_ref=dst, dst_ref=dst, send_sem=sems.at[0, s * NX + p], recv_sem=sems.at[1, s * NX + p],
            device_id=(p, gy, gz), device_id_type=MESH)

    def away(p, fn):
        @pl.when(gx != p)
        def _():
            fn()

    def core_take(core, p, cbuf, q, xbuf, n, m, s):
        core.wait_recv()
        rows = slice(m * 256, (m + 1) * 256)
        q[rows] = (p[gz, rows].astype(F32) + cbuf[rows].astype(F32)).astype(BF)
        for j in range(NX):
            if m * 256 < (j + 1) * n <= (m + 1) * 256:
                away(j, lambda j=j: x_copy(q.at[pl.ds(j * n, n)], xbuf.at[gx], xsem, s, j).start())

    def x_sum(q, xbuf, n, s):
        xbuf[gx] = q[pl.ds(pl.multiple_of(gx * n, 16), n), :]
        for j in range(NX):
            away(j, lambda j=j: x_from(xbuf.at[j], xsem, s, j).wait_recv())
        acc = xbuf[0].astype(F32)
        for j in range(1, NX):
            acc = acc + xbuf[j].astype(F32)
        return acc.astype(BF)

    def zb_start(acc, ybuf, s):
        ybuf[gy] = acc
        out = [remote(ybuf.at[gy], ybuf.at[gy], zsem, s * NY + k, at(0, k)) for k in range(1, NY)]
        for c in out:
            c.start()
        return out

    def xg_start(rows, g, n, s):
        mine = pl.ds(pl.multiple_of(gx * n, 16), n)
        g[gz, mine, :] = rows
        for j in range(NX):
            away(j, lambda j=j: x_copy(g.at[gz, mine], g.at[gz, mine], xgsem, s, j).start())

    def gathered_y(copies, ybuf):
        for c in copies:
            c.wait_recv()
        acc = ybuf[0].astype(F32)
        for k in range(1, NY):
            acc = acc + ybuf[k].astype(F32)
        return acc.astype(BF)

    def cg_start(g, n, s):
        out = []
        for quarter in range(4):
            for j in range(4 * quarter, 4 * quarter + 4):
                away(j, lambda j=j: x_from(g.at[gz, pl.ds(j * n, n)], xgsem, s, j).wait_recv())
            rows = pl.ds(4 * quarter * n, 4 * n)
            out.append(remote(g.at[gz, rows], g.at[gz, rows], cgsem, 4 * s + quarter, other))
            out[quarter].start()
        return out

    cores_a = []
    for d in range(7):
        rows = jnp.concatenate([view(cotx, x, OPP[d]) for x in range(4)], axis=0)
        acc = dot(hid_t[...], rows).astype(BF)
        for h in range(2):
            pa[h, d * 256:(d + 1) * 256, :] = acc[:, h * 128:(h + 1) * 128]
        cores_a.append(core_send(pa, ca, d, 0))
        if d >= 5:
            core_take(cores_a[d - 5], pa, ca, qa, xa, KA, d - 5, 0)
    for d in range(2, 7):
        core_take(cores_a[d], pa, ca, qa, xa, KA, d, 0)

    for c in rets:
        c.wait_recv()
    for c in range(8):
        back = rrcv[:, (c >> 1) * 16:(c >> 1) * 16 + 16, :].reshape(128, 256)
        grad = dot(stay_c, grads(c)) + dot(back_hot[c & 1], back)
        gr[c * NB:(c + 1) * NB, :] = (grad * slope[c * NB:(c + 1) * NB, :]).astype(BF)
    cores_d = []
    for m in range(4):
        acc = dot(fine_t[m * 256:(m + 1) * 256, :], gr[...]).astype(BF)
        for h in range(2):
            pd[h, m * 256:(m + 1) * 256, :] = acc[:, h * 128:(h + 1) * 128]
        cores_d.append(core_send(pd, cd, m, 1))

    take_faces(hidx, hrcv, hid_faces)
    for m in range(4):
        core_take(cores_d[m], pd, cd, qd, xd, KD, m, 1)

    def conv(x):
        rows = jnp.concatenate([view(hidx, x, d) for d in range(7)], axis=1)
        acc = dot(rows, wc[...])
        for p in range(16):
            for h in range(2):
                tall[h, pl.ds(x * 16 + p, BP, stride=64), :] = acc[p * BP:(p + 1) * BP, h * 128:(h + 1) * 128]

    for x in range(3):
        conv(x)
    zs_a = zb_start(x_sum(qa, xa, KA, 0), ya, 0)
    conv(3)
    zs_d = zb_start(x_sum(qd, xd, KD, 1), yd, 1)

    for c in range(8):
        flow = dot_nt(gr[c * NB:(c + 1) * NB, :], wd[...])
        for v in range(8):
            wide[pl.ds(c * 8 + v, NB, stride=64), :] = flow[:, v * 128:(v + 1) * 128]
    fineg_v[...] = wide[...].astype(BF)
    stores = [pltpu.make_async_copy(fineg_v, fineg_h, esem.at[1])]
    stores[0].start()

    for m in range(16 * MB):
        for h in range(2):
            coarse_v[m, :, h * 128:(h + 1) * 128] = tall[h, 4 * m:4 * m + 4, :].astype(BF)
    stores.append(pltpu.make_async_copy(coarse_v, coarse_h, esem.at[0]))
    stores[1].start()

    xg_start(gathered_y(zs_a, ya), ga, KA, 0)
    xg_start(gathered_y(zs_d, yd), gd, KD, 1)
    cg_a = cg_start(ga, KA, 0)
    stores.append(pltpu.make_async_copy(ga.at[gz], ga_h.at[gz], esem.at[2]))
    stores[2].start()
    cg_d = cg_start(gd, KD, 1)
    stores.append(pltpu.make_async_copy(gd.at[gz], gd_h.at[gz], esem.at[3]))
    stores[3].start()
    for c in cg_a:
        c.wait_recv()
    stores.append(pltpu.make_async_copy(ga.at[1 - gz], ga_h.at[1 - gz], esem.at[4]))
    stores[4].start()
    for c in cg_d:
        c.wait_recv()
    stores.append(pltpu.make_async_copy(gd.at[1 - gz], gd_h.at[1 - gz], esem.at[5]))
    stores[5].start()
    for c in stores:
        c.wait()
    for j in range(NX):
        def sent(j=j):
            x_from(xa.at[j], xsem, 0, j).wait_send()
            x_from(xd.at[j], xsem, 1, j).wait_send()
            x_from(ga.at[gz, pl.ds(j * KA, KA)], xgsem, 0, j).wait_send()
            x_from(gd.at[gz, pl.ds(j * KD, KD)], xgsem, 1, j).wait_send()

        away(j, sent)
    for c in (octs + cot_faces + rets + hid_faces + cores_a + cores_d + zs_a + zs_d + cg_a + cg_d):
        c.wait_send()


def finish(coarse_h, fineg_h, ga_h, gd_h, coarse_o, fineg_o, down_h, conv_h,
           coarse, fineg, ga, gd, down, conv, sem):
    reads = [pltpu.make_async_copy(gd_h, gd, sem.at[0])]
    for m in range(7):
        rows = pl.ds(m * 256, 256)
        reads.append(pltpu.make_async_copy(ga_h.at[:, rows], ga.at[:, rows], sem.at[1 + m]))
    reads += [pltpu.make_async_copy(coarse_h, coarse, sem.at[8]), pltpu.make_async_copy(fineg_h, fineg, sem.at[9])]
    for c in reads:
        c.start()
    scale = 1.0 / (64 * MB)
    reads[0].wait()
    for h in range(2):
        down[:, h * 128:(h + 1) * 128] = gd[h].astype(F32) * scale
    writes = [pltpu.make_async_copy(down, down_h, sem.at[10])]
    writes[0].start()
    for m in range(7):
        reads[1 + m].wait()
        rows = slice(m * 256, (m + 1) * 256)
        for h in range(2):
            conv[rows, h * 128:(h + 1) * 128] = ga[h, rows].astype(F32) * scale
        writes.append(pltpu.make_async_copy(conv.at[rows], conv_h.at[rows], sem.at[11 + m]))
        writes[1 + m].start()
    reads[8].wait()
    writes.append(pltpu.make_async_copy(coarse, coarse_o, sem.at[18]))
    writes[8].start()
    reads[9].wait()
    writes.append(pltpu.make_async_copy(fineg, fineg_o, sem.at[19]))
    writes[9].start()
    for c in writes:
        c.wait()


def shards(fine_field, target, neighbour, down_weight, conv_weight, out_cotangent):
    anyw = pl.BlockSpec(memory_space=pl.ANY)
    dma = pltpu.SemaphoreType.DMA
    coarse, fineg, ga, gd = pl.pallas_call(
        kernel,
        out_shape=(
            jax.ShapeDtypeStruct((16 * MB, 4, 256), BF),
            jax.ShapeDtypeStruct((64 * NB, 128), BF),
            jax.ShapeDtypeStruct((2, 1792, 128), BF),
            jax.ShapeDtypeStruct((2, 1024, 128), BF),
        ),
        in_specs=[anyw] * 6,
        out_specs=[anyw] * 4,
        scratch_shapes=[
            pltpu.VMEM((1, NB), I32),
            pltpu.VMEM((6, MB), I32),
            pltpu.VMEM((2, 1792, 128), BF),
            pltpu.VMEM((2, 1024, 128), BF),
            pltpu.VMEM((64 * NB, 128), BF),
            pltpu.VMEM((16 * MB, 4, 256), BF),
            pltpu.VMEM((1024, 256), BF),
            pltpu.VMEM((1792, 256), BF),
            pltpu.VMEM((1792, 256), BF),
            pltpu.VMEM((128, 128), I32),
            pltpu.VMEM((8, 128), I32),
            pltpu.VMEM((64 * NB, 128), F32),
            pltpu.VMEM((2, 64 * BP, 128), F32),
            pltpu.VMEM((8 * NB, 1024), BF),
            pltpu.VMEM((16 * MB, 4, 256), BF),
            pltpu.VMEM((64 * NB, 128), BF),
            pltpu.VMEM((6, 6, 6 * BP, 256), BF),
            pltpu.VMEM((6, 6, 6 * BP, 256), BF),
            pltpu.VMEM((4, 512, 256), BF),
            pltpu.VMEM((8 * NB, 256), BF),
            pltpu.VMEM((8 * NB, 256), F32),
            pltpu.VMEM((1024, 8 * NB), BF),
            pltpu.VMEM((256, 2048), BF),
            pltpu.VMEM((8 * NB, 256), BF),
            pltpu.VMEM((6, 32, 128), BF),
            pltpu.VMEM((6, 128, 256), BF),
            pltpu.VMEM((8, 80, 256), BF),
            pltpu.VMEM((8, 80, 256), BF),
            pltpu.VMEM((8, 64, 256), BF),
            pltpu.VMEM((8, 64, 256), BF),
            pltpu.VMEM((5, 128, 256), BF),
            pltpu.VMEM((5, 128, 256), BF),
            pltpu.VMEM((5, 128, 256), BF),
            pltpu.VMEM((5, 128, 256), BF),
            pltpu.VMEM((2, 1792, 128), BF),
            pltpu.VMEM((2, 1024, 128), BF),
            pltpu.VMEM((1792, 128), BF),
            pltpu.VMEM((1024, 128), BF),
            pltpu.VMEM((1792, 128), BF),
            pltpu.VMEM((1024, 128), BF),
            pltpu.VMEM((NX, KA, 128), BF),
            pltpu.VMEM((NX, KD, 128), BF),
            pltpu.VMEM((NY, KA, 128), BF),
            pltpu.VMEM((NY, KD, 128), BF),
            dma((6,)),
            dma((6,)),
            dma((2, 8)),
            dma((2, 8)),
            dma((2, 5)),
            dma((2, 5)),
            dma((2, 11)),
            dma((2, 2 * NX)),
            dma((2, 2 * NY)),
            dma((2, 2 * NX)),
            dma((2, 8)),
        ],
        compiler_params=pltpu.CompilerParams(
            collective_id=0, has_side_effects=True, vmem_limit_bytes=56 * 1024 * 1024),
        cost_estimate=pl.CostEstimate(flops=6_000_000_000, bytes_accessed=10_000_000, transcendentals=600_000),
    )(fine_field.reshape(64 * NB, 128), target.reshape(1, NB), neighbour.T, down_weight,
      conv_weight.reshape(1792, 256), out_cotangent.reshape(16 * MB, 4, 256))

    coarse, fineg, down_g, conv_g = pl.pallas_call(
        finish,
        out_shape=(
            jax.ShapeDtypeStruct((16 * MB, 4, 256), BF),
            jax.ShapeDtypeStruct((64 * NB, 128), BF),
            jax.ShapeDtypeStruct((1024, 256), F32),
            jax.ShapeDtypeStruct((1792, 256), F32),
        ),
        in_specs=[anyw] * 4,
        out_specs=[anyw] * 4,
        scratch_shapes=[
            pltpu.VMEM((16 * MB, 4, 256), BF),
            pltpu.VMEM((64 * NB, 128), BF),
            pltpu.VMEM((2, 1792, 128), BF),
            pltpu.VMEM((2, 1024, 128), BF),
            pltpu.VMEM((1024, 256), F32),
            pltpu.VMEM((1792, 256), F32),
            dma((20,)),
        ],
        compiler_params=pltpu.CompilerParams(vmem_limit_bytes=60 * 1024 * 1024),
    )(coarse, fineg, ga, gd)
    return (coarse.reshape(MB, 4, 4, 4, 256), fineg.reshape(NB, 8, 8, 128), down_g,
            conv_g.reshape(7, 256, 256))


def solution(mesh):
    every = ("gx", "gy", "gz")
    in_specs = (
        P(every, None, None, None),
        P(every),
        P(every, None),
        P(),
        P(),
        P(every, None, None, None, None),
    )
    out_specs = (
        P(every, None, None, None, None),
        P(every, None, None, None),
        P(),
        P(),
    )
    return jax.shard_map(shards, mesh=mesh, in_specs=in_specs, out_specs=out_specs, check_vma=False)
```

```python
import functools

import jax
import jax.numpy as jnp
from jax import lax
from jax.experimental import pallas as pl
from jax.experimental.pallas import tpu as pltpu
from jax.sharding import PartitionSpec as P

MESH = pl.DeviceIdType.MESH
BF = jnp.bfloat16
F32 = jnp.float32
I32 = jnp.int32

NX, NY, NZ = 16, 8, 2
MB = 18
BP = 32
NB = 80
CELLS = 8 * MB

OPP = (0, 2, 1, 4, 3, 6, 5)
OFFS = ((0, 0, 0), (-1, 0, 0), (1, 0, 0), (0, -1, 0), (0, 1, 0), (0, 0, -1), (0, 0, 1))
DIRS = ((-1, -1), (-1, 0), (-1, 1), (0, -1), (0, 1), (1, -1), (1, 0), (1, 1))
KA, KD = 112, 64


def iota(shape, dim):
    return lax.broadcasted_iota(I32, shape, dim)


def dot(a, b):
    return jnp.dot(a, b, preferred_element_type=F32)


def dot_nt(a, b):
    return lax.dot_general(a, b, (((1,), (1,)), ((), ())), preferred_element_type=F32)


def onehot(mask):
    return jnp.where(mask, 1.0, 0.0).astype(BF)


def ninth(u):
    return lax.shift_right_arithmetic(u * 7282, 16)


def view(ext, x, d):
    dx, dy, dz = OFFS[d]
    rows = ext[1 + x + dx, 1 + dy:5 + dy, BP * (1 + dz):BP * (5 + dz), :]
    return rows.reshape(16 * BP, 256)


def layer_quad(ext, k, q):
    if k == 0:
        return ext[4, 1 + q, BP:5 * BP, :]
    if k == 1:
        return ext[1, 1 + q, BP:5 * BP, :]
    if k == 2:
        return ext[1 + q, 4, BP:5 * BP, :]
    if k == 3:
        return ext[1 + q, 1, BP:5 * BP, :]
    z = 4 if k == 4 else 1
    return ext[1 + q, 1:5, BP * z:BP * (z + 1), :].reshape(4 * BP, 256)


def put_halo(ext, k, q, rows):
    if k == 0:
        ext[0, 1 + q, BP:5 * BP, :] = rows
    elif k == 1:
        ext[5, 1 + q, BP:5 * BP, :] = rows
    elif k == 2:
        ext[1 + q, 0, BP:5 * BP, :] = rows
    elif k == 3:
        ext[1 + q, 5, BP:5 * BP, :] = rows
    else:
        z = 0 if k == 4 else 5
        ext[1 + q, 1:5, BP * z:BP * (z + 1), :] = rows.reshape(4, BP, 256)


def kernel(fine_h, tgt_h, nb_h, wd_h, wc_h, cot_h,
           coarse_h, fineg_h, ga_h, gd_h,
           tgt, nb, ga, gd, fin, cin, wd, wc, wt, t_scr, n_scr, wide, tall, fine, coarse_v, fineg_v,
           cotx, hidx, gh, red, slope, fine_t, hid_t, gr, selc, selp,
           nsnd, nrcv, osnd, orcv, rsnd, rrcv, fsnd, frcv, hsnd, hrcv,
           pa, pd, ca, cd, qa, qd, xa, xd, ya, yd,
           isem, esem, nsem, osem, rsem, fsem, hsem, coresem, xsem, zsem, xgsem, cgsem):
    gx, gy, gz = lax.axis_index("gx"), lax.axis_index("gy"), lax.axis_index("gz")
    myself = (gx * NY + gy) * NZ + gz

    def at(dx, dy):
        return (lax.rem(gx + dx + NX, NX), lax.rem(gy + dy + NY, NY), gz)

    other = (gx, gy, 1 - gz)

    barrier = pltpu.get_barrier_semaphore()
    peers = [at(k, 0) for k in range(1, NX)] + [at(0, k) for k in range(1, NY)]
    peers += [at(a, b) for a in (-1, 1) for b in (-1, 1)] + [other]
    for peer in peers:
        pl.semaphore_signal(barrier, inc=1, device_id=peer, device_id_type=MESH)

    loads = [pltpu.make_async_copy(src, dst, isem.at[i]) for i, (src, dst) in enumerate(
        ((tgt_h, tgt), (cot_h, cin), (nb_h, nb), (fine_h, fin), (wd_h, wd), (wc_h, wc)))]
    for c in loads:
        c.start()

    def remote(src, dst, sems, i, device):
        return pltpu.make_async_remote_copy(
            src_ref=src, dst_ref=dst, send_sem=sems.at[0, i], recv_sem=sems.at[1, i],
            device_id=device, device_id_type=MESH)

    def place(t):
        owner = ninth(lax.shift_right_arithmetic(t, 4))
        cell = t - owner * CELLS
        moving = owner != myself
        sx = lax.shift_right_arithmetic(owner, 4) - gx
        sy = (lax.shift_right_arithmetic(owner, 1) & 7) - gy
        flat = (sx + 1) * 3 + (sy + 1)
        return cell, moving, jnp.where(flat > 4, flat - 1, flat)

    loads[0].wait()
    t_scr[:, 0:NB] = jnp.broadcast_to(tgt[...], (128, NB))
    cell_c, moving_c, dest_c = place(t_scr[...].T[0:NB, 0:1])
    cell_r, moving_r, dest_r = place(tgt[...])
    member_c = jnp.where(moving_c & (dest_c == iota((NB, 128), 1)), 1.0, 0.0)
    lower = onehot(iota((NB, NB), 1) < iota((NB, NB), 0))
    order_c = jnp.sum(dot(lower, member_c.astype(BF)) * member_c, axis=1, keepdims=True)
    member_r = jnp.where(moving_r & (dest_r == iota((16, NB), 0)), 1.0, 0.0)
    upper = onehot(iota((NB, NB), 0) < iota((NB, NB), 1))
    order_r = jnp.sum(dot(member_r.astype(BF), upper) * member_r, axis=0, keepdims=True)
    key_c = jnp.where(moving_c, dest_c * 16 + order_c.astype(I32), -1000)
    key_r = jnp.where(moving_r, dest_r * 16 + order_r.astype(I32), -1000)

    def table_name(shape, dim):
        r = iota(shape, dim)
        b = r & 31
        return jnp.where(b < MB, b * 8 + lax.shift_right_arithmetic(r, 5), -7)

    send_hot = [onehot(key_r + 8 * h == iota((128, NB), 0)) for h in range(2)]
    back_hot = [onehot(key_c + 8 * h == iota((NB, 128), 1)) for h in range(2)]
    stay_c = onehot((cell_c == table_name((NB, 256), 1)) & jnp.logical_not(moving_c))
    stay_r = onehot((cell_r == table_name((256, NB), 0)) & jnp.logical_not(moving_r))

    tags = jnp.broadcast_to((cell_c + 1).astype(F32), (NB, 256)).astype(BF)
    out = (dot(send_hot[0], tags) + dot(send_hot[1], tags)).astype(BF)
    for d in range(8):
        nsnd[d] = out[d * 16:(d + 1) * 16]

    quad_c = lax.shift_right_arithmetic(iota((128, 128), 0), 5)
    lane = iota((128, 128), 1)

    loads[2].wait()
    n_scr[...] = jnp.full((8, 128), -1, I32)
    for q in range(4):
        n_scr[0:6, BP * q:BP * q + MB] = nb[...]
    nb_r = n_scr[...]
    nb_c = nb_r.T

    def names(v):
        owner = ninth(lax.shift_right_arithmetic(v, 1))
        return v - owner * MB, (v >= 0) & (owner == myself), (v >= 0) & (owner != myself)

    for k in range(6):
        vc = nb_c[:, k:k + 1]
        vr = nb_r[k:k + 1, :]
        idx_c, home_c, far_c = names(vc)
        idx_r, home_r, far_r = names(vr)
        less = far_r & (vr < vc) & (lane < 32)
        rank_c = jnp.sum(jnp.where(less, 1.0, 0.0), axis=1, keepdims=True).astype(I32)
        selp[k, :, 0:128] = onehot(home_c & (idx_c + 32 * quad_c == lane))
        selp[k, :, 128:256] = onehot(far_c & (rank_c + 8 * quad_c == lane))
        early = far_c[0:32] & (iota((32, 128), 0) < (iota((32, 128), 1) & 31))
        rank_r = jnp.sum(jnp.where(early, 1.0, 0.0), axis=0, keepdims=True).astype(I32)
        slot = rank_r + 8 * lax.shift_right_arithmetic(iota((32, 128), 1), 5)
        selc[k] = onehot(far_r & (slot == iota((32, 128), 0)))

    face_to = (at(1, 0), at(-1, 0), at(0, 1), at(0, -1), other)

    def send_faces(ext, snd, rcv, sems):
        copies = [remote(snd.at[k], rcv.at[k], sems, k, face_to[k]) for k in range(5)]
        for k in range(4):
            for q in range(4):
                snd[k, q * 32:(q + 1) * 32, :] = dot(selc[OPP[k + 1] - 1], layer_quad(ext, k, q)).astype(BF)
            copies[k].start()
        for q in range(4):
            both = dot(selc[5], layer_quad(ext, 4, q)) + dot(selc[4], layer_quad(ext, 5, q))
            snd[4, q * 32:(q + 1) * 32, :] = both.astype(BF)
        copies[4].start()
        return copies

    def take_faces(ext, rcv, copies):
        for c in copies:
            c.wait_recv()
        for k in range(6):
            for q in range(4):
                near = dot(selp[k, :, 0:128], layer_quad(ext, k, q))
                far = dot(selp[k, :, 128:160], rcv[min(k, 4), q * 32:(q + 1) * 32, :])
                put_halo(ext, k, q, (near + far).astype(BF))

    loads[1].wait()
    tall[...] = jnp.zeros_like(tall)
    for m in range(16 * MB):
        part = cin[m].astype(F32)
        for h in range(2):
            tall[h, 4 * m:4 * m + 4, :] = part[:, h * 128:(h + 1) * 128]
    for p in range(64):
        x, y, z = p >> 4, (p >> 2) & 3, p & 3
        for h in range(2):
            rows = tall[h, pl.ds(p, BP, stride=64), :]
            cotx[1 + x, 1 + y, BP * (1 + z):BP * (2 + z), h * 128:(h + 1) * 128] = rows.astype(BF)
    pl.semaphore_wait(barrier, len(peers))
    tells = [remote(nsnd.at[d], nrcv.at[d], nsem, d, at(*DIRS[d])) for d in range(8)]
    for c in tells:
        c.start()
    cot_faces = send_faces(cotx, fsnd, frcv, fsem)

    loads[3].wait()
    wide[...] = fin[...].astype(F32)
    for c in range(8):
        for v in range(8):
            part = wide[pl.ds(c * 8 + v, NB, stride=64), :]
            fine[c * NB:(c + 1) * NB, v * 128:(v + 1) * 128] = part.astype(BF)
    loads[4].wait()
    red[...] = dot(fine[...], wd[...]).astype(BF)
    for pair in range(4):
        out = sum(dot(send_hot[h], red[(2 * pair + h) * NB:(2 * pair + h + 1) * NB, :]) for h in range(2))
        out = out.astype(BF)
        for d in range(8):
            osnd[d, pair * 16:(pair + 1) * 16, :] = out[d * 16:(d + 1) * 16]
    octs = [remote(osnd.at[d], orcv.at[d], osem, d, at(*DIRS[d])) for d in range(8)]
    for c in octs:
        c.start()

    fine_t[...] = fine[...].T
    pre = red[...].astype(F32)
    sig = 1.0 / (1.0 + jnp.exp(-pre))
    slope[...] = sig * (1.0 + pre * (1.0 - sig))
    loads[5].wait()
    for d in range(7):
        wt[d * 256:(d + 1) * 256, :] = wc[d * 256:(d + 1) * 256, :].T
    take_faces(cotx, frcv, cot_faces)

    for x in range(4):
        rows = jnp.concatenate([view(cotx, x, OPP[d]) for d in range(7)], axis=1)
        gh[x] = dot(rows, wt[...]).astype(BF)

    for c in tells:
        c.wait_recv()
    tag = nrcv[...].reshape(128, 256).astype(F32)
    row_half = lax.shift_right_arithmetic(iota((128, 256), 0), 3) & 1
    match = tag - 1.0 == table_name((128, 256), 1).astype(F32)
    came = [jnp.where(match & (row_half == h), 1.0, 0.0) for h in range(2)]
    came_t = [m.T.astype(BF) for m in came]
    came = [m.astype(BF) for m in came]

    def grads(c):
        i, j, k = c >> 2, (c >> 1) & 1, c & 1
        out = []
        for o in range(8):
            x, y, z = 2 * (o >> 2) + i, 2 * ((o >> 1) & 1) + j, 2 * (o & 1) + k
            out.append(gh[x, (y * 4 + z) * BP:(y * 4 + z + 1) * BP, :])
        return jnp.concatenate(out, axis=0)

    for pair in range(4):
        out = (dot(came[0], grads(2 * pair)) + dot(came[1], grads(2 * pair + 1))).astype(BF)
        for d in range(8):
            rsnd[d, pair * 16:(pair + 1) * 16, :] = out[d * 16:(d + 1) * 16]
    rets = [remote(rsnd.at[d], rrcv.at[d], rsem, d, at(-DIRS[d][0], -DIRS[d][1])) for d in range(8)]
    for c in rets:
        c.start()

    for c in octs:
        c.wait_recv()
    for c in range(8):
        i, j, k = c >> 2, (c >> 1) & 1, c & 1
        pair = c >> 1
        got = orcv[:, pair * 16:(pair + 1) * 16, :].reshape(128, 256)
        pre = dot(came_t[c & 1], got) + dot(stay_r, red[c * NB:(c + 1) * NB, :])
        hid = (pre / (1.0 + jnp.exp(-pre))).astype(BF)
        for o in range(8):
            x, y, z = 2 * (o >> 2) + i, 2 * ((o >> 1) & 1) + j, 2 * (o & 1) + k
            hidx[1 + x, 1 + y, BP * (1 + z):BP * (2 + z), :] = hid[o * BP:(o + 1) * BP]
    hid_faces = send_faces(hidx, hsnd, hrcv, hsem)

    def core_send(p, cbuf, m, s):
        rows = pl.ds(m * 256, 256)
        c = remote(p.at[1 - gz, rows], cbuf.at[rows], coresem, 7 * s + m, other)
        c.start()
        return c

    def x_copy(src, dst, sems, s, p):
        return pltpu.make_async_remote_copy(
            src_ref=src, dst_ref=dst, send_sem=sems.at[0, s * NX + p], recv_sem=sems.at[1, s * NX + gx],
            device_id=(p, gy, gz), device_id_type=MESH)

    def x_from(dst, sems, s, p):
        return pltpu.make_async_remote_copy(
            src_ref=dst, dst_ref=dst, send_sem=sems.at[0, s * NX + p], recv_sem=sems.at[1, s * NX + p],
            device_id=(p, gy, gz), device_id_type=MESH)

    def away(p, fn):
        @pl.when(gx != p)
        def _():
            fn()

    def core_take(core, p, cbuf, q, xbuf, n, m, s):
        core.wait_recv()
        rows = slice(m * 256, (m + 1) * 256)
        q[rows] = (p[gz, rows].astype(F32) + cbuf[rows].astype(F32)).astype(BF)
        for j in range(NX):
            if m * 256 < (j + 1) * n <= (m + 1) * 256:
                away(j, lambda j=j: x_copy(q.at[pl.ds(j * n, n)], xbuf.at[gx], xsem, s, j).start())

    def x_sum(q, xbuf, n, s):
        xbuf[gx] = q[pl.ds(pl.multiple_of(gx * n, 16), n), :]
        for j in range(NX):
            away(j, lambda j=j: x_from(xbuf.at[j], xsem, s, j).wait_recv())
        acc = xbuf[0].astype(F32)
        for j in range(1, NX):
            acc = acc + xbuf[j].astype(F32)
        return acc.astype(BF)

    def zb_start(acc, ybuf, s):
        ybuf[gy] = acc
        out = [remote(ybuf.at[gy], ybuf.at[gy], zsem, s * NY + k, at(0, k)) for k in range(1, NY)]
        for c in out:
            c.start()
        return out

    def xg_start(rows, g, n, s):
        mine = pl.ds(pl.multiple_of(gx * n, 16), n)
        g[gz, mine, :] = rows
        for j in range(NX):
            away(j, lambda j=j: x_copy(g.at[gz, mine], g.at[gz, mine], xgsem, s, j).start())

    def gathered_y(copies, ybuf):
        for c in copies:
            c.wait_recv()
        acc = ybuf[0].astype(F32)
        for k in range(1, NY):
            acc = acc + ybuf[k].astype(F32)
        return acc.astype(BF)

    def cg_start(g, n, s):
        out = []
        for quarter in range(4):
            for j in range(4 * quarter, 4 * quarter + 4):
                away(j, lambda j=j: x_from(g.at[gz, pl.ds(j * n, n)], xgsem, s, j).wait_recv())
            rows = pl.ds(4 * quarter * n, 4 * n)
            out.append(remote(g.at[gz, rows], g.at[gz, rows], cgsem, 4 * s + quarter, other))
            out[quarter].start()
        return out

    for x in range(4):
        hid_t[:, x * 512:(x + 1) * 512] = view(hidx, x, 0).T
    cores_a = []
    for d in range(7):
        rows = jnp.concatenate([view(cotx, x, OPP[d]) for x in range(4)], axis=0)
        acc = dot(hid_t[...], rows).astype(BF)
        for h in range(2):
            pa[h, d * 256:(d + 1) * 256, :] = acc[:, h * 128:(h + 1) * 128]
        cores_a.append(core_send(pa, ca, d, 0))
        if d >= 5:
            core_take(cores_a[d - 5], pa, ca, qa, xa, KA, d - 5, 0)
    for d in range(2, 7):
        core_take(cores_a[d], pa, ca, qa, xa, KA, d, 0)

    for c in rets:
        c.wait_recv()
    for c in range(8):
        back = rrcv[:, (c >> 1) * 16:(c >> 1) * 16 + 16, :].reshape(128, 256)
        grad = dot(stay_c, grads(c)) + dot(back_hot[c & 1], back)
        gr[c * NB:(c + 1) * NB, :] = (grad * slope[c * NB:(c + 1) * NB, :]).astype(BF)
    cores_d = []
    for m in range(4):
        acc = dot(fine_t[m * 256:(m + 1) * 256, :], gr[...]).astype(BF)
        for h in range(2):
            pd[h, m * 256:(m + 1) * 256, :] = acc[:, h * 128:(h + 1) * 128]
        cores_d.append(core_send(pd, cd, m, 1))

    take_faces(hidx, hrcv, hid_faces)
    for m in range(4):
        core_take(cores_d[m], pd, cd, qd, xd, KD, m, 1)

    def conv(x):
        rows = jnp.concatenate([view(hidx, x, d) for d in range(7)], axis=1)
        acc = dot(rows, wc[...])
        for p in range(16):
            for h in range(2):
                tall[h, pl.ds(x * 16 + p, BP, stride=64), :] = acc[p * BP:(p + 1) * BP, h * 128:(h + 1) * 128]

    for x in range(3):
        conv(x)
    zs_a = zb_start(x_sum(qa, xa, KA, 0), ya, 0)
    conv(3)
    zs_d = zb_start(x_sum(qd, xd, KD, 1), yd, 1)

    for c in range(8):
        flow = dot_nt(gr[c * NB:(c + 1) * NB, :], wd[...])
        for v in range(8):
            wide[pl.ds(c * 8 + v, NB, stride=64), :] = flow[:, v * 128:(v + 1) * 128]
    fineg_v[...] = wide[...].astype(BF)
    stores = [pltpu.make_async_copy(fineg_v, fineg_h, esem.at[1])]
    stores[0].start()

    for m in range(16 * MB):
        for h in range(2):
            coarse_v[m, :, h * 128:(h + 1) * 128] = tall[h, 4 * m:4 * m + 4, :].astype(BF)
    stores.append(pltpu.make_async_copy(coarse_v, coarse_h, esem.at[0]))
    stores[1].start()

    xg_start(gathered_y(zs_a, ya), ga, KA, 0)
    xg_start(gathered_y(zs_d, yd), gd, KD, 1)
    cg_a = cg_start(ga, KA, 0)
    stores.append(pltpu.make_async_copy(ga.at[gz], ga_h.at[gz], esem.at[2]))
    stores[2].start()
    cg_d = cg_start(gd, KD, 1)
    stores.append(pltpu.make_async_copy(gd.at[gz], gd_h.at[gz], esem.at[3]))
    stores[3].start()
    for c in cg_a:
        c.wait_recv()
    stores.append(pltpu.make_async_copy(ga.at[1 - gz], ga_h.at[1 - gz], esem.at[4]))
    stores[4].start()
    for c in cg_d:
        c.wait_recv()
    stores.append(pltpu.make_async_copy(gd.at[1 - gz], gd_h.at[1 - gz], esem.at[5]))
    stores[5].start()
    for c in stores:
        c.wait()
    for j in range(NX):
        def sent(j=j):
            x_from(xa.at[j], xsem, 0, j).wait_send()
            x_from(xd.at[j], xsem, 1, j).wait_send()
            x_from(ga.at[gz, pl.ds(j * KA, KA)], xgsem, 0, j).wait_send()
            x_from(gd.at[gz, pl.ds(j * KD, KD)], xgsem, 1, j).wait_send()

        away(j, sent)
    for c in (tells + octs + cot_faces + rets + hid_faces + cores_a + cores_d + zs_a + zs_d + cg_a + cg_d):
        c.wait_send()


def finish(coarse_h, fineg_h, ga_h, gd_h, coarse_o, fineg_o, down_h, conv_h,
           coarse, fineg, ga, gd, down, conv, sem):
    reads = [pltpu.make_async_copy(gd_h, gd, sem.at[0])]
    for m in range(7):
        rows = pl.ds(m * 256, 256)
        reads.append(pltpu.make_async_copy(ga_h.at[:, rows], ga.at[:, rows], sem.at[1 + m]))
    reads += [pltpu.make_async_copy(coarse_h, coarse, sem.at[8]), pltpu.make_async_copy(fineg_h, fineg, sem.at[9])]
    for c in reads:
        c.start()
    scale = 1.0 / (64 * MB)
    reads[0].wait()
    for h in range(2):
        down[:, h * 128:(h + 1) * 128] = gd[h].astype(F32) * scale
    writes = [pltpu.make_async_copy(down, down_h, sem.at[10])]
    writes[0].start()
    for m in range(7):
        reads[1 + m].wait()
        rows = slice(m * 256, (m + 1) * 256)
        for h in range(2):
            conv[rows, h * 128:(h + 1) * 128] = ga[h, rows].astype(F32) * scale
        writes.append(pltpu.make_async_copy(conv.at[rows], conv_h.at[rows], sem.at[11 + m]))
        writes[1 + m].start()
    reads[8].wait()
    writes.append(pltpu.make_async_copy(coarse, coarse_o, sem.at[18]))
    writes[8].start()
    reads[9].wait()
    writes.append(pltpu.make_async_copy(fineg, fineg_o, sem.at[19]))
    writes[9].start()
    for c in writes:
        c.wait()


def shards(fine_field, target, neighbour, down_weight, conv_weight, out_cotangent):
    anyw = pl.BlockSpec(memory_space=pl.ANY)
    dma = pltpu.SemaphoreType.DMA
    coarse, fineg, ga, gd = pl.pallas_call(
        kernel,
        out_shape=(
            jax.ShapeDtypeStruct((16 * MB, 4, 256), BF),
            jax.ShapeDtypeStruct((64 * NB, 128), BF),
            jax.ShapeDtypeStruct((2, 1792, 128), BF),
            jax.ShapeDtypeStruct((2, 1024, 128), BF),
        ),
        in_specs=[anyw] * 6,
        out_specs=[anyw] * 4,
        scratch_shapes=[
            pltpu.VMEM((1, NB), I32),
            pltpu.VMEM((6, MB), I32),
            pltpu.VMEM((2, 1792, 128), BF),
            pltpu.VMEM((2, 1024, 128), BF),
            pltpu.VMEM((64 * NB, 128), BF),
            pltpu.VMEM((16 * MB, 4, 256), BF),
            pltpu.VMEM((1024, 256), BF),
            pltpu.VMEM((1792, 256), BF),
            pltpu.VMEM((1792, 256), BF),
            pltpu.VMEM((128, 128), I32),
            pltpu.VMEM((8, 128), I32),
            pltpu.VMEM((64 * NB, 128), F32),
            pltpu.VMEM((2, 64 * BP, 128), F32),
            pltpu.VMEM((8 * NB, 1024), BF),
            pltpu.VMEM((16 * MB, 4, 256), BF),
            pltpu.VMEM((64 * NB, 128), BF),
            pltpu.VMEM((6, 6, 6 * BP, 256), BF),
            pltpu.VMEM((6, 6, 6 * BP, 256), BF),
            pltpu.VMEM((4, 512, 256), BF),
            pltpu.VMEM((8 * NB, 256), BF),
            pltpu.VMEM((8 * NB, 256), F32),
            pltpu.VMEM((1024, 8 * NB), BF),
            pltpu.VMEM((256, 2048), BF),
            pltpu.VMEM((8 * NB, 256), BF),
            pltpu.VMEM((6, 32, 128), BF),
            pltpu.VMEM((6, 128, 256), BF),
            pltpu.VMEM((8, 16, 256), BF),
            pltpu.VMEM((8, 16, 256), BF),
            pltpu.VMEM((8, 64, 256), BF),
            pltpu.VMEM((8, 64, 256), BF),
            pltpu.VMEM((8, 64, 256), BF),
            pltpu.VMEM((8, 64, 256), BF),
            pltpu.VMEM((5, 128, 256), BF),
            pltpu.VMEM((5, 128, 256), BF),
            pltpu.VMEM((5, 128, 256), BF),
            pltpu.VMEM((5, 128, 256), BF),
            pltpu.VMEM((2, 1792, 128), BF),
            pltpu.VMEM((2, 1024, 128), BF),
            pltpu.VMEM((1792, 128), BF),
            pltpu.VMEM((1024, 128), BF),
            pltpu.VMEM((1792, 128), BF),
            pltpu.VMEM((1024, 128), BF),
            pltpu.VMEM((NX, KA, 128), BF),
            pltpu.VMEM((NX, KD, 128), BF),
            pltpu.VMEM((NY, KA, 128), BF),
            pltpu.VMEM((NY, KD, 128), BF),
            dma((6,)),
            dma((6,)),
            dma((2, 8)),
            dma((2, 8)),
            dma((2, 8)),
            dma((2, 5)),
            dma((2, 5)),
            dma((2, 11)),
            dma((2, 2 * NX)),
            dma((2, 2 * NY)),
            dma((2, 2 * NX)),
            dma((2, 8)),
        ],
        compiler_params=pltpu.CompilerParams(
            collective_id=0, has_side_effects=True, vmem_limit_bytes=56 * 1024 * 1024),
        cost_estimate=pl.CostEstimate(flops=6_000_000_000, bytes_accessed=10_000_000, transcendentals=600_000),
    )(fine_field.reshape(64 * NB, 128), target.reshape(1, NB), neighbour.T, down_weight,
      conv_weight.reshape(1792, 256), out_cotangent.reshape(16 * MB, 4, 256))

    coarse, fineg, down_g, conv_g = pl.pallas_call(
        finish,
        out_shape=(
            jax.ShapeDtypeStruct((16 * MB, 4, 256), BF),
            jax.ShapeDtypeStruct((64 * NB, 128), BF),
            jax.ShapeDtypeStruct((1024, 256), F32),
            jax.ShapeDtypeStruct((1792, 256), F32),
        ),
        in_specs=[anyw] * 4,
        out_specs=[anyw] * 4,
        scratch_shapes=[
            pltpu.VMEM((16 * MB, 4, 256), BF),
            pltpu.VMEM((64 * NB, 128), BF),
            pltpu.VMEM((2, 1792, 128), BF),
            pltpu.VMEM((2, 1024, 128), BF),
            pltpu.VMEM((1024, 256), F32),
            pltpu.VMEM((1792, 256), F32),
            dma((20,)),
        ],
        compiler_params=pltpu.CompilerParams(vmem_limit_bytes=60 * 1024 * 1024),
    )(coarse, fineg, ga, gd)
    return (coarse.reshape(MB, 4, 4, 4, 256), fineg.reshape(NB, 8, 8, 128), down_g,
            conv_g.reshape(7, 256, 256))


def solution(mesh):
    every = ("gx", "gy", "gz")
    in_specs = (
        P(every, None, None, None),
        P(every),
        P(every, None),
        P(),
        P(),
        P(every, None, None, None, None),
    )
    out_specs = (
        P(every, None, None, None, None),
        P(every, None, None, None),
        P(),
        P(),
    )
    return jax.shard_map(shards, mesh=mesh, in_specs=in_specs, out_specs=out_specs, check_vma=False)
```

```python
import functools

import jax
import jax.numpy as jnp
from jax import lax
from jax.experimental import pallas as pl
from jax.experimental.pallas import tpu as pltpu
from jax.sharding import PartitionSpec as P

MESH = pl.DeviceIdType.MESH
BF = jnp.bfloat16
F32 = jnp.float32
I32 = jnp.int32

NX, NY, NZ = 16, 8, 2
MB = 18
BP = 32
NB = 80
CELLS = 8 * MB

OPP = (0, 2, 1, 4, 3, 6, 5)
OFFS = ((0, 0, 0), (-1, 0, 0), (1, 0, 0), (0, -1, 0), (0, 1, 0), (0, 0, -1), (0, 0, 1))
DIRS = ((-1, -1), (-1, 0), (-1, 1), (0, -1), (0, 1), (1, -1), (1, 0), (1, 1))
KA, KD = 112, 64


def iota(shape, dim):
    return lax.broadcasted_iota(I32, shape, dim)


def dot(a, b):
    return jnp.dot(a, b, preferred_element_type=F32)


def dot_nt(a, b):
    return lax.dot_general(a, b, (((1,), (1,)), ((), ())), preferred_element_type=F32)


def onehot(mask):
    return jnp.where(mask, 1.0, 0.0).astype(BF)


def ninth(u):
    return lax.shift_right_arithmetic(u * 7282, 16)


def view(ext, x, d):
    dx, dy, dz = OFFS[d]
    rows = ext[1 + x + dx, 1 + dy:5 + dy, BP * (1 + dz):BP * (5 + dz), :]
    return rows.reshape(16 * BP, 256)


def layer_quad(ext, k, q):
    if k == 0:
        return ext[4, 1 + q, BP:5 * BP, :]
    if k == 1:
        return ext[1, 1 + q, BP:5 * BP, :]
    if k == 2:
        return ext[1 + q, 4, BP:5 * BP, :]
    if k == 3:
        return ext[1 + q, 1, BP:5 * BP, :]
    z = 4 if k == 4 else 1
    return ext[1 + q, 1:5, BP * z:BP * (z + 1), :].reshape(4 * BP, 256)


def put_halo(ext, k, q, rows):
    if k == 0:
        ext[0, 1 + q, BP:5 * BP, :] = rows
    elif k == 1:
        ext[5, 1 + q, BP:5 * BP, :] = rows
    elif k == 2:
        ext[1 + q, 0, BP:5 * BP, :] = rows
    elif k == 3:
        ext[1 + q, 5, BP:5 * BP, :] = rows
    else:
        z = 0 if k == 4 else 5
        ext[1 + q, 1:5, BP * z:BP * (z + 1), :] = rows.reshape(4, BP, 256)


def kernel(fine_h, tgt_h, nb_h, wd_h, wc_h, cot_h,
           coarse_h, fineg_h, ga_h, gd_h,
           tgt, nb, ga, gd, fin, cin, wd, wc, wt, t_scr, n_scr, wide, tall, fine, coarse_v, fineg_v,
           cotx, hidx, gh, red, slope, fine_t, hid_t, gr, selc, selp,
           nsnd, nrcv, osnd, orcv, rsnd, rrcv, fsnd, frcv, hsnd, hrcv,
           pa, pd, ca, cd, qa, qd, xa, xd, ya, yd,
           isem, esem, nsem, osem, rsem, fsem, hsem, coresem, xsem, zsem, xgsem, cgsem):
    gx, gy, gz = lax.axis_index("gx"), lax.axis_index("gy"), lax.axis_index("gz")
    myself = (gx * NY + gy) * NZ + gz

    def at(dx, dy):
        return (lax.rem(gx + dx + NX, NX), lax.rem(gy + dy + NY, NY), gz)

    other = (gx, gy, 1 - gz)

    barrier = pltpu.get_barrier_semaphore()
    peers = [at(k, 0) for k in range(1, NX)] + [at(0, k) for k in range(1, NY)]
    peers += [at(a, b) for a in (-1, 1) for b in (-1, 1)] + [other]
    for peer in peers:
        pl.semaphore_signal(barrier, inc=1, device_id=peer, device_id_type=MESH)

    loads = [pltpu.make_async_copy(src, dst, isem.at[i]) for i, (src, dst) in enumerate(
        ((tgt_h, tgt), (cot_h, cin), (nb_h, nb), (fine_h, fin), (wd_h, wd), (wc_h, wc)))]
    for c in loads:
        c.start()

    def remote(src, dst, sems, i, device):
        return pltpu.make_async_remote_copy(
            src_ref=src, dst_ref=dst, send_sem=sems.at[0, i], recv_sem=sems.at[1, i],
            device_id=device, device_id_type=MESH)

    def place(t):
        owner = ninth(lax.shift_right_arithmetic(t, 4))
        cell = t - owner * CELLS
        moving = owner != myself
        sx = lax.shift_right_arithmetic(owner, 4) - gx
        sy = (lax.shift_right_arithmetic(owner, 1) & 7) - gy
        flat = (sx + 1) * 3 + (sy + 1)
        return cell, moving, jnp.where(flat > 4, flat - 1, flat)

    loads[0].wait()
    t_scr[:, 0:NB] = jnp.broadcast_to(tgt[...], (128, NB))
    cell_c, moving_c, dest_c = place(t_scr[...].T[0:NB, 0:1])
    cell_r, moving_r, dest_r = place(tgt[...])
    member_c = jnp.where(moving_c & (dest_c == iota((NB, 128), 1)), 1.0, 0.0)
    lower = onehot(iota((NB, NB), 1) < iota((NB, NB), 0))
    order_c = jnp.sum(dot(lower, member_c.astype(BF)) * member_c, axis=1, keepdims=True)
    member_r = jnp.where(moving_r & (dest_r == iota((16, NB), 0)), 1.0, 0.0)
    upper = onehot(iota((NB, NB), 0) < iota((NB, NB), 1))
    order_r = jnp.sum(dot(member_r.astype(BF), upper) * member_r, axis=0, keepdims=True)
    key_c = jnp.where(moving_c, dest_c * 16 + order_c.astype(I32), -1000)
    key_r = jnp.where(moving_r, dest_r * 16 + order_r.astype(I32), -1000)

    def table_name(shape, dim):
        r = iota(shape, dim)
        b = r & 31
        return jnp.where(b < MB, b * 8 + lax.shift_right_arithmetic(r, 5), -7)

    send_hot = [onehot(key_r + 8 * h == iota((128, NB), 0)) for h in range(2)]
    back_hot = [onehot(key_c + 8 * h == iota((NB, 128), 1)) for h in range(2)]
    stay_c = onehot((cell_c == table_name((NB, 256), 1)) & jnp.logical_not(moving_c))
    stay_r = onehot((cell_r == table_name((256, NB), 0)) & jnp.logical_not(moving_r))

    tags = jnp.broadcast_to((cell_c + 1).astype(F32), (NB, 256)).astype(BF)
    out = (dot(send_hot[0], tags) + dot(send_hot[1], tags)).astype(BF)
    for d in range(8):
        nsnd[d] = out[d * 16:(d + 1) * 16]

    quad_c = lax.shift_right_arithmetic(iota((128, 128), 0), 5)
    lane = iota((128, 128), 1)

    loads[2].wait()
    n_scr[...] = jnp.full((8, 128), -1, I32)
    for q in range(4):
        n_scr[0:6, BP * q:BP * q + MB] = nb[...]
    nb_r = n_scr[...]
    nb_c = nb_r.T

    def names(v):
        owner = ninth(lax.shift_right_arithmetic(v, 1))
        return v - owner * MB, (v >= 0) & (owner == myself), (v >= 0) & (owner != myself)

    for k in range(6):
        vc = nb_c[:, k:k + 1]
        vr = nb_r[k:k + 1, :]
        idx_c, home_c, far_c = names(vc)
        idx_r, home_r, far_r = names(vr)
        less = far_r & (vr < vc) & (lane < 32)
        rank_c = jnp.sum(jnp.where(less, 1.0, 0.0), axis=1, keepdims=True).astype(I32)
        selp[k, :, 0:128] = onehot(home_c & (idx_c + 32 * quad_c == lane))
        selp[k, :, 128:256] = onehot(far_c & (rank_c + 8 * quad_c == lane))
        early = far_c[0:32] & (iota((32, 128), 0) < (iota((32, 128), 1) & 31))
        rank_r = jnp.sum(jnp.where(early, 1.0, 0.0), axis=0, keepdims=True).astype(I32)
        slot = rank_r + 8 * lax.shift_right_arithmetic(iota((32, 128), 1), 5)
        selc[k] = onehot(far_r & (slot == iota((32, 128), 0)))

    face_to = (at(1, 0), at(-1, 0), at(0, 1), at(0, -1), other)

    def send_faces(ext, snd, rcv, sems):
        copies = [remote(snd.at[k], rcv.at[k], sems, k, face_to[k]) for k in range(5)]
        for k in range(4):
            for q in range(4):
                snd[k, q * 32:(q + 1) * 32, :] = dot(selc[OPP[k + 1] - 1], layer_quad(ext, k, q)).astype(BF)
            copies[k].start()
        for q in range(4):
            both = dot(selc[5], layer_quad(ext, 4, q)) + dot(selc[4], layer_quad(ext, 5, q))
            snd[4, q * 32:(q + 1) * 32, :] = both.astype(BF)
        copies[4].start()
        return copies

    def take_faces(ext, rcv, copies):
        for c in copies:
            c.wait_recv()
        for k in range(6):
            for q in range(4):
                near = dot(selp[k, :, 0:128], layer_quad(ext, k, q))
                far = dot(selp[k, :, 128:160], rcv[min(k, 4), q * 32:(q + 1) * 32, :])
                put_halo(ext, k, q, (near + far).astype(BF))

    loads[1].wait()
    tall[...] = jnp.zeros_like(tall)
    for m in range(16 * MB):
        part = cin[m].astype(F32)
        for h in range(2):
            tall[h, 4 * m:4 * m + 4, :] = part[:, h * 128:(h + 1) * 128]
    for p in range(64):
        x, y, z = p >> 4, (p >> 2) & 3, p & 3
        for h in range(2):
            rows = tall[h, pl.ds(p, BP, stride=64), :]
            cotx[1 + x, 1 + y, BP * (1 + z):BP * (2 + z), h * 128:(h + 1) * 128] = rows.astype(BF)
    pl.semaphore_wait(barrier, len(peers))
    tells = [remote(nsnd.at[d], nrcv.at[d], nsem, d, at(*DIRS[d])) for d in range(8)]
    for c in tells:
        c.start()
    cot_faces = send_faces(cotx, fsnd, frcv, fsem)

    loads[3].wait()
    wide[...] = fin[...].astype(F32)
    for c in range(8):
        for v in range(8):
            part = wide[pl.ds(c * 8 + v, NB, stride=64), :]
            fine[c * NB:(c + 1) * NB, v * 128:(v + 1) * 128] = part.astype(BF)
    loads[4].wait()
    red[...] = dot(fine[...], wd[...]).astype(BF)
    for pair in range(4):
        out = sum(dot(send_hot[h], red[(2 * pair + h) * NB:(2 * pair + h + 1) * NB, :]) for h in range(2))
        out = out.astype(BF)
        for d in range(8):
            osnd[d, pair * 16:(pair + 1) * 16, :] = out[d * 16:(d + 1) * 16]
    octs = [remote(osnd.at[d], orcv.at[d], osem, d, at(*DIRS[d])) for d in range(8)]
    for c in octs:
        c.start()

    fine_t[...] = fine[...].T
    pre = red[...].astype(F32)
    sig = 1.0 / (1.0 + jnp.exp(-pre))
    slope[...] = sig * (1.0 + pre * (1.0 - sig))
    loads[5].wait()
    for d in range(7):
        wt[d * 256:(d + 1) * 256, :] = wc[d * 256:(d + 1) * 256, :].T
    take_faces(cotx, frcv, cot_faces)

    for x in range(4):
        rows = jnp.concatenate([view(cotx, x, OPP[d]) for d in range(7)], axis=1)
        gh[x] = dot(rows, wt[...]).astype(BF)

    for c in tells:
        c.wait_recv()
    tag = nrcv[...].reshape(128, 256).astype(F32)
    row_half = lax.shift_right_arithmetic(iota((128, 256), 0), 3) & 1
    match = tag - 1.0 == table_name((128, 256), 1).astype(F32)
    came = [jnp.where(match & (row_half == h), 1.0, 0.0) for h in range(2)]
    came_t = [m.T.astype(BF) for m in came]
    came = [m.astype(BF) for m in came]

    def grads(c):
        i, j, k = c >> 2, (c >> 1) & 1, c & 1
        out = []
        for o in range(8):
            x, y, z = 2 * (o >> 2) + i, 2 * ((o >> 1) & 1) + j, 2 * (o & 1) + k
            out.append(gh[x, (y * 4 + z) * BP:(y * 4 + z + 1) * BP, :])
        return jnp.concatenate(out, axis=0)

    for pair in range(4):
        out = (dot(came[0], grads(2 * pair)) + dot(came[1], grads(2 * pair + 1))).astype(BF)
        for d in range(8):
            rsnd[d, pair * 16:(pair + 1) * 16, :] = out[d * 16:(d + 1) * 16]
    rets = [remote(rsnd.at[d], rrcv.at[d], rsem, d, at(-DIRS[d][0], -DIRS[d][1])) for d in range(8)]
    for c in rets:
        c.start()

    for c in octs:
        c.wait_recv()
    for c in range(8):
        i, j, k = c >> 2, (c >> 1) & 1, c & 1
        pair = c >> 1
        got = orcv[:, pair * 16:(pair + 1) * 16, :].reshape(128, 256)
        pre = dot(came_t[c & 1], got) + dot(stay_r, red[c * NB:(c + 1) * NB, :])
        hid = (pre / (1.0 + jnp.exp(-pre))).astype(BF)
        for o in range(8):
            x, y, z = 2 * (o >> 2) + i, 2 * ((o >> 1) & 1) + j, 2 * (o & 1) + k
            hidx[1 + x, 1 + y, BP * (1 + z):BP * (2 + z), :] = hid[o * BP:(o + 1) * BP]
    hid_faces = send_faces(hidx, hsnd, hrcv, hsem)

    def core_send(p, cbuf, m, s):
        rows = pl.ds(m * 256, 256)
        c = remote(p.at[1 - gz, rows], cbuf.at[rows], coresem, 7 * s + m, other)
        c.start()
        return c

    def x_copy(src, dst, sems, s, p):
        return pltpu.make_async_remote_copy(
            src_ref=src, dst_ref=dst, send_sem=sems.at[0, s * NX + p], recv_sem=sems.at[1, s * NX + gx],
            device_id=(p, gy, gz), device_id_type=MESH)

    def x_from(dst, sems, s, p):
        return pltpu.make_async_remote_copy(
            src_ref=dst, dst_ref=dst, send_sem=sems.at[0, s * NX + p], recv_sem=sems.at[1, s * NX + p],
            device_id=(p, gy, gz), device_id_type=MESH)

    def away(p, fn):
        @pl.when(gx != p)
        def _():
            fn()

    def core_take(core, p, cbuf, q, xbuf, n, m, s):
        core.wait_recv()
        rows = slice(m * 256, (m + 1) * 256)
        q[rows] = (p[gz, rows].astype(F32) + cbuf[rows].astype(F32)).astype(BF)
        for j in range(NX):
            if m * 256 < (j + 1) * n <= (m + 1) * 256:
                away(j, lambda j=j: x_copy(q.at[pl.ds(j * n, n)], xbuf.at[gx], xsem, s, j).start())

    def x_sum(q, xbuf, n, s):
        xbuf[gx] = q[pl.ds(pl.multiple_of(gx * n, 16), n), :]
        for j in range(NX):
            away(j, lambda j=j: x_from(xbuf.at[j], xsem, s, j).wait_recv())
        acc = xbuf[0].astype(F32)
        for j in range(1, NX):
            acc = acc + xbuf[j].astype(F32)
        return acc.astype(BF)

    def zb_start(acc, ybuf, s):
        ybuf[gy] = acc
        out = [remote(ybuf.at[gy], ybuf.at[gy], zsem, s * NY + k, at(0, k)) for k in range(1, NY)]
        for c in out:
            c.start()
        return out

    def xg_start(rows, g, n, s):
        mine = pl.ds(pl.multiple_of(gx * n, 16), n)
        g[gz, mine, :] = rows
        for j in range(NX):
            away(j, lambda j=j: x_copy(g.at[gz, mine], g.at[gz, mine], xgsem, s, j).start())

    def gathered_y(copies, ybuf):
        for c in copies:
            c.wait_recv()
        acc = ybuf[0].astype(F32)
        for k in range(1, NY):
            acc = acc + ybuf[k].astype(F32)
        return acc.astype(BF)

    def cg_start(g, n, s):
        out = []
        for quarter in range(4):
            for j in range(4 * quarter, 4 * quarter + 4):
                away(j, lambda j=j: x_from(g.at[gz, pl.ds(j * n, n)], xgsem, s, j).wait_recv())
            rows = pl.ds(4 * quarter * n, 4 * n)
            out.append(remote(g.at[gz, rows], g.at[gz, rows], cgsem, 4 * s + quarter, other))
            out[quarter].start()
        return out

    for x in range(4):
        hid_t[:, x * 512:(x + 1) * 512] = view(hidx, x, 0).T
    cores_a = []
    for d in range(7):
        rows = jnp.concatenate([view(cotx, x, OPP[d]) for x in range(4)], axis=0)
        acc = dot(hid_t[...], rows).astype(BF)
        for h in range(2):
            pa[h, d * 256:(d + 1) * 256, :] = acc[:, h * 128:(h + 1) * 128]
        cores_a.append(core_send(pa, ca, d, 0))
        if d >= 5:
            core_take(cores_a[d - 5], pa, ca, qa, xa, KA, d - 5, 0)
    for d in range(2, 7):
        core_take(cores_a[d], pa, ca, qa, xa, KA, d, 0)

    for c in rets:
        c.wait_recv()
    for c in range(8):
        back = rrcv[:, (c >> 1) * 16:(c >> 1) * 16 + 16, :].reshape(128, 256)
        grad = dot(stay_c, grads(c)) + dot(back_hot[c & 1], back)
        gr[c * NB:(c + 1) * NB, :] = (grad * slope[c * NB:(c + 1) * NB, :]).astype(BF)
    cores_d = []
    for m in range(4):
        acc = dot(fine_t[m * 256:(m + 1) * 256, :], gr[...]).astype(BF)
        for h in range(2):
            pd[h, m * 256:(m + 1) * 256, :] = acc[:, h * 128:(h + 1) * 128]
        cores_d.append(core_send(pd, cd, m, 1))

    for m in range(4):
        core_take(cores_d[m], pd, cd, qd, xd, KD, m, 1)
    take_faces(hidx, hrcv, hid_faces)

    def conv(x):
        rows = jnp.concatenate([view(hidx, x, d) for d in range(7)], axis=1)
        acc = dot(rows, wc[...])
        for p in range(16):
            for h in range(2):
                tall[h, pl.ds(x * 16 + p, BP, stride=64), :] = acc[p * BP:(p + 1) * BP, h * 128:(h + 1) * 128]

    for x in range(4):
        conv(x)
    zs_a = zb_start(x_sum(qa, xa, KA, 0), ya, 0)
    zs_d = zb_start(x_sum(qd, xd, KD, 1), yd, 1)

    for c in range(8):
        flow = dot_nt(gr[c * NB:(c + 1) * NB, :], wd[...])
        for v in range(8):
            wide[pl.ds(c * 8 + v, NB, stride=64), :] = flow[:, v * 128:(v + 1) * 128]
    fineg_v[...] = wide[...].astype(BF)
    stores = [pltpu.make_async_copy(fineg_v, fineg_h, esem.at[1])]
    stores[0].start()

    for m in range(16 * MB):
        for h in range(2):
            coarse_v[m, :, h * 128:(h + 1) * 128] = tall[h, 4 * m:4 * m + 4, :].astype(BF)
    stores.append(pltpu.make_async_copy(coarse_v, coarse_h, esem.at[0]))
    stores[1].start()

    xg_start(gathered_y(zs_a, ya), ga, KA, 0)
    xg_start(gathered_y(zs_d, yd), gd, KD, 1)
    cg_a = cg_start(ga, KA, 0)
    stores.append(pltpu.make_async_copy(ga.at[gz], ga_h.at[gz], esem.at[2]))
    stores[2].start()
    cg_d = cg_start(gd, KD, 1)
    stores.append(pltpu.make_async_copy(gd.at[gz], gd_h.at[gz], esem.at[3]))
    stores[3].start()
    for c in cg_a:
        c.wait_recv()
    stores.append(pltpu.make_async_copy(ga.at[1 - gz], ga_h.at[1 - gz], esem.at[4]))
    stores[4].start()
    for c in cg_d:
        c.wait_recv()
    stores.append(pltpu.make_async_copy(gd.at[1 - gz], gd_h.at[1 - gz], esem.at[5]))
    stores[5].start()
    for c in stores:
        c.wait()
    for j in range(NX):
        def sent(j=j):
            x_from(xa.at[j], xsem, 0, j).wait_send()
            x_from(xd.at[j], xsem, 1, j).wait_send()
            x_from(ga.at[gz, pl.ds(j * KA, KA)], xgsem, 0, j).wait_send()
            x_from(gd.at[gz, pl.ds(j * KD, KD)], xgsem, 1, j).wait_send()

        away(j, sent)
    for c in (tells + octs + cot_faces + rets + hid_faces + cores_a + cores_d + zs_a + zs_d + cg_a + cg_d):
        c.wait_send()


def finish(coarse_h, fineg_h, ga_h, gd_h, coarse_o, fineg_o, down_h, conv_h,
           coarse, fineg, ga, gd, down, conv, sem):
    reads = [pltpu.make_async_copy(gd_h, gd, sem.at[0])]
    for m in range(7):
        rows = pl.ds(m * 256, 256)
        reads.append(pltpu.make_async_copy(ga_h.at[:, rows], ga.at[:, rows], sem.at[1 + m]))
    reads += [pltpu.make_async_copy(coarse_h, coarse, sem.at[8]), pltpu.make_async_copy(fineg_h, fineg, sem.at[9])]
    for c in reads:
        c.start()
    scale = 1.0 / (64 * MB)
    reads[0].wait()
    for h in range(2):
        down[:, h * 128:(h + 1) * 128] = gd[h].astype(F32) * scale
    writes = [pltpu.make_async_copy(down, down_h, sem.at[10])]
    writes[0].start()
    for m in range(7):
        reads[1 + m].wait()
        rows = slice(m * 256, (m + 1) * 256)
        for h in range(2):
            conv[rows, h * 128:(h + 1) * 128] = ga[h, rows].astype(F32) * scale
        writes.append(pltpu.make_async_copy(conv.at[rows], conv_h.at[rows], sem.at[11 + m]))
        writes[1 + m].start()
    reads[8].wait()
    writes.append(pltpu.make_async_copy(coarse, coarse_o, sem.at[18]))
    writes[8].start()
    reads[9].wait()
    writes.append(pltpu.make_async_copy(fineg, fineg_o, sem.at[19]))
    writes[9].start()
    for c in writes:
        c.wait()


def shards(fine_field, target, neighbour, down_weight, conv_weight, out_cotangent):
    anyw = pl.BlockSpec(memory_space=pl.ANY)
    dma = pltpu.SemaphoreType.DMA
    coarse, fineg, ga, gd = pl.pallas_call(
        kernel,
        out_shape=(
            jax.ShapeDtypeStruct((16 * MB, 4, 256), BF),
            jax.ShapeDtypeStruct((64 * NB, 128), BF),
            jax.ShapeDtypeStruct((2, 1792, 128), BF),
            jax.ShapeDtypeStruct((2, 1024, 128), BF),
        ),
        in_specs=[anyw] * 6,
        out_specs=[anyw] * 4,
        scratch_shapes=[
            pltpu.VMEM((1, NB), I32),
            pltpu.VMEM((6, MB), I32),
            pltpu.VMEM((2, 1792, 128), BF),
            pltpu.VMEM((2, 1024, 128), BF),
            pltpu.VMEM((64 * NB, 128), BF),
            pltpu.VMEM((16 * MB, 4, 256), BF),
            pltpu.VMEM((1024, 256), BF),
            pltpu.VMEM((1792, 256), BF),
            pltpu.VMEM((1792, 256), BF),
            pltpu.VMEM((128, 128), I32),
            pltpu.VMEM((8, 128), I32),
            pltpu.VMEM((64 * NB, 128), F32),
            pltpu.VMEM((2, 64 * BP, 128), F32),
            pltpu.VMEM((8 * NB, 1024), BF),
            pltpu.VMEM((16 * MB, 4, 256), BF),
            pltpu.VMEM((64 * NB, 128), BF),
            pltpu.VMEM((6, 6, 6 * BP, 256), BF),
            pltpu.VMEM((6, 6, 6 * BP, 256), BF),
            pltpu.VMEM((4, 512, 256), BF),
            pltpu.VMEM((8 * NB, 256), BF),
            pltpu.VMEM((8 * NB, 256), F32),
            pltpu.VMEM((1024, 8 * NB), BF),
            pltpu.VMEM((256, 2048), BF),
            pltpu.VMEM((8 * NB, 256), BF),
            pltpu.VMEM((6, 32, 128), BF),
            pltpu.VMEM((6, 128, 256), BF),
            pltpu.VMEM((8, 16, 256), BF),
            pltpu.VMEM((8, 16, 256), BF),
            pltpu.VMEM((8, 64, 256), BF),
            pltpu.VMEM((8, 64, 256), BF),
            pltpu.VMEM((8, 64, 256), BF),
            pltpu.VMEM((8, 64, 256), BF),
            pltpu.VMEM((5, 128, 256), BF),
            pltpu.VMEM((5, 128, 256), BF),
            pltpu.VMEM((5, 128, 256), BF),
            pltpu.VMEM((5, 128, 256), BF),
            pltpu.VMEM((2, 1792, 128), BF),
            pltpu.VMEM((2, 1024, 128), BF),
            pltpu.VMEM((1792, 128), BF),
            pltpu.VMEM((1024, 128), BF),
            pltpu.VMEM((1792, 128), BF),
            pltpu.VMEM((1024, 128), BF),
            pltpu.VMEM((NX, KA, 128), BF),
            pltpu.VMEM((NX, KD, 128), BF),
            pltpu.VMEM((NY, KA, 128), BF),
            pltpu.VMEM((NY, KD, 128), BF),
            dma((6,)),
            dma((6,)),
            dma((2, 8)),
            dma((2, 8)),
            dma((2, 8)),
            dma((2, 5)),
            dma((2, 5)),
            dma((2, 11)),
            dma((2, 2 * NX)),
            dma((2, 2 * NY)),
            dma((2, 2 * NX)),
            dma((2, 8)),
        ],
        compiler_params=pltpu.CompilerParams(
            collective_id=0, has_side_effects=True, vmem_limit_bytes=56 * 1024 * 1024),
        cost_estimate=pl.CostEstimate(flops=6_000_000_000, bytes_accessed=10_000_000, transcendentals=600_000),
    )(fine_field.reshape(64 * NB, 128), target.reshape(1, NB), neighbour.T, down_weight,
      conv_weight.reshape(1792, 256), out_cotangent.reshape(16 * MB, 4, 256))

    coarse, fineg, down_g, conv_g = pl.pallas_call(
        finish,
        out_shape=(
            jax.ShapeDtypeStruct((16 * MB, 4, 256), BF),
            jax.ShapeDtypeStruct((64 * NB, 128), BF),
            jax.ShapeDtypeStruct((1024, 256), F32),
            jax.ShapeDtypeStruct((1792, 256), F32),
        ),
        in_specs=[anyw] * 4,
        out_specs=[anyw] * 4,
        scratch_shapes=[
            pltpu.VMEM((16 * MB, 4, 256), BF),
            pltpu.VMEM((64 * NB, 128), BF),
            pltpu.VMEM((2, 1792, 128), BF),
            pltpu.VMEM((2, 1024, 128), BF),
            pltpu.VMEM((1024, 256), F32),
            pltpu.VMEM((1792, 256), F32),
            dma((20,)),
        ],
        compiler_params=pltpu.CompilerParams(vmem_limit_bytes=60 * 1024 * 1024),
    )(coarse, fineg, ga, gd)
    return (coarse.reshape(MB, 4, 4, 4, 256), fineg.reshape(NB, 8, 8, 128), down_g,
            conv_g.reshape(7, 256, 256))


def solution(mesh):
    every = ("gx", "gy", "gz")
    in_specs = (
        P(every, None, None, None),
        P(every),
        P(every, None),
        P(),
        P(),
        P(every, None, None, None, None),
    )
    out_specs = (
        P(every, None, None, None, None),
        P(every, None, None, None),
        P(),
        P(),
    )
    return jax.shard_map(shards, mesh=mesh, in_specs=in_specs, out_specs=out_specs, check_vma=False)
```
